128 devices in a mesh: dp: 16 (over z_hi, y, core), fsdp: 8 (over z_lo, x).
Axes of the slice: x: 4, y: 4, z: 4 (z_hi: 2, z_lo: 2; z = z_hi * 2 + z_lo), core: 2. Of those that a mesh axis runs over, the one named last changes fastest.
Arguments:
- block_in: bfloat16 [2, 16, 1024, 1024], P(None, 'dp', 'fsdp'), may hold values from -6 to 6
- cotangent: float32 [2, 16, 1024, 1024], P(None, 'dp', 'fsdp'), may hold values from -6 to 6
- lengths: int32 [2, 16], P(None, 'dp'), may hold values from 512 to 1024, as said below
- vector_params: float32 [5, 1024], replicated
- vector_first: float32 [5, 1024], replicated, may hold values from -448 to 448
- vector_second: float32 [5, 1024], replicated, may hold values from 6144 to 24576
- w_in: bfloat16 [1024, 3072], P('fsdp'), may hold values from -0.1875 to 0.1875
- w_out: bfloat16 [1024, 1024], P('fsdp'), may hold values from -0.1875 to 0.1875
- w_gate: bfloat16 [1024, 4608], P('fsdp'), may hold values from -0.1875 to 0.1875
- w_up: bfloat16 [1024, 4608], P('fsdp'), may hold values from -0.1875 to 0.1875
- w_down: bfloat16 [1024, 4608], P('fsdp'), may hold values from -0.09375 to 0.09375
- tile_owner: int32 [8, 140], P('fsdp'), may hold values from 0 to 15, as said below
- tile_master: float32 [8, 192, 128, 128], P('fsdp', 'dp'), may hold values from -0.4375 to 0.4375
- tile_first: float32 [8, 192, 128, 128], P('fsdp', 'dp'), may hold values from -448 to 448
- tile_second: float32 [8, 192, 128, 128], P('fsdp', 'dp'), may hold values from 6144 to 24576
- tile_stats: float32 [8, 192, 2, 128, 128], P('fsdp', 'dp'), as said below
- tile_bases: float32 [8, 192, 2, 128, 128], P('fsdp', 'dp'), as said below
Outputs:
- block_out: float32 [2, 16, 1024, 1024], P(None, 'dp', 'fsdp')
- grad_in: float32 [2, 16, 1024, 1024], P(None, 'dp', 'fsdp')
- vector_new: float32 [5, 1024], replicated
- vector_first_new: float32 [5, 1024], replicated
- vector_second_new: float32 [5, 1024], replicated
- w_in_new: bfloat16 [1024, 3072], P('fsdp')
- w_out_new: bfloat16 [1024, 1024], P('fsdp')
- w_gate_new: bfloat16 [1024, 4608], P('fsdp')
- w_up_new: bfloat16 [1024, 4608], P('fsdp')
- w_down_new: bfloat16 [1024, 4608], P('fsdp')
- tile_master_new: float32 [8, 192, 128, 128], P('fsdp', 'dp')
- tile_first_new: float32 [8, 192, 128, 128], P('fsdp', 'dp')
- tile_second_new: float32 [8, 192, 128, 128], P('fsdp', 'dp')
- tile_stats_new: float32 [8, 192, 2, 128, 128], P('fsdp', 'dp')
- tile_bases_new: float32 [8, 192, 2, 128, 128], P('fsdp', 'dp')
The draws below stay inside these ranges and needn't reach their ends.
Inputs may be any that keep to these rules, and one draw needn't show every extreme that they name: `lengths`: positions below a sequence's length are live, the rest padding; in each sequence index some micro-batch is full, and some entry is 512. `tile_owner`: no owner gets more than 12 tiles of one shard; in every shard one owner gets exactly 12. `tile_stats`: each matrix is symmetric positive definite. `tile_bases`: each matrix is orthogonal.
All inputs are finite; a program needn't handle non-finite values.
Results may differ from the reference program's by a relative error of at most 0.0085.
Values may be sent and summed in bfloat16 or wider, within the bound.
No kernel may reach another device: no remote copies, remote signals or barrier semaphores. Data moves between devices by JAX's collectives and lax.ppermute only.
A program may use at most 768 MiB of HBM per device.

```python
import math
import jax
import jax.numpy as jnp
from jax import lax

D = 1024
FF = 4608
MICRO = 2
P_SIZE = 128
STEP = 10
SEQS = 16
SHARDS = 8
SLOT = 1024
COLS = 17920
TILES = 140
CAP = 12
SLOTS = 192


def draw_lengths(key, part):
    key = jax.random.fold_in(key, 11)
    key_list = jax.random.split(key, 3)
    base_len = jax.random.randint(key_list[0], (MICRO, SEQS), SLOT // 2, SLOT + 1)
    full_micro = jax.random.randint(key_list[1], (SEQS,), 0, MICRO)
    micro_index = jnp.arange(MICRO)[:, None]
    seq_index = jnp.arange(SEQS)[None, :]
    result_len = jnp.where(micro_index == full_micro[None, :], SLOT, base_len)
    short_seq = jax.random.randint(key_list[2], (), 0, SEQS)
    short_micro = (full_micro[short_seq] + 1) % MICRO
    result_len = jnp.where((micro_index == short_micro) & (seq_index == short_seq), SLOT // 2, result_len)
    return result_len.astype(jnp.int32)


def draw_vector_params(key, part):
    key = jax.random.fold_in(key, 12)
    first_key, second_key = jax.random.split(key)
    gain_rows = 1.0 + 0.4 * jax.random.uniform(first_key, (2, D), jnp.float32, -1.0, 1.0)
    kernel = jax.random.uniform(second_key, (3, D), jnp.float32, -0.8, 0.8)
    return jnp.concatenate([gain_rows, kernel], axis=0)


def owner_shard(shard_key):
    first_key, second_key, third_key = jax.random.split(shard_key, 3)
    full_owner = jax.random.randint(first_key, (), 0, SEQS)
    others = jax.random.permutation(second_key, (SEQS - 1) * CAP)[:TILES - CAP] // CAP
    others = others + (others >= full_owner).astype(others.dtype)
    owners_all = jnp.concatenate([jnp.full((CAP,), full_owner, jnp.int32), others.astype(jnp.int32)])
    return jax.random.permutation(third_key, owners_all).astype(jnp.int32)


def draw_tile_owner(key, part):
    key = jax.random.fold_in(key, 13)
    shard_keys = jax.random.split(key, SHARDS)
    return jax.vmap(owner_shard)(shard_keys)


def draw_tile_stats(key, part):
    key = jax.random.fold_in(key, 14)
    level = 0.1875 * MICRO * SEQS * SLOT * P_SIZE
    diag_vals = level * jnp.exp(jax.random.uniform(key, (SHARDS, SLOTS, 2, P_SIZE), jnp.float32, 0.0, math.log(4.0)))
    return diag_vals[..., None] * jnp.eye(P_SIZE, dtype=jnp.float32)


def one_perm(perm_key):
    return jax.random.permutation(perm_key, P_SIZE)


def draw_tile_bases(key, part):
    key = jax.random.fold_in(key, 15)
    perm_key, sign_key = jax.random.split(key)
    total = SHARDS * SLOTS * 2
    perms = jax.vmap(one_perm)(jax.random.split(perm_key, total))
    signs = (2 * jax.random.randint(sign_key, (total, P_SIZE), 0, 2) - 1).astype(jnp.float32)
    freq = perms.astype(jnp.float32)[:, :, None]
    column = jnp.arange(P_SIZE, dtype=jnp.float32)[None, None, :]
    factor = jnp.where(freq == 0.0, math.sqrt(1.0 / P_SIZE), math.sqrt(2.0 / P_SIZE))
    table = factor * jnp.cos(math.pi * (2.0 * column + 1.0) * freq / (2.0 * P_SIZE))
    return (table * signs[:, :, None]).reshape(SHARDS, SLOTS, 2, P_SIZE, P_SIZE)


def block_scale(stream_key, shape, pieces, least, high):
    def one(position, parts):
        draws = jax.random.uniform(jax.random.fold_in(jax.random.fold_in(stream_key, 6), position), (parts,), jnp.float32, least / len(pieces), high / len(pieces))
        return jnp.repeat(jnp.exp(draws), shape[position] // parts).reshape((-1,) + (1,) * (len(shape) - position - 1))

    level = one(*pieces[0])
    for cut in pieces[1:]:
        level = level * one(*cut)
    return level


def gaussian(key, shape, scale, bound, pieces=(), held_as=jnp.bfloat16):
    gain = block_scale(key, shape, pieces, -0.22, 0.18) if pieces else 1.0
    result = jax.random.normal(key, shape, jnp.float32) * scale * gain
    return jnp.minimum(jnp.maximum(result, -bound), bound).astype(held_as)


def setup_inputs(seed: int = 0) -> dict:
    keys = jax.random.split(jax.random.key(seed), 18)
    block_in = gaussian(keys[0], (MICRO, SEQS, SLOT, D), 1.0, 6.0, ((1, 16), (2, 8)))
    cotangent = gaussian(keys[1], (MICRO, SEQS, SLOT, D), 1.0, 6.0, ((1, 16), (2, 8)), jnp.float32)
    lengths = draw_lengths(jax.random.fold_in(keys[17], 71), 0)
    vector_params = draw_vector_params(jax.random.fold_in(keys[17], 71), 0)
    vector_first = gaussian(keys[4], (5, D), (0.5 * (0.75 * MICRO * SEQS * SLOT) ** 0.5), 448.0, (), jnp.float32)
    vector_second = jnp.clip(jnp.exp(jax.random.uniform(keys[5], (5, D), jnp.float32, math.log(6144.0), math.log(24576.0))), 6144.0, 24576.0)
    w_in = gaussian(keys[6], (D, 3 * D), D ** -0.5, 0.1875, ((0, 8),))
    w_out = gaussian(keys[7], (D, D), D ** -0.5, 0.1875, ((0, 8),))
    w_gate = gaussian(keys[8], (D, FF), D ** -0.5, 0.1875, ((0, 8),))
    w_up = gaussian(keys[9], (D, FF), D ** -0.5, 0.1875, ((0, 8),))
    w_down = gaussian(keys[10], (D, FF), FF ** -0.5, 0.09375, ((0, 8),))
    tile_owner = draw_tile_owner(jax.random.fold_in(keys[17], 71), 0)
    tile_master = gaussian(keys[12], (SHARDS, SLOTS, P_SIZE, P_SIZE), 0.03, 0.4375, ((0, 8), (1, 16)), jnp.float32)
    tile_first = gaussian(keys[13], (SHARDS, SLOTS, P_SIZE, P_SIZE), (0.5 * (0.75 * MICRO * SEQS * SLOT) ** 0.5), 448.0, ((0, 8), (1, 16)), jnp.float32)
    tile_second = jnp.clip(jnp.exp(math.log(24576.0) - 1.3862944 * jax.random.uniform(keys[14], (SHARDS, SLOTS, P_SIZE, P_SIZE), jnp.float32) ** block_scale(keys[14], (SHARDS, SLOTS, P_SIZE, P_SIZE), ((0, 8), (1, 16)), -0.2, 0.2)), 6144.0, 24576.0)
    tile_stats = draw_tile_stats(jax.random.fold_in(keys[17], 71), 0)
    tile_bases = draw_tile_bases(jax.random.fold_in(keys[17], 71), 0)
    return {"block_in": block_in, "cotangent": cotangent, "lengths": lengths, "vector_params": vector_params, "vector_first": vector_first, "vector_second": vector_second, "w_in": w_in, "w_out": w_out, "w_gate": w_gate, "w_up": w_up, "w_down": w_down, "tile_owner": tile_owner, "tile_master": tile_master, "tile_first": tile_first, "tile_second": tile_second, "tile_stats": tile_stats, "tile_bases": tile_bases}


@jax.custom_vjp
def low(v):
    return lax.optimization_barrier(v.astype(jnp.bfloat16)).astype(jnp.float32)

@jax.custom_vjp
def low_back(v):
    return v

def low_keep(v):
    return (low(v), None)

def low_pass(kept, grad):
    return (grad,)

def back_keep(v):
    return (v, None)

def back_low(kept, grad):
    return (low(grad),)
low.defvjp(low_keep, low_pass)
low_back.defvjp(back_keep, back_low)
EPS_NORM = 1e-05
EPS_ADAM = 1e-08
BETA_ONE = 0.5
BETA_TWO = 0.5
BETA_STAT = 0.5
RATE_MATRIX = 0.03
RATE_VECTOR = 0.2
DECAY_WEIGHT = 0.01
PRECISE = lax.Precision.HIGHEST

def precise_dot(left_arr, right_arr):
    return jnp.dot(left_arr, right_arr, precision=PRECISE)

def rms_factor(values):
    return lax.rsqrt(lax.optimization_barrier(jnp.mean(values * values, axis=-1, keepdims=True)) + EPS_NORM)

def one_sequence(params, token_rows):
    vectors, w_in, w_out, w_gate, w_up, w_down = params
    model_width = token_rows.shape[1]
    normed = low(token_rows * rms_factor(token_rows) * vectors[0])
    mixed_all = low_back(precise_dot(normed, w_in))
    part_b = mixed_all[:, :model_width]
    part_c = mixed_all[:, model_width:2 * model_width]
    part_x = mixed_all[:, 2 * model_width:]
    product = part_b * part_x
    extended = jnp.concatenate([jnp.zeros((2, model_width), product.dtype), product], axis=0)
    convolved = vectors[2] * extended[:-2] + vectors[3] * extended[1:-1] + vectors[4] * extended[2:]
    gated_conv = low(part_c * convolved)
    branch = low_back(precise_dot(gated_conv, w_out))
    residual = token_rows + branch
    normed_two = low(residual * rms_factor(residual) * vectors[1])
    gate_val = low_back(precise_dot(normed_two, w_gate))
    up_val = low_back(precise_dot(normed_two, w_up))
    activation = low(jax.nn.silu(gate_val) * up_val)
    ffn_out = low_back(precise_dot(activation, w_down.T))
    return residual + ffn_out

def slot_table(owner_row, per_owner):
    tile_count = owner_row.shape[0]
    same_owner = owner_row[None, :] == owner_row[:, None]
    before = jnp.arange(tile_count, dtype=jnp.int32)[None, :] < jnp.arange(tile_count, dtype=jnp.int32)[:, None]
    slot_rank = lax.optimization_barrier(jnp.sum((same_owner & before).astype(jnp.int32), axis=1))
    return (owner_row * per_owner + slot_rank).astype(jnp.int32)

def rotate_into(left_basis, matrix, right_basis):
    step_one = jnp.einsum('sji,sjk->sik', left_basis, matrix, precision=PRECISE)
    return jnp.einsum('sik,skl->sil', step_one, right_basis, precision=PRECISE)

def rotate_back(left_basis, matrix, right_basis):
    step_one = jnp.einsum('sij,sjk->sik', left_basis, matrix, precision=PRECISE)
    return jnp.einsum('sik,slk->sil', step_one, right_basis, precision=PRECISE)

def solve_lower(lower_factor, rhs_matrix):
    return jax.scipy.linalg.solve_triangular(lower_factor, rhs_matrix, lower=True)

def orthonormal(matrix):
    gram = jnp.einsum('sji,sjk->sik', matrix, matrix, precision=PRECISE)
    lower_factor = jnp.linalg.cholesky(gram)
    solved = jax.vmap(solve_lower)(lower_factor, jnp.swapaxes(matrix, 1, 2))
    return jnp.swapaxes(solved, 1, 2)

def soap_update(grad_tiles, master, first, second, stats, bases):
    left_basis = bases[:, 0]
    right_basis = bases[:, 1]
    rotated = rotate_into(left_basis, grad_tiles, right_basis)
    first_new = BETA_ONE * first + (1.0 - BETA_ONE) * grad_tiles
    second_new = BETA_TWO * second + (1.0 - BETA_TWO) * rotated * rotated
    moment_rot = rotate_into(left_basis, first_new, right_basis)
    direction = moment_rot / (1.0 - BETA_ONE ** STEP) / (jnp.sqrt(second_new / (1.0 - BETA_TWO ** STEP)) + EPS_ADAM)
    master_new = master - RATE_MATRIX * (rotate_back(left_basis, direction, right_basis) + DECAY_WEIGHT * master)
    stat_left = BETA_STAT * stats[:, 0] + (1.0 - BETA_STAT) * jnp.einsum('sik,sjk->sij', grad_tiles, grad_tiles, precision=PRECISE)
    stat_right = BETA_STAT * stats[:, 1] + (1.0 - BETA_STAT) * jnp.einsum('ski,skj->sij', grad_tiles, grad_tiles, precision=PRECISE)
    left_new = orthonormal(jnp.einsum('sij,sjk->sik', stat_left, left_basis, precision=PRECISE))
    right_new = orthonormal(jnp.einsum('sij,sjk->sik', stat_right, right_basis, precision=PRECISE))
    return (master_new, first_new, second_new, jnp.stack([stat_left, stat_right], axis=1), jnp.stack([left_new, right_new], axis=1))

def reference(block_in, cotangent, lengths, vector_params, vector_first, vector_second, w_in, w_out, w_gate, w_up, w_down, tile_owner, tile_master, tile_first, tile_second, tile_stats, tile_bases):
    model_width = block_in.shape[3]
    slot_len = block_in.shape[2]
    inputs = block_in.astype(jnp.float32).reshape(-1, slot_len, model_width)
    params = (vector_params, w_in.astype(jnp.float32), w_out.astype(jnp.float32), w_gate.astype(jnp.float32), w_up.astype(jnp.float32), w_down.astype(jnp.float32))

    def forward(params_all, inputs_all):

        def sequence_step(token_rows):
            return jax.checkpoint(one_sequence)(params_all, token_rows)
        return lax.map(sequence_step, inputs_all)
    outputs, pullback = jax.vjp(forward, params, inputs)
    positions = jnp.arange(slot_len, dtype=jnp.int32)
    live_mask = (positions[None, None, :] < lengths[:, :, None]).astype(outputs.dtype)
    seed_grad = (cotangent.astype(outputs.dtype) * live_mask[..., None]).reshape(outputs.shape)
    grads_params, grads_inputs = pullback(seed_grad)
    grad_vec = grads_params[0]
    vec_first = BETA_ONE * vector_first + (1.0 - BETA_ONE) * grad_vec
    vec_second = BETA_TWO * vector_second + (1.0 - BETA_TWO) * grad_vec * grad_vec
    vec_new = vector_params - RATE_VECTOR * (vec_first / (1.0 - BETA_ONE ** STEP)) / (jnp.sqrt(vec_second / (1.0 - BETA_TWO ** STEP)) + EPS_ADAM)
    grad_whole = jnp.concatenate(grads_params[1:], axis=1)
    tile_rows = D // SHARDS // P_SIZE
    tile_cols = COLS // P_SIZE
    tiles = grad_whole.reshape(SHARDS, tile_rows, P_SIZE, tile_cols, P_SIZE).transpose(0, 1, 3, 2, 4).reshape(SHARDS, TILES, P_SIZE, P_SIZE)
    slot_index = jax.vmap(lambda owner_row: slot_table(owner_row, CAP))(tile_owner)

    def place_tiles(shard_tiles, shard_slots):
        return jnp.zeros((SLOTS, P_SIZE, P_SIZE), shard_tiles.dtype).at[shard_slots].set(shard_tiles)
    slot_grads = jax.vmap(place_tiles)(tiles, slot_index)

    def flatten(array):
        return array.reshape((SHARDS * SLOTS,) + array.shape[2:])

    def unflatten(array):
        return array.reshape((SHARDS, SLOTS) + array.shape[1:])
    updated = soap_update(flatten(slot_grads), flatten(tile_master), flatten(tile_first), flatten(tile_second), flatten(tile_stats), flatten(tile_bases))
    master_new, first_new, second_new, stats_new, bases_new = [unflatten(item) for item in updated]
    copies = master_new.astype(jnp.bfloat16)
    tiles_back = jax.vmap(lambda copy_set, shard_slots: copy_set[shard_slots])(copies, slot_index)
    whole_new = tiles_back.reshape(SHARDS, tile_rows, tile_cols, P_SIZE, P_SIZE).transpose(0, 1, 3, 2, 4).reshape(D, COLS)
    w_in_new = whole_new[:, :3 * D]
    w_out_new = whole_new[:, 3 * D:4 * D]
    w_gate_new = whole_new[:, 4 * D:4 * D + FF]
    w_up_new = whole_new[:, 4 * D + FF:4 * D + 2 * FF]
    w_down_new = whole_new[:, 4 * D + 2 * FF:]
    block_out = outputs.reshape(block_in.shape)
    grad_in = grads_inputs.reshape(block_in.shape)
    return (block_out, grad_in, vec_new, vec_first, vec_second, w_in_new, w_out_new, w_gate_new, w_up_new, w_down_new, master_new, first_new, second_new, stats_new, bases_new)
```

```python
import functools

import jax
import jax.numpy as jnp
from jax import lax
from jax.experimental import pallas as pl
from jax.experimental.pallas import tpu as pltpu
from jax.sharding import PartitionSpec as P

STEP = 10


EPS_NORM = 1e-05
EPS_ADAM = 1e-08
BETA_ONE = 0.5
BETA_TWO = 0.5
BETA_STAT = 0.5
RATE_MATRIX = 0.03
RATE_VECTOR = 0.2
DECAY_WEIGHT = 0.01
PRECISE = lax.Precision.HIGHEST
BACK_DIMS = (((1,), (1,)), ((), ()))
TOKEN_DIMS = (((0,), (0,)), ((), ()))

PANEL = 32


def from_behind(value, axis, by):
    length = lax.axis_size(axis)
    pairs = [(i, i + by) for i in range(length) if 0 <= i + by < length]
    return lax.ppermute(value, axis, pairs)


def flip(value, axis, bit):
    length = lax.axis_size(axis)
    return lax.ppermute(value, axis, [(i, i ^ bit) for i in range(length)])


def sum_all(value):
    for axis, bit in (("dp", 1), ("fsdp", 1), ("fsdp", 2), ("fsdp", 4), ("dp", 2), ("dp", 4), ("dp", 8)):
        value = value + flip(value, axis, bit)
    return value


def rms_factor(values):
    return lax.rsqrt(jnp.mean(values * values, axis=-1, keepdims=True) + EPS_NORM)


def norm_back(values, scale_val, gain_row, grad_out):
    weighted = grad_out * gain_row
    inner = jnp.mean(values * weighted, axis=-1, keepdims=True)
    grad_values = scale_val * weighted - values * scale_val * scale_val * scale_val * inner
    grad_gain = jnp.sum(values * scale_val * grad_out, axis=0)
    return (grad_values, grad_gain)


def outer_sum(left_arr, right_arr):
    return lax.dot_general(left_arr, right_arr, TOKEN_DIMS, preferred_element_type=jnp.float32)


def back_dot(left_arr, right_arr):
    return lax.dot_general(left_arr, right_arr, BACK_DIMS, preferred_element_type=jnp.float32)


def exchange(value, axis, groups=None):
    return lax.all_to_all(value, axis, 0, 0, axis_index_groups=groups)


def token_scatter(partial_rows):
    parts = lax.axis_size("fsdp")
    cut = partial_rows.astype(jnp.bfloat16).reshape(parts, -1, partial_rows.shape[1])
    return jnp.sum(exchange(cut, "fsdp").astype(jnp.float32), axis=0)


def to_columns(shard):
    parts = lax.axis_size("fsdp")
    rows, width = shard.shape
    cut = shard.reshape(rows, parts, width // parts).transpose(1, 0, 2)
    return exchange(cut, "fsdp").reshape(parts * rows, width // parts)


def chip_sum(value, core):
    parts = lax.axis_size("fsdp")
    half = value.shape[0] // parts // 2
    cut = value.reshape(parts, 2, half, value.shape[1])
    mine = lax.dynamic_index_in_dim(cut, core, 1, keepdims=False)
    other = lax.dynamic_index_in_dim(cut, 1 - core, 1, keepdims=False)
    return mine + flip(other.astype(jnp.bfloat16), "dp", 1).astype(jnp.float32)


def slot_table(owner_row, per_owner):
    tile_count = owner_row.shape[0]
    same_owner = owner_row[None, :] == owner_row[:, None]
    before = (
        jnp.arange(tile_count, dtype=jnp.int32)[None, :]
        < jnp.arange(tile_count, dtype=jnp.int32)[:, None]
    )
    slot_rank = jnp.sum((same_owner & before).astype(jnp.int32), axis=1)
    return owner_row * per_owner + slot_rank


def rotate_into(left_basis, matrix, right_basis):
    step_one = jnp.einsum("sji,sjk->sik", left_basis, matrix, precision=PRECISE)
    return jnp.einsum("sik,skl->sil", step_one, right_basis, precision=PRECISE)


def rotate_back(left_basis, matrix, right_basis):
    step_one = jnp.einsum("sij,sjk->sik", left_basis, matrix, precision=PRECISE)
    return jnp.einsum("sik,slk->sil", step_one, right_basis, precision=PRECISE)


def orthonormal_kernel(m_ref, q_ref, w_ref):
    count, side = m_ref.shape[0], m_ref.shape[1]
    shape = (PANEL, side)
    rows = lax.broadcasted_iota(jnp.int32, shape, 0)
    lanes = lax.broadcasted_iota(jnp.int32, shape, 1)
    all_rows = lax.broadcasted_iota(jnp.int32, (side, side), 0)
    all_lanes = lax.broadcasted_iota(jnp.int32, (side, side), 1)
    for g in range(count):
        w_ref[g] = lax.dot_general(
            m_ref[g], m_ref[g], TOKEN_DIMS, precision=PRECISE, preferred_element_type=jnp.float32
        )

    def block(b, carry):
        base = pl.multiple_of(b * PANEL, PANEL)
        panels = [w_ref[g, pl.ds(base, PANEL), :] for g in range(count)]
        pivots = [jnp.zeros(shape, jnp.float32)] * count
        for k in range(PANEL):
            first = (k // 8) * 8
            row, lane = rows[first:], lanes[first:]
            copies = (PANEL - first) // 8
            for g in range(count):
                part = panels[g][first:]
                column = jnp.broadcast_to(part[:, k : k + 1], part.shape)
                pivot = jnp.broadcast_to(column[k - first : k - first + 1], (8, side))
                top = jnp.broadcast_to(part[k - first : k - first + 1], (8, side))
                top = jnp.where(lane[:8] == k, 1.0, top)
                scaled = jnp.concatenate([top / pivot] * copies, 0)
                kept = jnp.where((lane == k) & (row > k), 0.0, part)
                part = kept - jnp.where(row > k, column, 0.0) * scaled
                part = jnp.where(row == k, jnp.concatenate([top] * copies, 0), part)
                panels[g] = jnp.concatenate([panels[g][:first], part], 0) if first else part
                pivots[g] = jnp.where(rows == k, jnp.concatenate([pivot] * (PANEL // 8), 0), pivots[g])
        below = all_rows >= base + PANEL
        for g in range(count):
            done = panels[g] * lax.rsqrt(pivots[g])
            coef = jnp.where((lanes >= PANEL) & (lanes < side - base), done, 0.0)
            source = jnp.where((lanes < PANEL) & (lanes > rows), 0.0, done)
            change = lax.dot_general(
                coef, source, TOKEN_DIMS, precision=PRECISE, preferred_element_type=jnp.float32
            )
            change = pltpu.roll(change, base, 0)
            kept = jnp.where(below & (all_lanes < PANEL), 0.0, w_ref[g])
            w_ref[g] = kept - jnp.where(below, change, 0.0)
            w_ref[g, pl.ds(base, PANEL), :] = done
            w_ref[g] = pltpu.roll(w_ref[g], side - PANEL, 1)
        return carry

    lax.fori_loop(0, side // PANEL, block, 0)
    for g in range(count):
        inverse = jnp.where(all_lanes <= all_rows, w_ref[g], 0.0)
        q_ref[g] = lax.dot_general(
            m_ref[g], inverse, BACK_DIMS, precision=PRECISE, preferred_element_type=jnp.float32
        )


def orthonormal(matrix):
    return pl.pallas_call(
        orthonormal_kernel,
        out_shape=jax.ShapeDtypeStruct(matrix.shape, jnp.float32),
        in_specs=[pl.BlockSpec(memory_space=pltpu.VMEM)],
        out_specs=pl.BlockSpec(memory_space=pltpu.VMEM),
        scratch_shapes=[pltpu.VMEM(matrix.shape, jnp.float32)],
        compiler_params=pltpu.CompilerParams(vmem_limit_bytes=32 * 2**20),
    )(matrix)


def soap_update(grad_tiles, master, first, second, stats, bases):
    left_basis = bases[:, 0]
    right_basis = bases[:, 1]
    rotated = rotate_into(left_basis, grad_tiles, right_basis)
    first_new = BETA_ONE * first + (1.0 - BETA_ONE) * grad_tiles
    second_new = BETA_TWO * second + (1.0 - BETA_TWO) * rotated * rotated
    moment_rot = rotate_into(left_basis, first_new, right_basis)
    direction = (
        moment_rot
        / (1.0 - BETA_ONE**STEP)
        / (jnp.sqrt(second_new / (1.0 - BETA_TWO**STEP)) + EPS_ADAM)
    )
    master_new = master - RATE_MATRIX * (
        rotate_back(left_basis, direction, right_basis) + DECAY_WEIGHT * master
    )
    stat_left = BETA_STAT * stats[:, 0] + (1.0 - BETA_STAT) * jnp.einsum(
        "sik,sjk->sij", grad_tiles, grad_tiles, precision=PRECISE
    )
    stat_right = BETA_STAT * stats[:, 1] + (1.0 - BETA_STAT) * jnp.einsum(
        "ski,skj->sij", grad_tiles, grad_tiles, precision=PRECISE
    )
    stats_new = jnp.stack([stat_left, stat_right], axis=1)
    turned = jnp.einsum("stij,stjk->stik", stats_new, bases, precision=PRECISE)
    bases_new = orthonormal(turned.reshape((-1,) + turned.shape[2:])).reshape(bases.shape)
    return (master_new, first_new, second_new, stats_new, bases_new)


def shards(
    block_in,
    cotangent,
    lengths,
    vector_params,
    vector_first,
    vector_second,
    w_in,
    w_out,
    w_gate,
    w_up,
    w_down,
    tile_owner,
    tile_master,
    tile_first,
    tile_second,
    tile_stats,
    tile_bases,
):
    micro_count, _, tok_count, model_width = block_in.shape
    hidden_width = w_gate.shape[1]
    parts = lax.axis_size("fsdp")
    core = lax.axis_index("dp") % 2
    g_one, g_two, k_zero, k_one, k_two = [vector_params[i] for i in range(5)]

    whole_in = lax.all_gather(w_in, "fsdp", axis=0, tiled=True)
    whole_out = lax.all_gather(w_out, "fsdp", axis=0, tiled=True)
    positions = lax.axis_index("fsdp") * tok_count + jnp.arange(tok_count, dtype=jnp.int32)
    live_mask = (positions[None, :] < lengths).astype(jnp.float32)[:, :, None]
    seed_grad = (cotangent[:, 0] * live_mask).reshape(-1, model_width)
    grad_feed = lax.all_gather(seed_grad.astype(jnp.bfloat16), "fsdp", axis=0, tiled=True)
    gate_cols = to_columns(w_gate)
    up_cols = to_columns(w_up)
    down_cols = to_columns(w_down)

    token_rows = block_in.astype(jnp.float32).reshape(-1, model_width)
    scale_one = rms_factor(token_rows)
    normed = (token_rows * scale_one * g_one).astype(jnp.bfloat16)
    mixed_all = jnp.dot(normed, whole_in, preferred_element_type=jnp.float32)
    part_b = mixed_all[:, :model_width]
    part_c = mixed_all[:, model_width : 2 * model_width]
    part_x = mixed_all[:, 2 * model_width :]
    product = (part_b * part_x).reshape(micro_count, tok_count, model_width)
    extended = jnp.concatenate([from_behind(product[:, -2:], "fsdp", 1), product], axis=1)
    convolved = (
        k_zero * extended[:, :-2] + k_one * extended[:, 1:-1] + k_two * extended[:, 2:]
    ).reshape(-1, model_width)
    gated_conv = (part_c * convolved).astype(jnp.bfloat16)
    residual = token_rows + jnp.dot(gated_conv, whole_out, preferred_element_type=jnp.float32)
    scale_two = rms_factor(residual)
    normed_two = (residual * scale_two * g_two).astype(jnp.bfloat16)

    fed = lax.all_gather(normed_two, "fsdp", axis=0, tiled=True)
    gate_val = jnp.dot(fed, gate_cols, preferred_element_type=jnp.float32)
    up_val = jnp.dot(fed, up_cols, preferred_element_type=jnp.float32)
    sigmoid_gate = jax.nn.sigmoid(gate_val)
    activation = (gate_val * sigmoid_gate * up_val).astype(jnp.bfloat16)
    grad_act = jnp.dot(grad_feed, down_cols, preferred_element_type=jnp.float32)
    grad_gate = (grad_act * up_val * sigmoid_gate * (1.0 + gate_val * (1.0 - sigmoid_gate))).astype(
        jnp.bfloat16
    )
    grad_up = (grad_act * gate_val * sigmoid_gate).astype(jnp.bfloat16)
    grad_normed_two = token_scatter(back_dot(grad_gate, gate_cols) + back_dot(grad_up, up_cols))
    result_rows = residual + lax.psum_scatter(
        back_dot(activation, down_cols).astype(jnp.bfloat16), "fsdp", scatter_dimension=0, tiled=True
    ).astype(jnp.float32)
    feed_grads = jnp.concatenate(
        [outer_sum(fed, grad_gate), outer_sum(fed, grad_up), outer_sum(grad_feed, activation)], axis=1
    )
    feed_half = exchange(chip_sum(feed_grads, core).astype(jnp.bfloat16), "fsdp")
    half_rows = feed_half.shape[1]
    feed_half = (
        feed_half.reshape(parts, half_rows, 3, -1).transpose(1, 2, 0, 3).reshape(half_rows, 3 * hidden_width)
    )

    grad_res_norm, grad_gain_two = norm_back(residual, scale_two, g_two, grad_normed_two)
    grad_resid = seed_grad + grad_res_norm
    grad_branch = grad_resid.astype(jnp.bfloat16)
    grad_gated = back_dot(grad_branch, whole_out)
    grad_part_c = grad_gated * convolved
    grad_conv = (grad_gated * part_c).reshape(micro_count, tok_count, model_width)
    grad_ext = jnp.concatenate([grad_conv, from_behind(grad_conv[:, :2], "fsdp", -1)], axis=1)
    grad_product = (
        k_two * grad_conv + k_one * grad_ext[:, 1 : tok_count + 1] + k_zero * grad_ext[:, 2:]
    ).reshape(-1, model_width)
    grad_kernel = jnp.stack(
        [
            jnp.sum(grad_conv * extended[:, :-2], axis=(0, 1)),
            jnp.sum(grad_conv * extended[:, 1:-1], axis=(0, 1)),
            jnp.sum(grad_conv * extended[:, 2:], axis=(0, 1)),
        ]
    )
    grad_mixed = jnp.concatenate(
        [grad_product * part_x, grad_part_c, grad_product * part_b], axis=1
    ).astype(jnp.bfloat16)
    conv_grads = jnp.concatenate([outer_sum(normed, grad_mixed), outer_sum(gated_conv, grad_branch)], axis=1)
    conv_half = exchange(chip_sum(conv_grads, core).astype(jnp.bfloat16), "fsdp")
    conv_half = jnp.sum(conv_half.astype(jnp.float32), axis=0).astype(jnp.bfloat16)
    grad_normed = back_dot(grad_mixed, whole_in)
    grad_rows_norm, grad_gain_one = norm_back(token_rows, scale_one, g_one, grad_normed)
    grad_rows = grad_resid + grad_rows_norm

    vector_grads = sum_all(
        jnp.concatenate([grad_gain_one[None], grad_gain_two[None], grad_kernel], axis=0)
    )
    vec_first = BETA_ONE * vector_first + (1.0 - BETA_ONE) * vector_grads
    vec_second = BETA_TWO * vector_second + (1.0 - BETA_TWO) * vector_grads * vector_grads
    vec_new = vector_params - RATE_VECTOR * (vec_first / (1.0 - BETA_ONE**STEP)) / (
        jnp.sqrt(vec_second / (1.0 - BETA_TWO**STEP)) + EPS_ADAM
    )

    tile_side = tile_master.shape[-1]
    per_owner = tile_master.shape[1]
    owners = lax.axis_size("dp")
    half_grads = jnp.concatenate([conv_half, feed_half], axis=1)
    all_cols = half_grads.shape[1]
    tile_cols = all_cols // tile_side
    half_tiles = half_grads.reshape(half_rows, tile_cols, tile_side).transpose(1, 0, 2)
    slot_index = slot_table(tile_owner[0], per_owner)
    slot_match = slot_index[None, :] == jnp.arange(per_owner * owners, dtype=jnp.int32)[:, None]
    source = jnp.sum(
        jnp.where(slot_match, jnp.arange(tile_cols, dtype=jnp.int32)[None, :], 0), axis=1
    )
    filled = jnp.any(slot_match, axis=1)
    outgoing = jnp.where(
        filled[:, None, None], jnp.take(half_tiles, source, axis=0), jnp.zeros((), jnp.bfloat16)
    )
    chips = owners // 2
    same_core = [[2 * i + c for i in range(chips)] for c in range(2)]
    arrived = exchange(
        outgoing.reshape(chips, 2 * per_owner, half_rows, tile_side), "dp", same_core
    )
    chip_slots = jnp.sum(arrived.astype(jnp.float32), axis=0).reshape(
        2, per_owner, half_rows, tile_side
    )
    mine = lax.dynamic_index_in_dim(chip_slots, core, 0, keepdims=False)
    theirs = flip(lax.dynamic_index_in_dim(chip_slots, 1 - core, 0, keepdims=False), "dp", 1)
    owned_grads = jnp.where(
        core == 0,
        jnp.concatenate([mine, theirs], axis=1),
        jnp.concatenate([theirs, mine], axis=1),
    )
    master_new, first_new, second_new, stats_new, bases_new = soap_update(
        owned_grads, tile_master[0], tile_first[0], tile_second[0], tile_stats[0], tile_bases[0]
    )
    gathered = lax.all_gather(master_new.astype(jnp.bfloat16), "dp", axis=0, tiled=True)
    tiles_back = jnp.take(gathered, slot_index, axis=0)
    whole_new = tiles_back.transpose(1, 0, 2).reshape(tile_side, all_cols)
    w_in_new = whole_new[:, : 3 * model_width]
    w_out_new = whole_new[:, 3 * model_width : 4 * model_width]
    w_gate_new = whole_new[:, 4 * model_width : 4 * model_width + hidden_width]
    w_up_new = whole_new[:, 4 * model_width + hidden_width : 4 * model_width + 2 * hidden_width]
    w_down_new = whole_new[:, 4 * model_width + 2 * hidden_width :]
    whole_shape = (micro_count, 1, tok_count, model_width)
    return (
        result_rows.reshape(whole_shape),
        grad_rows.reshape(whole_shape),
        vec_new,
        vec_first,
        vec_second,
        w_in_new,
        w_out_new,
        w_gate_new,
        w_up_new,
        w_down_new,
        master_new[None],
        first_new[None],
        second_new[None],
        stats_new[None],
        bases_new[None],
    )


def solution(mesh):
    return jax.shard_map(
        shards,
        mesh=mesh,
        in_specs=(
            P(None, "dp", "fsdp", None),
            P(None, "dp", "fsdp", None),
            P(None, "dp"),
            P(),
            P(),
            P(),
            P("fsdp", None),
            P("fsdp", None),
            P("fsdp", None),
            P("fsdp", None),
            P("fsdp", None),
            P("fsdp", None),
            P("fsdp", "dp", None, None),
            P("fsdp", "dp", None, None),
            P("fsdp", "dp", None, None),
            P("fsdp", "dp", None, None, None),
            P("fsdp", "dp", None, None, None),
        ),
        out_specs=(
            P(None, "dp", "fsdp", None),
            P(None, "dp", "fsdp", None),
            P(),
            P(),
            P(),
            P("fsdp", None),
            P("fsdp", None),
            P("fsdp", None),
            P("fsdp", None),
            P("fsdp", None),
            P("fsdp", "dp", None, None),
            P("fsdp", "dp", None, None),
            P("fsdp", "dp", None, None),
            P("fsdp", "dp", None, None, None),
            P("fsdp", "dp", None, None, None),
        ),
        check_vma=False,
    )
```

```python
import functools

import jax
import jax.numpy as jnp
from jax import lax
from jax.experimental import pallas as pl
from jax.experimental.pallas import tpu as pltpu
from jax.sharding import PartitionSpec as P

STEP = 10


EPS_NORM = 1e-05
EPS_ADAM = 1e-08
BETA_ONE = 0.5
BETA_TWO = 0.5
BETA_STAT = 0.5
RATE_MATRIX = 0.03
RATE_VECTOR = 0.2
DECAY_WEIGHT = 0.01
PRECISE = lax.Precision.HIGHEST
BACK_DIMS = (((1,), (1,)), ((), ()))
TOKEN_DIMS = (((0,), (0,)), ((), ()))

PANEL = 32


def from_behind(value, axis, by):
    length = lax.axis_size(axis)
    pairs = [(i, i + by) for i in range(length) if 0 <= i + by < length]
    return lax.ppermute(value, axis, pairs)


def flip(value, axis, bit):
    length = lax.axis_size(axis)
    return lax.ppermute(value, axis, [(i, i ^ bit) for i in range(length)])


RING = 4


def ring(value, axis, by):
    length = lax.axis_size(axis)
    low = 2 if axis == "dp" else 1
    pairs = []
    for i in range(length):
        place = i // low % RING
        pairs.append((i, i + ((place + by) % RING - place) * low))
    return lax.ppermute(value, axis, pairs)


def pair(value, axis):
    return flip(value, axis, lax.axis_size(axis) // 2)


def swap(value):
    return flip(value, "dp", 1)


def place_of(axis):
    index = lax.axis_index(axis)
    low = 2 if axis == "dp" else 1
    return index // low % RING, index // (low * RING)


def spread(block, axis):
    half = block.shape[0] // 2
    before, after, side = ring(block, axis, 1), ring(block, axis, -1), pair(block, axis)
    fore = ring(jnp.concatenate([before[:half], side[:half]]), axis, 1)
    back = ring(jnp.concatenate([after[half:], side[half:]]), axis, -1)
    cross = pair(jnp.concatenate([before[half:], after[:half]]), axis)
    far_one = ring(fore[half:], axis, 1)
    far_two = ring(back[half:], axis, -1)
    return [
        (block, [(0, 2 * half, 0, 0, None)]),
        (before, [(0, 2 * half, -1, 0, None)]),
        (after, [(0, 2 * half, 1, 0, None)]),
        (side, [(0, 2 * half, 0, 1, None)]),
        (fore, [(0, half, 2, 0, 0), (half, half, -1, 1, 0)]),
        (back, [(0, half, 2, 0, 1), (half, half, 1, 1, 1)]),
        (cross, [(0, half, -1, 1, 1), (half, half, 1, 1, 0)]),
        (far_one, [(0, half, 2, 1, 0)]),
        (far_two, [(0, half, 2, 1, 1)]),
    ]


def spread_ring(block, axis):
    half = block.shape[0] // 2
    before, after = ring(block, axis, 1), ring(block, axis, -1)
    return jnp.concatenate(
        [block, before, after, ring(before[:half], axis, 1), ring(after[half:], axis, -1)]
    )


def collect_ring(parts, axis):
    size = parts.shape[0] // RING
    half = size // 2
    own, before, ahead = parts[:size], parts[size : 2 * size], parts[2 * size : 3 * size]
    low = jnp.bfloat16
    one = ring(parts[3 * size : 3 * size + half].astype(low), axis, -1)
    two = ring(parts[3 * size + half :].astype(low), axis, 1)
    before = jnp.concatenate([before[:half] + one.astype(jnp.float32), before[half:]])
    ahead = jnp.concatenate([ahead[:half], ahead[half:] + two.astype(jnp.float32)])
    from_ahead = ring(before.astype(low), axis, -1)
    from_before = ring(ahead.astype(low), axis, 1)
    return own + from_ahead.astype(jnp.float32) + from_before.astype(jnp.float32)


def after(value, *others):
    return lax.optimization_barrier((value,) + others)[0]


def sum_over(value, axis):
    bit = 1
    while bit < lax.axis_size(axis):
        value = value + flip(value, axis, bit)
        bit *= 2
    return value


ANYWHERE = pl.BlockSpec(memory_space=pl.ANY)
SCALARS = pl.BlockSpec(memory_space=pltpu.SMEM)
INSIDE = pl.BlockSpec(memory_space=pltpu.VMEM)
ROOM = pltpu.CompilerParams(vmem_limit_bytes=56 * 2**20)


def assemble_kernel(spans, widths, offsets_ref, *refs):
    count = len(spans)
    pieces, outs, sems = refs[: -len(widths) - 1], refs[-len(widths) - 1 : -1], refs[-1]
    for i, (which, first, rows) in enumerate(spans):
        offset = pl.multiple_of(offsets_ref[i], rows)
        column = 0
        for j, width in enumerate(widths):
            pltpu.make_async_copy(
                pieces[which].at[pl.ds(first, rows), pl.ds(column, width)],
                outs[j].at[pl.ds(offset, rows), :],
                sems.at[j],
            ).start()
            column += width
    for j in range(len(widths)):
        pltpu.make_async_copy(outs[j], outs[j], sems.at[j]).wait()


def assemble(pieces, widths):
    core = lax.axis_index("dp") % 2
    place, side = place_of("fsdp")
    arrays, spans, offsets = [], [], []
    for who in range(2):
        for array, cuts in pieces:
            arrays.append(array if who == 0 else swap(array))
            for first, count, step, across, half in cuts:
                owner = (side ^ across) * RING + (place + step) % RING
                block = array.shape[0] // len(cuts) * (1 if half is None else 2)
                spans.append((len(arrays) - 1, first, count))
                offsets.append((owner * 2 + (core ^ who)) * block + (half or 0) * count)
    rows = 2 * block * 2 * RING
    return pl.pallas_call(
        functools.partial(assemble_kernel, spans, widths),
        out_shape=[jax.ShapeDtypeStruct((rows, width), pieces[0][0].dtype) for width in widths],
        in_specs=[SCALARS] + [ANYWHERE] * len(arrays),
        out_specs=[INSIDE] * len(widths),
        compiler_params=ROOM,
        scratch_shapes=[pltpu.SemaphoreType.DMA((len(widths),))],
    )(jnp.stack(offsets).astype(jnp.int32), *arrays)


def pick_kernel(table_ref, conv_ref, feed_ref, mine_ref, other_ref, held, sem):
    slots, side = mine_ref.shape[0], mine_ref.shape[1]
    half = side // 2
    held[...] = jnp.zeros_like(held)

    def one(i, finish):
        at = 5 * i
        kind, piece = table_ref[at], table_ref[at + 1]
        first = pl.multiple_of(table_ref[at + 4] * half, half)

        def move(source, target):
            copy = pltpu.make_async_copy(source, target, sem)
            if finish:
                copy.wait()
            else:
                copy.start()

        def column(k):
            return pl.ds(pl.multiple_of(k * side, side), side)

        @pl.when(kind == 1)
        def _():
            move(
                conv_ref.at[piece, :, column(table_ref[at + 2])], held.at[0, i, pl.ds(first, half), :]
            )

        for which in range(2):

            @pl.when((kind == 2) & (table_ref[at + 2 + which] >= 0))
            def _():
                move(feed_ref.at[piece + which, :, column(table_ref[at + 2 + which])], held.at[which, i])

    for finish in (False, True):

        def step(i, carry):
            one(i, finish)
            return carry

        lax.fori_loop(0, 2 * slots, step, 0)
    for q in range(slots):
        mine_ref[q] = held[0, q].astype(jnp.float32) + held[1, q].astype(jnp.float32)
        other_ref[q] = held[0, slots + q]


def pick(table, conv, feed, slots, side):
    shape = (slots, side, side)
    return pl.pallas_call(
        pick_kernel,
        out_shape=[jax.ShapeDtypeStruct(shape, jnp.float32), jax.ShapeDtypeStruct(shape, conv.dtype)],
        in_specs=[SCALARS, ANYWHERE, ANYWHERE],
        out_specs=[INSIDE, INSIDE],
        compiler_params=ROOM,
        scratch_shapes=[
            pltpu.VMEM((2, 2 * slots, side, side), conv.dtype),
            pltpu.SemaphoreType.DMA,
        ],
    )(table, conv, feed)


def put_kernel(core_ref, slot_ref, mine_ref, other_ref, *refs):
    count = (len(refs) - 3) // 2
    outs, pages = refs[:count], refs[count : 2 * count]
    held, in_sems, out_sems = refs[-3:]
    chips, slots, side = mine_ref.shape[0], mine_ref.shape[1], mine_ref.shape[2]
    loads = [
        pltpu.make_async_copy(source, held.at[i], in_sems.at[i])
        for i, source in enumerate((mine_ref, other_ref))
    ]
    for load in loads:
        load.start()
    for load in loads:
        load.wait()
    tile = 0
    for j in range(count):
        for k in range(outs[j].shape[1] // side):
            slot = slot_ref[tile]
            owner = slot // slots
            pages[j][:, k * side : (k + 1) * side] = held[owner % 2 ^ core_ref[0], owner // 2, slot % slots]
            tile += 1
        pltpu.make_async_copy(pages[j], outs[j], out_sems.at[j]).start()
    for j in range(count):
        pltpu.make_async_copy(pages[j], outs[j], out_sems.at[j]).wait()


def put(core, slot_index, mine, other, widths):
    side = mine.shape[-1]
    return pl.pallas_call(
        put_kernel,
        out_shape=[jax.ShapeDtypeStruct((side, width), mine.dtype) for width in widths],
        in_specs=[SCALARS, SCALARS, ANYWHERE, ANYWHERE],
        out_specs=[ANYWHERE] * len(widths),
        compiler_params=ROOM,
        scratch_shapes=[pltpu.VMEM((side, width), mine.dtype) for width in widths]
        + [
            pltpu.VMEM((2,) + mine.shape, mine.dtype),
            pltpu.SemaphoreType.DMA((2,)),
            pltpu.SemaphoreType.DMA((len(widths),)),
        ],
    )(core.astype(jnp.int32).reshape(1), slot_index, mine, other)


def feed_kernel(order_ref, fed_ref, dy_ref, w_ref, both_ref, act_ref, own_ref, other_ref, out_ref):
    width = act_ref.shape[-1]
    mixed = jnp.dot(fed_ref[0], w_ref[:, : 2 * width], preferred_element_type=jnp.float32)
    grad_act = jnp.dot(dy_ref[0], w_ref[:, 2 * width :], preferred_element_type=jnp.float32)
    gate, up = mixed[:, :width], mixed[:, width:]
    sigmoid = jax.nn.sigmoid(gate)
    passed = gate * sigmoid
    activation = (passed * up).astype(jnp.bfloat16)
    grad_gate = grad_act * up * sigmoid * (1.0 + gate * (1.0 - sigmoid))
    grad_up = grad_act * passed
    both = jnp.concatenate([grad_gate.astype(jnp.bfloat16), grad_up.astype(jnp.bfloat16)], axis=1)
    both_ref[0] = both
    act_ref[0] = activation
    back = back_dot(both, w_ref[:, : 2 * width]).astype(jnp.bfloat16)

    @pl.when(pl.program_id(0) < RING)
    def _():
        own_ref[0] = back

    @pl.when(pl.program_id(0) >= RING)
    def _():
        other_ref[0] = back

    out_ref[0] = back_dot(activation, w_ref[:, 2 * width :]).astype(jnp.bfloat16)


def feed_forward(order, fed, grad_feed, weights):
    blocks, rows, model_width = fed.shape
    width = weights.shape[1] // 3

    def own(i, order_ref):
        return (i, 0, 0)

    def turned(i, order_ref):
        return (order_ref[i], 0, 0)

    def shape(columns, count=blocks):
        return jax.ShapeDtypeStruct((count, rows, columns), jnp.bfloat16)

    return pl.pallas_call(
        feed_kernel,
        grid_spec=pltpu.PrefetchScalarGridSpec(
            num_scalar_prefetch=1,
            grid=(blocks,),
            in_specs=[
                pl.BlockSpec((1, rows, model_width), own),
                pl.BlockSpec((1, rows, model_width), turned),
                pl.BlockSpec(weights.shape, lambda i, order_ref: (0, 0)),
            ],
            out_specs=[
                pl.BlockSpec((1, rows, 2 * width), own),
                pl.BlockSpec((1, rows, width), turned),
                pl.BlockSpec((1, rows, model_width), lambda i, order_ref: (jnp.minimum(i, RING - 1), 0, 0)),
                pl.BlockSpec((1, rows, model_width), lambda i, order_ref: (jnp.maximum(i - RING, 0), 0, 0)),
                pl.BlockSpec((1, rows, model_width), turned),
            ],
        ),
        out_shape=[
            shape(2 * width),
            shape(width),
            shape(model_width, RING),
            shape(model_width, RING),
            shape(model_width),
        ],
        compiler_params=ROOM,
        cost_estimate=pl.CostEstimate(
            flops=2 * blocks * rows * model_width * width * 6,
            bytes_accessed=blocks * rows * (4 * model_width + 3 * width) * 2,
            transcendentals=blocks * rows * width,
        ),
    )(order, fed, grad_feed, weights)


def rms_factor(values):
    return lax.rsqrt(jnp.mean(values * values, axis=-1, keepdims=True) + EPS_NORM)


def norm_back(values, scale_val, gain_row, grad_out):
    weighted = grad_out * gain_row
    inner = jnp.mean(values * weighted, axis=-1, keepdims=True)
    grad_values = scale_val * weighted - values * scale_val * scale_val * scale_val * inner
    grad_gain = jnp.sum(values * scale_val * grad_out, axis=0)
    return (grad_values, grad_gain)


def outer_sum(left_arr, right_arr):
    return lax.dot_general(left_arr, right_arr, TOKEN_DIMS, preferred_element_type=jnp.float32)


def back_dot(left_arr, right_arr):
    return lax.dot_general(left_arr, right_arr, BACK_DIMS, preferred_element_type=jnp.float32)


def exchange(value, axis, groups=None):
    return lax.all_to_all(value, axis, 0, 0, axis_index_groups=groups)


def chip_sum(mine, other):
    return (mine + swap(other.astype(jnp.bfloat16)).astype(jnp.float32)).astype(jnp.bfloat16)


def column_halves(value, parts, core):
    cut = value.reshape(value.shape[0], parts, 2, -1)
    mine = lax.dynamic_index_in_dim(cut, core, 2, keepdims=False)
    other = lax.dynamic_index_in_dim(cut, 1 - core, 2, keepdims=False)
    return mine.reshape(value.shape[0], -1), other.reshape(value.shape[0], -1)


def slot_table(owner_row, per_owner):
    tile_count = owner_row.shape[0]
    same_owner = owner_row[None, :] == owner_row[:, None]
    before = (
        jnp.arange(tile_count, dtype=jnp.int32)[None, :]
        < jnp.arange(tile_count, dtype=jnp.int32)[:, None]
    )
    slot_rank = jnp.sum((same_owner & before).astype(jnp.int32), axis=1)
    return owner_row * per_owner + slot_rank


def rotate_into(left_basis, matrix, right_basis):
    step_one = jnp.einsum("sji,sjk->sik", left_basis, matrix, precision=PRECISE)
    return jnp.einsum("sik,skl->sil", step_one, right_basis, precision=PRECISE)


def rotate_back(left_basis, matrix, right_basis):
    step_one = jnp.einsum("sij,sjk->sik", left_basis, matrix, precision=PRECISE)
    return jnp.einsum("sik,slk->sil", step_one, right_basis, precision=PRECISE)


def orthonormal_kernel(m_ref, q_ref, w_ref):
    count, side = m_ref.shape[0], m_ref.shape[1]
    shape = (PANEL, side)
    rows = lax.broadcasted_iota(jnp.int32, shape, 0)
    lanes = lax.broadcasted_iota(jnp.int32, shape, 1)
    row = lax.broadcasted_iota(jnp.int32, (8, side), 0)
    lane = lax.broadcasted_iota(jnp.int32, (8, side), 1)
    all_rows = lax.broadcasted_iota(jnp.int32, (side, side), 0)
    all_lanes = lax.broadcasted_iota(jnp.int32, (side, side), 1)
    for g in range(count):
        w_ref[g] = lax.dot_general(
            m_ref[g], m_ref[g], TOKEN_DIMS, precision=PRECISE, preferred_element_type=jnp.float32
        )

    def block(b, carry):
        base = pl.multiple_of(b * PANEL, PANEL)
        panels = [
            [w_ref[g, pl.ds(base + 8 * i, 8), :] for i in range(PANEL // 8)] for g in range(count)
        ]
        for k in range(PANEL):
            at, inside = k // 8, k % 8
            hit = lane == k
            for g in range(count):
                panel = panels[g]
                column = jnp.broadcast_to(panel[at][:, k : k + 1], (8, side))
                scale = lax.rsqrt(jnp.broadcast_to(column[inside : inside + 1], (8, side)))
                top = jnp.broadcast_to(panel[at][inside : inside + 1], (8, side))
                top = jnp.where(hit, scale, top * scale)
                part = jnp.where(hit, 0.0, panel[at]) - column * scale * top
                panel[at] = jnp.where(row > inside, part, jnp.where(row == inside, top, panel[at]))
                for i in range(at + 1, PANEL // 8):
                    column = jnp.broadcast_to(panel[i][:, k : k + 1], (8, side))
                    panel[i] = jnp.where(hit, 0.0, panel[i]) - column * scale * top
        below = all_rows >= base + PANEL
        for g in range(count):
            done = jnp.concatenate(panels[g], axis=0)
            coef = jnp.where((lanes >= PANEL) & (lanes < side - base), done, 0.0)
            source = jnp.where((lanes < PANEL) & (lanes > rows), 0.0, done)
            change = lax.dot_general(
                coef, source, TOKEN_DIMS, precision=PRECISE, preferred_element_type=jnp.float32
            )
            change = pltpu.roll(change, base, 0)
            kept = jnp.where(below & (all_lanes < PANEL), 0.0, w_ref[g])
            w_ref[g] = kept - jnp.where(below, change, 0.0)
            w_ref[g, pl.ds(base, PANEL), :] = done
            w_ref[g] = pltpu.roll(w_ref[g], side - PANEL, 1)
        return carry

    lax.fori_loop(0, side // PANEL, block, 0)
    for g in range(count):
        inverse = jnp.where(all_lanes <= all_rows, w_ref[g], 0.0)
        q_ref[g] = lax.dot_general(
            m_ref[g], inverse, BACK_DIMS, precision=PRECISE, preferred_element_type=jnp.float32
        )


def orthonormal(matrix):
    return pl.pallas_call(
        orthonormal_kernel,
        out_shape=jax.ShapeDtypeStruct(matrix.shape, jnp.float32),
        in_specs=[pl.BlockSpec(memory_space=pltpu.VMEM)],
        out_specs=pl.BlockSpec(memory_space=pltpu.VMEM),
        scratch_shapes=[pltpu.VMEM(matrix.shape, jnp.float32)],
        compiler_params=ROOM,
        cost_estimate=pl.CostEstimate(
            flops=30 * 10**9, bytes_accessed=2 * matrix.size * 4, transcendentals=0
        ),
    )(matrix)


def soap_update(grad_tiles, master, first, second, stats, bases):
    left_basis = bases[:, 0]
    right_basis = bases[:, 1]
    rotated = rotate_into(left_basis, grad_tiles, right_basis)
    first_new = BETA_ONE * first + (1.0 - BETA_ONE) * grad_tiles
    second_new = BETA_TWO * second + (1.0 - BETA_TWO) * rotated * rotated
    moment_rot = rotate_into(left_basis, first_new, right_basis)
    direction = (
        moment_rot
        / (1.0 - BETA_ONE**STEP)
        / (jnp.sqrt(second_new / (1.0 - BETA_TWO**STEP)) + EPS_ADAM)
    )
    master_new = master - RATE_MATRIX * (
        rotate_back(left_basis, direction, right_basis) + DECAY_WEIGHT * master
    )
    stat_left = BETA_STAT * stats[:, 0] + (1.0 - BETA_STAT) * jnp.einsum(
        "sik,sjk->sij", grad_tiles, grad_tiles, precision=PRECISE
    )
    stat_right = BETA_STAT * stats[:, 1] + (1.0 - BETA_STAT) * jnp.einsum(
        "ski,skj->sij", grad_tiles, grad_tiles, precision=PRECISE
    )
    stats_new = jnp.stack([stat_left, stat_right], axis=1)
    turned = jnp.einsum("stij,stjk->stik", stats_new, bases, precision=PRECISE)
    bases_new = orthonormal(turned.reshape((-1,) + turned.shape[2:])).reshape(bases.shape)
    return (master_new, first_new, second_new, stats_new, bases_new)


def shards(
    block_in,
    cotangent,
    lengths,
    vector_params,
    vector_first,
    vector_second,
    w_in,
    w_out,
    w_gate,
    w_up,
    w_down,
    tile_owner,
    tile_master,
    tile_first,
    tile_second,
    tile_stats,
    tile_bases,
):
    micro_count, _, tok_count, model_width = block_in.shape
    hidden_width = w_gate.shape[1]
    shard_rows = w_in.shape[0]
    half_rows = shard_rows // 2
    parts = lax.axis_size("fsdp")
    owners = lax.axis_size("dp")
    chips = owners // 2
    owner_id = lax.axis_index("dp")
    core = owner_id % 2
    place, far = place_of("dp")
    chip_group = [list(range(i, i + 2 * RING)) for i in range(0, owners, 2 * RING)]
    same_core = [[2 * i + c for i in range(chips)] for c in range(2)]
    tile_side = tile_master.shape[-1]
    per_owner = tile_master.shape[1]
    tile_count = tile_owner.shape[1]
    g_one, g_two, k_zero, k_one, k_two = [vector_params[i] for i in range(5)]

    def half_of(matrix):
        return lax.dynamic_slice(matrix, (core * half_rows, 0), (half_rows, matrix.shape[1]))

    conv_block = jnp.concatenate([half_of(w_in), half_of(w_out)], axis=1)
    conv_pieces = spread(conv_block, "fsdp")
    whole_in, whole_out = assemble(conv_pieces, (3 * model_width, model_width))
    positions = lax.axis_index("fsdp") * tok_count + jnp.arange(tok_count, dtype=jnp.int32)
    live_mask = (positions[None, :] < lengths).astype(jnp.float32)[:, :, None]
    seed_grad = (cotangent[:, 0] * live_mask).reshape(-1, model_width)
    grad_feed = lax.all_gather(
        seed_grad.astype(jnp.bfloat16), "dp", axis_index_groups=chip_group, axis=0
    )
    hidden = hidden_width // RING // 2
    wide = -(-hidden // tile_side) * tile_side
    shift = 2 * hidden - wide
    columns = jnp.arange(wide, dtype=jnp.int32)
    kept = (columns >= core * (wide - hidden)) & (columns < hidden + core * (wide - hidden))

    def slice_of(matrix):
        first = place * (2 * hidden) + core * shift
        return jnp.where(
            kept[None, :], lax.dynamic_slice(matrix, (0, first), (shard_rows, wide)), jnp.zeros((), matrix.dtype)
        )

    feed_block = jnp.concatenate([slice_of(matrix) for matrix in (w_gate, w_up, w_down)], axis=1)
    feed_weights = lax.all_gather(
        after(feed_block, *[array for array, _ in conv_pieces[4:7]]), "fsdp", axis=0, tiled=True
    )

    token_rows = block_in.astype(jnp.float32).reshape(-1, model_width)
    scale_one = rms_factor(token_rows)
    normed = (token_rows * scale_one * g_one).astype(jnp.bfloat16)
    mixed_all = jnp.dot(normed, whole_in, preferred_element_type=jnp.float32)
    part_b = mixed_all[:, :model_width]
    part_c = mixed_all[:, model_width : 2 * model_width]
    part_x = mixed_all[:, 2 * model_width :]
    product = (part_b * part_x).reshape(micro_count, tok_count, model_width)
    extended = jnp.concatenate([from_behind(product[:, -2:], "fsdp", 1), product], axis=1)
    convolved = (
        k_zero * extended[:, :-2] + k_one * extended[:, 1:-1] + k_two * extended[:, 2:]
    ).reshape(-1, model_width)
    gated_conv = (part_c * convolved).astype(jnp.bfloat16)
    residual = token_rows + jnp.dot(gated_conv, whole_out, preferred_element_type=jnp.float32)
    scale_two = rms_factor(residual)
    normed_two = (residual * scale_two * g_two).astype(jnp.bfloat16)

    fed = spread_ring(normed_two, "dp")
    fed = jnp.concatenate([fed, swap(fed)]).reshape(2 * RING, -1, model_width)
    steps = jnp.array([0, RING - 1, 1, 2], dtype=jnp.int32)
    ring_places = (place + steps) % RING * 2
    order = jnp.concatenate([ring_places + core, ring_places + 1 - core]).astype(jnp.int32)
    grad_both, activation, back_own, back_other, out_parts = feed_forward(
        order, fed, grad_feed, feed_weights
    )
    back_other = swap(back_other)
    grad_both, activation = lax.optimization_barrier((grad_both, activation, back_other))[:2]
    back_parts = back_own.astype(jnp.float32) + back_other.astype(jnp.float32)
    grad_normed_two = collect_ring(back_parts.reshape(-1, model_width), "dp")
    low = jnp.bfloat16
    feed_sums = jnp.concatenate(
        [
            outer_sum(fed.reshape(-1, model_width), grad_both.reshape(-1, 2 * wide)).astype(low),
            outer_sum(grad_feed.reshape(-1, model_width), activation.reshape(-1, wide)).astype(low),
        ],
        axis=1,
    )
    feed_rows = lax.psum_scatter(feed_sums, "fsdp", scatter_dimension=0, tiled=True)

    normed_mine, normed_other = column_halves(normed, parts, core)
    gated_mine, gated_other = column_halves(gated_conv, parts, core)
    grad_res_norm, grad_gain_two = norm_back(residual, scale_two, g_two, grad_normed_two)
    grad_resid = seed_grad + grad_res_norm
    grad_branch = grad_resid.astype(jnp.bfloat16)
    grad_gated = back_dot(grad_branch, whole_out)
    grad_part_c = grad_gated * convolved
    grad_conv = (grad_gated * part_c).reshape(micro_count, tok_count, model_width)
    grad_ext = jnp.concatenate([grad_conv, from_behind(grad_conv[:, :2], "fsdp", -1)], axis=1)
    grad_product = (
        k_two * grad_conv + k_one * grad_ext[:, 1 : tok_count + 1] + k_zero * grad_ext[:, 2:]
    ).reshape(-1, model_width)
    grad_kernel = jnp.stack(
        [
            jnp.sum(grad_conv * extended[:, :-2], axis=(0, 1)),
            jnp.sum(grad_conv * extended[:, 1:-1], axis=(0, 1)),
            jnp.sum(grad_conv * extended[:, 2:], axis=(0, 1)),
        ]
    )
    grad_mixed = jnp.concatenate(
        [
            (grad_product * part_x).astype(jnp.bfloat16),
            grad_part_c.astype(jnp.bfloat16),
            (grad_product * part_b).astype(jnp.bfloat16),
        ],
        axis=1,
    )
    conv_sums = jnp.concatenate(
        [
            chip_sum(outer_sum(normed_mine, grad_mixed), outer_sum(normed_other, grad_mixed)),
            chip_sum(outer_sum(gated_mine, grad_branch), outer_sum(gated_other, grad_branch)),
        ],
        axis=1,
    ).reshape(parts, half_rows, -1)
    conv_rows = exchange(conv_sums, "fsdp")

    feed_rows = after(feed_rows, conv_sums)
    feed_own = feed_rows.astype(jnp.float32) + pair(feed_rows, "dp").astype(jnp.float32)
    feed_tiles = lax.all_gather(feed_own.astype(low), "dp", axis_index_groups=chip_group, axis=0)
    feed_out = lax.psum_scatter(
        after(out_parts, feed_own), "dp", scatter_dimension=0, axis_index_groups=chip_group
    )
    grad_normed = back_dot(grad_mixed, whole_in)
    grad_rows_norm, grad_gain_one = norm_back(token_rows, scale_one, g_one, grad_normed)
    grad_rows = grad_resid + grad_rows_norm
    vector_grads = sum_over(
        jnp.concatenate([grad_gain_one[None], grad_gain_two[None], grad_kernel], axis=0), "dp"
    )
    conv_rows, grad_rows, vector_grads = lax.optimization_barrier((conv_rows, grad_rows, vector_grads))
    vector_grads = sum_over(vector_grads, "fsdp")
    conv_rows = jnp.sum(conv_rows.astype(jnp.float32), axis=0).astype(low)
    conv_cut = conv_rows.reshape(half_rows, chips, -1).transpose(1, 0, 2)
    conv_own = jnp.sum(exchange(conv_cut, "dp", same_core).astype(jnp.float32), axis=0).astype(low)
    conv_tiles = exchange(jnp.broadcast_to(conv_own, (chips,) + conv_own.shape), "dp", same_core)
    conv_tiles, vector_grads = lax.optimization_barrier((conv_tiles, vector_grads))
    result_rows = residual + after(feed_out, conv_tiles).astype(jnp.float32)

    vec_first = BETA_ONE * vector_first + (1.0 - BETA_ONE) * vector_grads
    vec_second = BETA_TWO * vector_second + (1.0 - BETA_TWO) * vector_grads * vector_grads
    vec_new = vector_params - RATE_VECTOR * (vec_first / (1.0 - BETA_ONE**STEP)) / (
        jnp.sqrt(vec_second / (1.0 - BETA_TWO**STEP)) + EPS_ADAM
    )

    slot_index = slot_table(tile_owner[0], per_owner)
    slot_match = slot_index[None, :] == jnp.arange(per_owner * owners, dtype=jnp.int32)[:, None]
    tile_of_slot = (
        jnp.sum(
            jnp.where(slot_match, jnp.arange(1, tile_count + 1, dtype=jnp.int32)[None, :], 0), axis=1
        )
        - 1
    )
    wanted = jnp.concatenate(
        [
            lax.dynamic_slice(tile_of_slot, (owner_id * per_owner,), (per_owner,)),
            lax.dynamic_slice(tile_of_slot, ((owner_id ^ 1) * per_owner,), (per_owner,)),
        ]
    )
    conv_count = 4 * model_width // tile_side
    each_conv, each_feed = conv_count // chips, 2 * hidden // tile_side
    feed_tile = wanted - conv_count
    within = feed_tile % each_feed
    feed_first = feed_tile // (each_feed * RING) * (wide // tile_side)
    is_conv = wanted < conv_count
    own_slot = jnp.arange(2 * per_owner) < per_owner
    left, right = within < wide // tile_side, within >= shift // tile_side
    table = jnp.stack(
        [
            jnp.where(is_conv, 1, jnp.where(own_slot, 2, 0)),
            jnp.where(is_conv, wanted // each_conv, feed_tile // each_feed % RING * 2),
            jnp.where(is_conv, wanted % each_conv, jnp.where(left, feed_first + within, -1)),
            jnp.where(right, feed_first + within - shift // tile_side, -1),
            jnp.where(is_conv, core, 0),
        ],
        axis=1,
    )
    table = jnp.where(wanted[:, None] < 0, 0, table).astype(jnp.int32).reshape(-1)
    mine, other = pick(table, conv_tiles, feed_tiles, per_owner, tile_side)
    owned_grads = mine + swap(other).astype(jnp.float32)
    master_new, first_new, second_new, stats_new, bases_new = soap_update(
        owned_grads, tile_master[0], tile_first[0], tile_second[0], tile_stats[0], tile_bases[0]
    )
    master_low = master_new.astype(low)
    masters = exchange(jnp.broadcast_to(master_low, (chips,) + master_low.shape), "dp", same_core)
    masters, bases_new = lax.optimization_barrier((masters, bases_new))
    w_in_new, w_out_new, w_gate_new, w_up_new, w_down_new = put(
        core,
        slot_index,
        masters,
        swap(masters),
        (3 * model_width, model_width, hidden_width, hidden_width, hidden_width),
    )
    whole_shape = (micro_count, 1, tok_count, model_width)
    return (
        result_rows.reshape(whole_shape),
        grad_rows.reshape(whole_shape),
        vec_new,
        vec_first,
        vec_second,
        w_in_new,
        w_out_new,
        w_gate_new,
        w_up_new,
        w_down_new,
        master_new[None],
        first_new[None],
        second_new[None],
        stats_new[None],
        bases_new[None],
    )


def solution(mesh):
    return jax.shard_map(
        shards,
        mesh=mesh,
        in_specs=(
            P(None, "dp", "fsdp", None),
            P(None, "dp", "fsdp", None),
            P(None, "dp"),
            P(),
            P(),
            P(),
            P("fsdp", None),
            P("fsdp", None),
            P("fsdp", None),
            P("fsdp", None),
            P("fsdp", None),
            P("fsdp", None),
            P("fsdp", "dp", None, None),
            P("fsdp", "dp", None, None),
            P("fsdp", "dp", None, None),
            P("fsdp", "dp", None, None, None),
            P("fsdp", "dp", None, None, None),
        ),
        out_specs=(
            P(None, "dp", "fsdp", None),
            P(None, "dp", "fsdp", None),
            P(),
            P(),
            P(),
            P("fsdp", None),
            P("fsdp", None),
            P("fsdp", None),
            P("fsdp", None),
            P("fsdp", None),
            P("fsdp", "dp", None, None),
            P("fsdp", "dp", None, None),
            P("fsdp", "dp", None, None),
            P("fsdp", "dp", None, None, None),
            P("fsdp", "dp", None, None, None),
        ),
        check_vma=False,
    )
```

```python
import functools

import jax
import jax.numpy as jnp
from jax import lax
from jax.experimental import pallas as pl
from jax.experimental.pallas import tpu as pltpu
from jax.sharding import PartitionSpec as P

STEP = 10


EPS_NORM = 1e-05
EPS_ADAM = 1e-08
BETA_ONE = 0.5
BETA_TWO = 0.5
BETA_STAT = 0.5
RATE_MATRIX = 0.03
RATE_VECTOR = 0.2
DECAY_WEIGHT = 0.01
PRECISE = lax.Precision.HIGHEST
BACK_DIMS = (((1,), (1,)), ((), ()))
TOKEN_DIMS = (((0,), (0,)), ((), ()))

PANEL = 16


def from_behind(value, axis, by):
    length = lax.axis_size(axis)
    pairs = [(i, i + by) for i in range(length) if 0 <= i + by < length]
    return lax.ppermute(value, axis, pairs)


def flip(value, axis, bit):
    length = lax.axis_size(axis)
    return lax.ppermute(value, axis, [(i, i ^ bit) for i in range(length)])


RING = 4


def ring(value, axis, by):
    length = lax.axis_size(axis)
    low = 2 if axis == "dp" else 1
    pairs = []
    for i in range(length):
        place = i // low % RING
        pairs.append((i, i + ((place + by) % RING - place) * low))
    return lax.ppermute(value, axis, pairs)


def pair(value, axis):
    return flip(value, axis, lax.axis_size(axis) // 2)


def swap(value):
    return flip(value, "dp", 1)


def place_of(axis):
    index = lax.axis_index(axis)
    low = 2 if axis == "dp" else 1
    return index // low % RING, index // (low * RING)


def spread(block, axis):
    half = block.shape[0] // 2
    before, after, side = ring(block, axis, 1), ring(block, axis, -1), pair(block, axis)
    fore = ring(jnp.concatenate([before[:half], side[:half]]), axis, 1)
    back = ring(jnp.concatenate([after[half:], side[half:]]), axis, -1)
    cross = pair(jnp.concatenate([before[half:], after[:half]]), axis)
    far_one = ring(fore[half:], axis, 1)
    far_two = ring(back[half:], axis, -1)
    return [
        (block, [(0, 2 * half, 0, 0, None)]),
        (before, [(0, 2 * half, -1, 0, None)]),
        (after, [(0, 2 * half, 1, 0, None)]),
        (side, [(0, 2 * half, 0, 1, None)]),
        (fore, [(0, half, 2, 0, 0), (half, half, -1, 1, 0)]),
        (back, [(0, half, 2, 0, 1), (half, half, 1, 1, 1)]),
        (cross, [(0, half, -1, 1, 1), (half, half, 1, 1, 0)]),
        (far_one, [(0, half, 2, 1, 0)]),
        (far_two, [(0, half, 2, 1, 1)]),
    ]


def spread_ring(block, axis):
    half = block.shape[0] // 2
    before, after = ring(block, axis, 1), ring(block, axis, -1)
    return jnp.concatenate(
        [block, before, after, ring(before[:half], axis, 1), ring(after[half:], axis, -1)]
    )


def collect_ring(mine, other, axis):
    half = mine.shape[1] // 2
    low, wide = jnp.bfloat16, jnp.float32
    far = mine[3].astype(wide) + swap(other[3]).astype(wide)
    rest = swap(other[:3])
    one = ring(far[:half].astype(low), axis, -1)
    two = ring(far[half:].astype(low), axis, 1)
    behind = mine[1].astype(wide) + rest[1].astype(wide)
    ahead = mine[2].astype(wide) + rest[2].astype(wide)
    behind = jnp.concatenate([behind[:half] + one.astype(wide), behind[half:]])
    ahead = jnp.concatenate([ahead[:half], ahead[half:] + two.astype(wide)])
    from_ahead = ring(behind.astype(low), axis, -1)
    from_back = ring(ahead.astype(low), axis, 1)
    total = mine[0].astype(wide) + rest[0].astype(wide) + from_ahead.astype(wide) + from_back.astype(wide)
    return total, (one, two)


def after(value, *others):
    return lax.optimization_barrier((value,) + others)[0]


def packed(rows, width):
    high = rows.astype(jnp.bfloat16)
    rest = (rows - high.astype(jnp.float32)).astype(jnp.bfloat16)
    cut = jnp.concatenate([high, rest]).reshape(-1, width)
    return jnp.pad(cut, ((0, -cut.shape[0] % 32), (0, 0)))


def unpacked(cut, count):
    width = cut.shape[1]
    pairs = cut[: 2 * count * (1024 // width)].reshape(2 * count, -1)
    return pairs[:count] + pairs[count:]


ANYWHERE = pl.BlockSpec(memory_space=pl.ANY)
SCALARS = pl.BlockSpec(memory_space=pltpu.SMEM)
INSIDE = pl.BlockSpec(memory_space=pltpu.VMEM)
ROOM = pltpu.CompilerParams(vmem_limit_bytes=56 * 2**20)


def assemble_kernel(spans, widths, offsets_ref, *refs):
    count = len(spans)
    pieces, outs, sems = refs[: -len(widths) - 1], refs[-len(widths) - 1 : -1], refs[-1]
    for i, (which, first, rows) in enumerate(spans):
        offset = pl.multiple_of(offsets_ref[i], rows)
        column = 0
        for j, width in enumerate(widths):
            pltpu.make_async_copy(
                pieces[which].at[pl.ds(first, rows), pl.ds(column, width)],
                outs[j].at[pl.ds(offset, rows), :],
                sems.at[j],
            ).start()
            column += width
    for j in range(len(widths)):
        pltpu.make_async_copy(outs[j], outs[j], sems.at[j]).wait()


def assemble(pieces, widths):
    core = lax.axis_index("dp") % 2
    place, side = place_of("fsdp")
    arrays, spans, offsets = [], [], []
    for who in range(2):
        for array, cuts in pieces:
            arrays.append(array if who == 0 else swap(array))
            for first, count, step, across, half in cuts:
                owner = (side ^ across) * RING + (place + step) % RING
                block = array.shape[0] // len(cuts) * (1 if half is None else 2)
                spans.append((len(arrays) - 1, first, count))
                offsets.append((owner * 2 + (core ^ who)) * block + (half or 0) * count)
    rows = 2 * block * 2 * RING
    return pl.pallas_call(
        functools.partial(assemble_kernel, spans, widths),
        out_shape=[jax.ShapeDtypeStruct((rows, width), pieces[0][0].dtype) for width in widths],
        in_specs=[SCALARS] + [ANYWHERE] * len(arrays),
        out_specs=[INSIDE] * len(widths),
        compiler_params=ROOM,
        scratch_shapes=[pltpu.SemaphoreType.DMA((len(widths),))],
    )(jnp.stack(offsets).astype(jnp.int32), *arrays)


def pick_kernel(table_ref, conv_ref, feed_ref, mine_ref, other_ref, held, sem):
    slots, side = mine_ref.shape[0], mine_ref.shape[1]
    half = side // 2
    held[...] = jnp.zeros_like(held)

    def one(i, finish):
        at = 5 * i
        kind, piece = table_ref[at], table_ref[at + 1]
        first = pl.multiple_of(table_ref[at + 4] * half, half)

        def move(source, target):
            copy = pltpu.make_async_copy(source, target, sem)
            if finish:
                copy.wait()
            else:
                copy.start()

        def column(k):
            return pl.ds(pl.multiple_of(k * side, side), side)

        @pl.when(kind == 1)
        def _():
            move(
                conv_ref.at[piece, pl.ds(0, half), column(table_ref[at + 2])], held.at[0, i, pl.ds(first, half), :]
            )

        for which in range(2):

            @pl.when((kind == 2) & (table_ref[at + 2 + which] >= 0))
            def _():
                move(feed_ref.at[piece + which, :, column(table_ref[at + 2 + which])], held.at[which, i])

    for finish in (False, True):

        def step(i, carry):
            one(i, finish)
            return carry

        lax.fori_loop(0, 2 * slots, step, 0)
    for q in range(slots):
        mine_ref[q] = held[0, q].astype(jnp.float32) + held[1, q].astype(jnp.float32)
        other_ref[q] = held[0, slots + q]


def pick(table, conv, feed, slots, side):
    shape = (slots, side, side)
    return pl.pallas_call(
        pick_kernel,
        out_shape=[jax.ShapeDtypeStruct(shape, jnp.float32), jax.ShapeDtypeStruct(shape, conv.dtype)],
        in_specs=[SCALARS, ANYWHERE, ANYWHERE],
        out_specs=[INSIDE, INSIDE],
        compiler_params=ROOM,
        scratch_shapes=[
            pltpu.VMEM((2, 2 * slots, side, side), conv.dtype),
            pltpu.SemaphoreType.DMA,
        ],
    )(table, conv, feed)


def add_kernel(terms_ref, extra_ref, out_ref):
    width = out_ref.shape[2]
    parts = terms_ref.shape[2] // width
    rows = out_ref.shape[1] - extra_ref.shape[0]
    blocks = out_ref.shape[0] // parts
    for i in range(blocks):
        total = terms_ref[0, i * rows : (i + 1) * rows, :].astype(jnp.float32)
        for j in range(1, terms_ref.shape[0]):
            total = total + terms_ref[j, i * rows : (i + 1) * rows, :].astype(jnp.float32)
        total = total.astype(out_ref.dtype)
        for k in range(parts):
            out_ref[k * blocks + i, :rows, :] = total[:, k * width : (k + 1) * width]
            out_ref[k * blocks + i, rows:, :] = extra_ref[...]


def add_terms(terms, extra, blocks, parts):
    rows, width = terms.shape[1] // blocks, terms.shape[2] // parts
    return pl.pallas_call(
        add_kernel,
        out_shape=jax.ShapeDtypeStruct((parts * blocks, rows + extra.shape[0], width), terms.dtype),
        in_specs=[INSIDE, INSIDE],
        out_specs=INSIDE,
        compiler_params=ROOM,
        cost_estimate=pl.CostEstimate(
            flops=50 * 10**9, bytes_accessed=terms.size * 2, transcendentals=0
        ),
    )(terms, extra)


def put_kernel(core_ref, slot_ref, mine_ref, other_ref, *refs):
    count = (len(refs) - 3) // 2
    outs, pages = refs[:count], refs[count : 2 * count]
    held, in_sems, out_sems = refs[-3:]
    chips, slots, side = mine_ref.shape[0], mine_ref.shape[1], mine_ref.shape[2]
    loads = [
        pltpu.make_async_copy(source, held.at[i], in_sems.at[i])
        for i, source in enumerate((mine_ref, other_ref))
    ]
    for load in loads:
        load.start()
    for load in loads:
        load.wait()
    tile = 0
    for j in range(count):
        for k in range(outs[j].shape[1] // side):
            slot = slot_ref[tile]
            owner = slot // slots
            pages[j][:, k * side : (k + 1) * side] = held[owner % 2 ^ core_ref[0], owner // 2, slot % slots]
            tile += 1
        pltpu.make_async_copy(pages[j], outs[j], out_sems.at[j]).start()
    for j in range(count):
        pltpu.make_async_copy(pages[j], outs[j], out_sems.at[j]).wait()


def put(core, slot_index, mine, other, widths):
    side = mine.shape[-1]
    return pl.pallas_call(
        put_kernel,
        out_shape=[jax.ShapeDtypeStruct((side, width), mine.dtype) for width in widths],
        in_specs=[SCALARS, SCALARS, ANYWHERE, ANYWHERE],
        out_specs=[ANYWHERE] * len(widths),
        compiler_params=ROOM,
        scratch_shapes=[pltpu.VMEM((side, width), mine.dtype) for width in widths]
        + [
            pltpu.VMEM((2,) + mine.shape, mine.dtype),
            pltpu.SemaphoreType.DMA((2,)),
            pltpu.SemaphoreType.DMA((len(widths),)),
        ],
    )(core.astype(jnp.int32).reshape(1), slot_index, mine, other)


def feed_kernel(order_ref, fed_ref, dy_ref, w_ref, *refs):
    both_ref, act_ref, out_ref, back_ref = refs[-4:]
    width = act_ref.shape[-1]
    mixed = jnp.dot(fed_ref[0], w_ref[:, : 2 * width], preferred_element_type=jnp.float32)
    grad_act = jnp.dot(dy_ref[0], w_ref[:, 2 * width :], preferred_element_type=jnp.float32)
    gate, up = mixed[:, :width], mixed[:, width:]
    sigmoid = jax.nn.sigmoid(gate)
    passed = gate * sigmoid
    activation = (passed * up).astype(jnp.bfloat16)
    grad_gate = grad_act * up * sigmoid * (1.0 + gate * (1.0 - sigmoid))
    grad_up = grad_act * passed
    both = jnp.concatenate([grad_gate.astype(jnp.bfloat16), grad_up.astype(jnp.bfloat16)], axis=1)
    both_ref[0] = both
    act_ref[0] = activation
    back_ref[0] = back_dot(both, w_ref[:, : 2 * width]).astype(jnp.bfloat16)
    out_ref[0] = back_dot(activation, w_ref[:, 2 * width :]).astype(jnp.bfloat16)


def feed_forward(order, fed, grad_feed, weights, first, begun):
    blocks, rows, model_width = fed.shape
    width = weights.shape[1] // 3
    begun = list(begun)

    def turned(i, order_ref):
        return (order_ref[first + i], 0, 0)

    def shape(count, columns):
        return jax.ShapeDtypeStruct((count, rows, columns), jnp.bfloat16)

    whole = grad_feed.shape[0]

    return pl.pallas_call(
        feed_kernel,
        grid_spec=pltpu.PrefetchScalarGridSpec(
            num_scalar_prefetch=1,
            grid=(blocks,),
            in_specs=[
                pl.BlockSpec((1, rows, model_width), lambda i, order_ref: (i, 0, 0)),
                pl.BlockSpec((1, rows, model_width), turned),
                pl.BlockSpec(weights.shape, lambda i, order_ref: (0, 0)),
            ]
            + [ANYWHERE] * len(begun),
            out_specs=[
                pl.BlockSpec((1, rows, 2 * width), lambda i, order_ref: (first + i, 0, 0)),
                pl.BlockSpec((1, rows, width), turned),
                pl.BlockSpec((1, rows, model_width), turned),
                pl.BlockSpec((1, rows, model_width), lambda i, order_ref: (i, 0, 0)),
            ],
        ),
        out_shape=[
            shape(whole, 2 * width),
            shape(whole, width),
            shape(whole, model_width),
            shape(blocks, model_width),
        ],
        input_output_aliases={4 + i: i for i in range(len(begun))},
        compiler_params=ROOM,
        cost_estimate=pl.CostEstimate(
            flops=2 * blocks * rows * model_width * width * 6,
            bytes_accessed=blocks * rows * (4 * model_width + 3 * width) * 2,
            transcendentals=blocks * rows * width,
        ),
    )(order, fed, grad_feed, weights, *begun)


def rms_factor(values):
    return lax.rsqrt(jnp.mean(values * values, axis=-1, keepdims=True) + EPS_NORM)


def norm_back(values, scale_val, gain_row, grad_out):
    weighted = grad_out * gain_row
    inner = jnp.mean(values * weighted, axis=-1, keepdims=True)
    grad_values = scale_val * weighted - values * scale_val * scale_val * scale_val * inner
    grad_gain = jnp.sum(values * scale_val * grad_out, axis=0)
    return (grad_values, grad_gain)


def outer_sum(left_arr, right_arr):
    return lax.dot_general(left_arr, right_arr, TOKEN_DIMS, preferred_element_type=jnp.float32)


def back_dot(left_arr, right_arr):
    return lax.dot_general(left_arr, right_arr, BACK_DIMS, preferred_element_type=jnp.float32)


def exchange(value, axis, groups=None):
    return lax.all_to_all(value, axis, 0, 0, axis_index_groups=groups)


def chip_sum(mine, other):
    return (mine + swap(other.astype(jnp.bfloat16)).astype(jnp.float32)).astype(jnp.bfloat16)


def column_halves(value, parts, core):
    cut = value.reshape(value.shape[0], parts, 2, -1)
    mine = lax.dynamic_index_in_dim(cut, core, 2, keepdims=False)
    other = lax.dynamic_index_in_dim(cut, 1 - core, 2, keepdims=False)
    return mine.reshape(value.shape[0], -1), other.reshape(value.shape[0], -1)


def slot_table(owner_row, per_owner):
    tile_count = owner_row.shape[0]
    same_owner = owner_row[None, :] == owner_row[:, None]
    before = (
        jnp.arange(tile_count, dtype=jnp.int32)[None, :]
        < jnp.arange(tile_count, dtype=jnp.int32)[:, None]
    )
    slot_rank = jnp.sum((same_owner & before).astype(jnp.int32), axis=1)
    return owner_row * per_owner + slot_rank


def rotate_into(left_basis, matrix, right_basis):
    step_one = jnp.einsum("sji,sjk->sik", left_basis, matrix, precision=PRECISE)
    return jnp.einsum("sik,skl->sil", step_one, right_basis, precision=PRECISE)


def rotate_back(left_basis, matrix, right_basis):
    step_one = jnp.einsum("sij,sjk->sik", left_basis, matrix, precision=PRECISE)
    return jnp.einsum("sik,slk->sil", step_one, right_basis, precision=PRECISE)


def split_dot(left, right, dims, axis):
    def cut(value):
        high = value.astype(jnp.bfloat16)
        rest = value - high.astype(jnp.float32)
        middle = rest.astype(jnp.bfloat16)
        return high, middle, (rest - middle.astype(jnp.float32)).astype(jnp.bfloat16)

    left_cut, right_cut = cut(left), cut(right)
    pairs = ((0, 0), (0, 1), (1, 0), (1, 1), (0, 2), (2, 0))
    return lax.dot_general(
        jnp.concatenate([left_cut[i] for i, _ in pairs], axis),
        jnp.concatenate([right_cut[j] for _, j in pairs], axis),
        dims,
        preferred_element_type=jnp.float32,
    )


def orthonormal_kernel(m_ref, q_ref, w_ref):
    count, side = m_ref.shape[0], m_ref.shape[1]
    row = lax.broadcasted_iota(jnp.int32, (8, side), 0)
    lane = lax.broadcasted_iota(jnp.int32, (8, side), 1)
    rows = lax.broadcasted_iota(jnp.int32, (PANEL, side), 0)
    lanes = lax.broadcasted_iota(jnp.int32, (PANEL, side), 1)
    all_rows = lax.broadcasted_iota(jnp.int32, (side, side), 0)
    all_lanes = lax.broadcasted_iota(jnp.int32, (side, side), 1)
    for g in range(count):
        w_ref[g] = split_dot(m_ref[g], m_ref[g], TOKEN_DIMS, 0)
    for base in range(0, side, PANEL):
        end = base + PANEL
        panels = [[w_ref[g, i : i + 8, :] for i in range(base, end, 8)] for g in range(count)]
        for k in range(PANEL):
            at, inside = k // 8, k % 8
            hit = lane == base + k
            for g in range(count):
                panel = panels[g]
                column = jnp.broadcast_to(panel[at][:, base + k : base + k + 1], (8, side))
                scale = lax.rsqrt(jnp.broadcast_to(column[inside : inside + 1], (8, side)))
                top = jnp.broadcast_to(panel[at][inside : inside + 1], (8, side))
                top = jnp.where(hit, scale, top * scale)
                part = jnp.where(hit, 0.0, panel[at]) - column * scale * top
                panel[at] = jnp.where(row > inside, part, jnp.where(row == inside, top, panel[at]))
                for i in range(at + 1, PANEL // 8):
                    column = jnp.broadcast_to(panel[i][:, base + k : base + k + 1], (8, side))
                    panel[i] = jnp.where(hit, 0.0, panel[i]) - column * scale * top
        for g in range(count):
            done = jnp.concatenate(panels[g], axis=0)
            w_ref[g, base:end, :] = done
            if end < side:
                upper = (lanes >= base) & (lanes < end) & (lanes - base > rows)
                change = split_dot(done, jnp.where(upper, 0.0, done), TOKEN_DIMS, 0)[end:]
                gone = (all_lanes[end:] >= base) & (all_lanes[end:] < end)
                w_ref[g, end:, :] = jnp.where(gone, 0.0, w_ref[g, end:, :]) - change
    for g in range(count):
        inverse = jnp.where(all_lanes <= all_rows, w_ref[g], 0.0)
        q_ref[g] = split_dot(m_ref[g], inverse, BACK_DIMS, 1)


def orthonormal(matrix):
    return pl.pallas_call(
        orthonormal_kernel,
        out_shape=jax.ShapeDtypeStruct(matrix.shape, jnp.float32),
        in_specs=[pl.BlockSpec(memory_space=pltpu.VMEM)],
        out_specs=pl.BlockSpec(memory_space=pltpu.VMEM),
        scratch_shapes=[pltpu.VMEM(matrix.shape, jnp.float32)],
        compiler_params=ROOM,
        cost_estimate=pl.CostEstimate(
            flops=30 * 10**9, bytes_accessed=2 * matrix.size * 4, transcendentals=0
        ),
    )(matrix)


def soap_update(grad_tiles, master, first, second, stats, bases):
    left_basis = bases[:, 0]
    right_basis = bases[:, 1]
    rotated = rotate_into(left_basis, grad_tiles, right_basis)
    first_new = BETA_ONE * first + (1.0 - BETA_ONE) * grad_tiles
    second_new = BETA_TWO * second + (1.0 - BETA_TWO) * rotated * rotated
    moment_rot = rotate_into(left_basis, first_new, right_basis)
    direction = (
        moment_rot
        / (1.0 - BETA_ONE**STEP)
        / (jnp.sqrt(second_new / (1.0 - BETA_TWO**STEP)) + EPS_ADAM)
    )
    master_new = master - RATE_MATRIX * (
        rotate_back(left_basis, direction, right_basis) + DECAY_WEIGHT * master
    )
    stat_left = BETA_STAT * stats[:, 0] + (1.0 - BETA_STAT) * jnp.einsum(
        "sik,sjk->sij", grad_tiles, grad_tiles, precision=PRECISE
    )
    stat_right = BETA_STAT * stats[:, 1] + (1.0 - BETA_STAT) * jnp.einsum(
        "ski,skj->sij", grad_tiles, grad_tiles, precision=PRECISE
    )
    stats_new = jnp.stack([stat_left, stat_right], axis=1)
    turned = jnp.einsum("stij,stjk->stik", stats_new, bases, precision=PRECISE)
    bases_new = orthonormal(turned.reshape((-1,) + turned.shape[2:])).reshape(bases.shape)
    return (master_new, first_new, second_new, stats_new, bases_new)


def shards(
    block_in,
    cotangent,
    lengths,
    vector_params,
    vector_first,
    vector_second,
    w_in,
    w_out,
    w_gate,
    w_up,
    w_down,
    tile_owner,
    tile_master,
    tile_first,
    tile_second,
    tile_stats,
    tile_bases,
):
    micro_count, _, tok_count, model_width = block_in.shape
    hidden_width = w_gate.shape[1]
    shard_rows = w_in.shape[0]
    half_rows = shard_rows // 2
    parts = lax.axis_size("fsdp")
    owners = lax.axis_size("dp")
    chips = owners // 2
    owner_id = lax.axis_index("dp")
    core = owner_id % 2
    place, far = place_of("dp")
    chip_group = [list(range(i, i + 2 * RING)) for i in range(0, owners, 2 * RING)]
    same_core = [[2 * i + c for i in range(chips)] for c in range(2)]
    ring_group = [[i + 2 * j + c for j in range(RING)] for i in range(0, owners, 2 * RING) for c in range(2)]
    same_ring_place = [
        [(h * 2 * RING + i) * parts + f for h in range(owners // (2 * RING)) for f in range(parts)]
        for i in range(2 * RING)
    ]
    tile_side = tile_master.shape[-1]
    per_owner = tile_master.shape[1]
    tile_count = tile_owner.shape[1]
    g_one, g_two, k_zero, k_one, k_two = [vector_params[i] for i in range(5)]

    def half_of(matrix):
        return lax.dynamic_slice(matrix, (core * half_rows, 0), (half_rows, matrix.shape[1]))

    conv_block = jnp.concatenate([half_of(w_in), half_of(w_out)], axis=1)
    conv_pieces = spread(conv_block, "fsdp")
    whole_in, whole_out = assemble(conv_pieces, (3 * model_width, model_width))
    positions = lax.axis_index("fsdp") * tok_count + jnp.arange(tok_count, dtype=jnp.int32)
    live_mask = (positions[None, :] < lengths).astype(jnp.float32)[:, :, None]
    seed_grad = (cotangent[:, 0] * live_mask).reshape(-1, model_width)
    grad_feed = lax.all_gather(
        seed_grad.astype(jnp.bfloat16), "dp", axis_index_groups=chip_group, axis=0
    )
    hidden = hidden_width // RING // 2
    wide = -(-hidden // tile_side) * tile_side
    shift = 2 * hidden - wide
    columns = jnp.arange(wide, dtype=jnp.int32)
    kept = (columns >= core * (wide - hidden)) & (columns < hidden + core * (wide - hidden))

    def slice_of(matrix):
        first = place * (2 * hidden) + core * shift
        return jnp.where(
            kept[None, :], lax.dynamic_slice(matrix, (0, first), (shard_rows, wide)), jnp.zeros((), matrix.dtype)
        )

    feed_block = jnp.concatenate([slice_of(matrix) for matrix in (w_gate, w_up, w_down)], axis=1)
    feed_weights = lax.all_gather(
        after(feed_block, *[array for array, _ in conv_pieces[4:]]), "fsdp", axis=0, tiled=True
    )

    token_rows = block_in.astype(jnp.float32).reshape(-1, model_width)
    scale_one = rms_factor(token_rows)
    normed = (token_rows * scale_one * g_one).astype(jnp.bfloat16)
    mixed_all = jnp.dot(normed, whole_in, preferred_element_type=jnp.float32)
    part_b = mixed_all[:, :model_width]
    part_c = mixed_all[:, model_width : 2 * model_width]
    part_x = mixed_all[:, 2 * model_width :]
    product = (part_b * part_x).reshape(micro_count, tok_count, model_width)
    extended = jnp.concatenate([from_behind(product[:, -2:], "fsdp", 1), product], axis=1)
    convolved = (
        k_zero * extended[:, :-2] + k_one * extended[:, 1:-1] + k_two * extended[:, 2:]
    ).reshape(-1, model_width)
    gated_conv = (part_c * convolved).astype(jnp.bfloat16)
    residual = token_rows + jnp.dot(gated_conv, whole_out, preferred_element_type=jnp.float32)
    scale_two = rms_factor(residual)
    normed_two = (residual * scale_two * g_two).astype(jnp.bfloat16)

    fed = spread_ring(normed_two, "dp")
    fed, normed_halves, gated_halves = lax.optimization_barrier(
        (fed, column_halves(normed, parts, core), column_halves(gated_conv, parts, core))
    )
    steps = jnp.array([0, RING - 1, 1, 2], dtype=jnp.int32)
    ring_places = (place + steps) % RING * 2
    order = jnp.concatenate([ring_places + core, ring_places + 1 - core]).astype(jnp.int32)
    fed_other = swap(fed)
    begun, back_parts = (), []
    for who, rows in enumerate((fed, fed_other)):
        *begun, back = feed_forward(
            order, rows.reshape(RING, -1, model_width), grad_feed, feed_weights, who * RING, begun
        )
        back_parts.append(back)
    grad_both, activation, out_parts = begun
    grad_normed_two, far_parts = collect_ring(*back_parts, "dp")
    grad_both, far_parts = lax.optimization_barrier((grad_both, far_parts))
    fed = jnp.concatenate([fed, fed_other])
    low = jnp.bfloat16
    feed_sums = jnp.concatenate(
        [
            outer_sum(fed, grad_both.reshape(-1, 2 * wide)).astype(low),
            outer_sum(grad_feed.reshape(-1, model_width), activation.reshape(-1, wide)).astype(low),
        ],
        axis=1,
    )
    grad_normed_two, feed_sums = lax.optimization_barrier((grad_normed_two, feed_sums))
    feed_rows = lax.psum_scatter(feed_sums, "fsdp", scatter_dimension=0, tiled=True)

    normed_mine, normed_other = normed_halves
    gated_mine, gated_other = gated_halves
    grad_res_norm, grad_gain_two = norm_back(residual, scale_two, g_two, grad_normed_two)
    grad_resid = seed_grad + grad_res_norm
    grad_branch = grad_resid.astype(jnp.bfloat16)
    grad_gated = back_dot(grad_branch, whole_out)
    grad_part_c = grad_gated * convolved
    grad_conv = (grad_gated * part_c).reshape(micro_count, tok_count, model_width)
    grad_ext = jnp.concatenate([grad_conv, from_behind(grad_conv[:, :2], "fsdp", -1)], axis=1)
    grad_product = (
        k_two * grad_conv + k_one * grad_ext[:, 1 : tok_count + 1] + k_zero * grad_ext[:, 2:]
    ).reshape(-1, model_width)
    grad_kernel = jnp.stack(
        [
            jnp.sum(grad_conv * extended[:, :-2], axis=(0, 1)),
            jnp.sum(grad_conv * extended[:, 1:-1], axis=(0, 1)),
            jnp.sum(grad_conv * extended[:, 2:], axis=(0, 1)),
        ]
    )
    grad_mixed = jnp.concatenate(
        [
            (grad_product * part_x).astype(jnp.bfloat16),
            grad_part_c.astype(jnp.bfloat16),
            (grad_product * part_b).astype(jnp.bfloat16),
        ],
        axis=1,
    )
    conv_sums = [
        chip_sum(outer_sum(normed_mine, grad_mixed), outer_sum(normed_other, grad_mixed)),
        chip_sum(outer_sum(gated_mine, grad_branch), outer_sum(gated_other, grad_branch)),
    ]
    block_width = 4 * model_width // chips
    conv_sums = jnp.stack(
        [
            matrix[:, first : first + 2 * block_width]
            for matrix in conv_sums
            for first in range(0, matrix.shape[1], 2 * block_width)
        ]
    )
    conv_cols = exchange(conv_sums, "dp", ring_group)

    grad_normed = back_dot(grad_mixed, whole_in)
    grad_rows_norm, grad_gain_one = norm_back(token_rows, scale_one, g_one, grad_normed)
    grad_rows = grad_resid + grad_rows_norm
    vector_grads = jnp.concatenate([grad_gain_one[None], grad_gain_two[None], grad_kernel], axis=0)
    vector_rows = vector_grads.shape[0]
    feed_rows = after(feed_rows, conv_sums, grad_rows)
    feed_rows = feed_rows.astype(jnp.float32) + pair(feed_rows, "dp").astype(jnp.float32)
    feed_tiles = lax.all_gather(feed_rows.astype(low), "dp", axis_index_groups=chip_group, axis=0)
    feed_out = lax.psum_scatter(
        after(out_parts, feed_tiles), "dp", scatter_dimension=0, axis_index_groups=chip_group
    )
    conv_cols = add_terms(conv_cols, packed(vector_grads, block_width), parts, chips // RING)
    conv_own = exchange(conv_cols, ("dp", "fsdp"), same_ring_place)
    conv_own = jnp.sum(conv_own.astype(jnp.float32), axis=0)
    vector_part = unpacked(conv_own[half_rows:], vector_rows)
    conv_own = jnp.concatenate(
        [conv_own[:half_rows].astype(low), packed(vector_part, block_width)]
    )
    conv_tiles = exchange(jnp.broadcast_to(conv_own, (chips,) + conv_own.shape), "dp", same_core)
    vector_grads = unpacked(jnp.sum(conv_tiles[:RING, half_rows:].astype(jnp.float32), axis=0), vector_rows)
    vector_grads = vector_grads + swap(vector_grads)

    slot_index = slot_table(tile_owner[0], per_owner)
    slot_match = slot_index[None, :] == jnp.arange(per_owner * owners, dtype=jnp.int32)[:, None]
    tile_of_slot = (
        jnp.sum(
            jnp.where(slot_match, jnp.arange(1, tile_count + 1, dtype=jnp.int32)[None, :], 0), axis=1
        )
        - 1
    )
    wanted = jnp.concatenate(
        [
            lax.dynamic_slice(tile_of_slot, (owner_id * per_owner,), (per_owner,)),
            lax.dynamic_slice(tile_of_slot, ((owner_id ^ 1) * per_owner,), (per_owner,)),
        ]
    )
    conv_count = 4 * model_width // tile_side
    each_conv, each_feed = conv_count // chips, 2 * hidden // tile_side
    parts_far = chips // RING
    feed_tile = wanted - conv_count
    within = feed_tile % each_feed
    feed_first = feed_tile // (each_feed * RING) * (wide // tile_side)
    is_conv = wanted < conv_count
    own_slot = jnp.arange(2 * per_owner) < per_owner
    left, right = within < wide // tile_side, within >= shift // tile_side
    table = jnp.stack(
        [
            jnp.where(is_conv, 1, jnp.where(own_slot, 2, 0)),
            jnp.where(
                is_conv,
                wanted // each_conv % parts_far * RING + wanted // each_conv // parts_far,
                feed_tile // each_feed % RING * 2,
            ),
            jnp.where(is_conv, wanted % each_conv, jnp.where(left, feed_first + within, -1)),
            jnp.where(right, feed_first + within - shift // tile_side, -1),
            jnp.where(is_conv, core, 0),
        ],
        axis=1,
    )
    table = jnp.where(wanted[:, None] < 0, 0, table).astype(jnp.int32).reshape(-1)
    mine, other = pick(table, conv_tiles, feed_tiles, per_owner, tile_side)
    owned_grads = mine + swap(other).astype(jnp.float32)
    master_new, first_new, second_new, stats_new, bases_new = soap_update(
        owned_grads, tile_master[0], tile_first[0], tile_second[0], tile_stats[0], tile_bases[0]
    )
    master_low = master_new.astype(low)
    masters = exchange(jnp.broadcast_to(master_low, (chips,) + master_low.shape), "dp", same_core)
    masters, bases_new, feed_out = lax.optimization_barrier((masters, bases_new, feed_out))
    result_rows = residual + feed_out.astype(jnp.float32)
    vec_first = BETA_ONE * vector_first + (1.0 - BETA_ONE) * vector_grads
    vec_second = BETA_TWO * vector_second + (1.0 - BETA_TWO) * vector_grads * vector_grads
    vec_new = vector_params - RATE_VECTOR * (vec_first / (1.0 - BETA_ONE**STEP)) / (
        jnp.sqrt(vec_second / (1.0 - BETA_TWO**STEP)) + EPS_ADAM
    )
    w_in_new, w_out_new, w_gate_new, w_up_new, w_down_new = put(
        core,
        slot_index,
        masters,
        swap(masters),
        (3 * model_width, model_width, hidden_width, hidden_width, hidden_width),
    )
    whole_shape = (micro_count, 1, tok_count, model_width)
    return (
        result_rows.reshape(whole_shape),
        grad_rows.reshape(whole_shape),
        vec_new,
        vec_first,
        vec_second,
        w_in_new,
        w_out_new,
        w_gate_new,
        w_up_new,
        w_down_new,
        master_new[None],
        first_new[None],
        second_new[None],
        stats_new[None],
        bases_new[None],
    )


def solution(mesh):
    return jax.shard_map(
        shards,
        mesh=mesh,
        in_specs=(
            P(None, "dp", "fsdp", None),
            P(None, "dp", "fsdp", None),
            P(None, "dp"),
            P(),
            P(),
            P(),
            P("fsdp", None),
            P("fsdp", None),
            P("fsdp", None),
            P("fsdp", None),
            P("fsdp", None),
            P("fsdp", None),
            P("fsdp", "dp", None, None),
            P("fsdp", "dp", None, None),
            P("fsdp", "dp", None, None),
            P("fsdp", "dp", None, None, None),
            P("fsdp", "dp", None, None, None),
        ),
        out_specs=(
            P(None, "dp", "fsdp", None),
            P(None, "dp", "fsdp", None),
            P(),
            P(),
            P(),
            P("fsdp", None),
            P("fsdp", None),
            P("fsdp", None),
            P("fsdp", None),
            P("fsdp", None),
            P("fsdp", "dp", None, None),
            P("fsdp", "dp", None, None),
            P("fsdp", "dp", None, None),
            P("fsdp", "dp", None, None, None),
            P("fsdp", "dp", None, None, None),
        ),
        check_vma=False,
    )
```

```python
import functools

import jax
import jax.numpy as jnp
from jax import lax
from jax.experimental import pallas as pl
from jax.experimental.pallas import tpu as pltpu
from jax.sharding import PartitionSpec as P

STEP = 10


EPS_NORM = 1e-05
EPS_ADAM = 1e-08
BETA_ONE = 0.5
BETA_TWO = 0.5
BETA_STAT = 0.5
RATE_MATRIX = 0.03
RATE_VECTOR = 0.2
DECAY_WEIGHT = 0.01
PRECISE = lax.Precision.HIGHEST
BACK_DIMS = (((1,), (1,)), ((), ()))
TOKEN_DIMS = (((0,), (0,)), ((), ()))

PLAIN_DIMS = (((1,), (0,)), ((), ()))
PANEL = 16


def from_behind(value, axis, by):
    length = lax.axis_size(axis)
    pairs = [(i, i + by) for i in range(length) if 0 <= i + by < length]
    return lax.ppermute(value, axis, pairs)


def flip(value, axis, bit):
    length = lax.axis_size(axis)
    return lax.ppermute(value, axis, [(i, i ^ bit) for i in range(length)])


RING = 4


def ring(value, axis, by):
    length = lax.axis_size(axis)
    low = 2 if axis == "dp" else 1
    pairs = []
    for i in range(length):
        place = i // low % RING
        pairs.append((i, i + ((place + by) % RING - place) * low))
    return lax.ppermute(value, axis, pairs)


def pair(value, axis):
    return flip(value, axis, lax.axis_size(axis) // 2)


def swap(value):
    return flip(value, "dp", 1)


def place_of(axis):
    index = lax.axis_index(axis)
    low = 2 if axis == "dp" else 1
    return index // low % RING, index // (low * RING)


def spread(block, axis):
    half = block.shape[0] // 2
    behind, ahead, side = ring(block, axis, 1), ring(block, axis, -1), pair(block, axis)
    fore = ring(jnp.concatenate([behind[:half], side[:half]]), axis, 1)
    back = ring(jnp.concatenate([ahead[half:], side[half:]]), axis, -1)
    cross = pair(jnp.concatenate([behind[half:], ahead[:half]]), axis)
    early = [swap(array) for array in (block, behind, ahead)]
    *early, fore, back = lax.optimization_barrier((*early, fore, back))
    late = [fore, back, cross, ring(fore[half:], axis, 1), ring(back[half:], axis, -1)]
    other = early + [swap(array) for array in [side] + late]
    spans = [
        [(0, 2 * half, 0, 0, None)],
        [(0, 2 * half, -1, 0, None)],
        [(0, 2 * half, 1, 0, None)],
        [(0, 2 * half, 0, 1, None)],
        [(0, half, 2, 0, 0), (half, half, -1, 1, 0)],
        [(0, half, 2, 0, 1), (half, half, 1, 1, 1)],
        [(0, half, -1, 1, 1), (half, half, 1, 1, 0)],
        [(0, half, 2, 1, 0)],
        [(0, half, 2, 1, 1)],
    ]
    return [block, behind, ahead, side] + late, other, spans


def spread_ring(block, axis):
    half = block.shape[0] // 2
    before, after = ring(block, axis, 1), ring(block, axis, -1)
    return jnp.concatenate(
        [block, before, after, ring(before[:half], axis, 1), ring(after[half:], axis, -1)]
    )


def collect_ring(mine, other, axis):
    half = mine.shape[1] // 2
    low, wide = jnp.bfloat16, jnp.float32
    far = mine[3].astype(wide) + swap(other[3]).astype(wide)
    rest = swap(other[:3])
    one = ring(far[:half].astype(low), axis, -1)
    two = ring(far[half:].astype(low), axis, 1)
    behind = mine[1].astype(wide) + rest[1].astype(wide)
    ahead = mine[2].astype(wide) + rest[2].astype(wide)
    behind = jnp.concatenate([behind[:half] + one.astype(wide), behind[half:]])
    ahead = jnp.concatenate([ahead[:half], ahead[half:] + two.astype(wide)])
    from_ahead = ring(behind.astype(low), axis, -1)
    from_back = ring(ahead.astype(low), axis, 1)
    total = mine[0].astype(wide) + rest[0].astype(wide) + from_ahead.astype(wide) + from_back.astype(wide)
    return total, (one, two)


def after(value, *others):
    return lax.optimization_barrier((value,) + others)[0]


def packed(rows, width):
    high = rows.astype(jnp.bfloat16)
    rest = (rows - high.astype(jnp.float32)).astype(jnp.bfloat16)
    return high.reshape(-1, width), rest.reshape(-1, width)


def padded(rows, multiple):
    return jnp.pad(rows, ((0, -rows.shape[0] % multiple), (0, 0)))


ANYWHERE = pl.BlockSpec(memory_space=pl.ANY)
SCALARS = pl.BlockSpec(memory_space=pltpu.SMEM)
INSIDE = pl.BlockSpec(memory_space=pltpu.VMEM)
ROOM = pltpu.CompilerParams(vmem_limit_bytes=56 * 2**20)


def project_kernel(spans, offsets_ref, rows_ref, *refs):
    count = len(refs) - 6
    pieces, (out_ref, *whole_refs) = refs[:count], refs[count : count + 3]
    held, in_sem, out_sems = refs[count + 3 :]
    for i, (which, first, rows) in enumerate(spans):
        offset = pl.multiple_of(offsets_ref[i], rows)
        pltpu.make_async_copy(
            pieces[which].at[pl.ds(first, rows)], held.at[pl.ds(offset, rows)], in_sem
        ).start()
    pltpu.make_async_copy(held, held, in_sem).wait()
    stores, column = [], 0
    for j, whole in enumerate(whole_refs):
        width = whole.shape[1]
        stores.append(
            pltpu.make_async_copy(held.at[:, pl.ds(column, width)], whole, out_sems.at[j])
        )
        stores[-1].start()
        column += width
    step = 512
    for column in range(0, out_ref.shape[1], step):
        out_ref[:, column : column + step] = jnp.dot(
            rows_ref[...], held[:, column : column + step], preferred_element_type=jnp.float32
        )
    for store in stores:
        store.wait()


def project(rows, gathered, widths):
    core = lax.axis_index("dp") % 2
    place, side = place_of("fsdp")
    mine, other, pieces = gathered
    block = mine[0].shape[0]
    spans, offsets = [], []
    for who in range(2):
        for at, cuts in enumerate(pieces):
            for first, count, step, across, half in cuts:
                owner = (side ^ across) * RING + (place + step) % RING
                spans.append((who * len(pieces) + at, first, count))
                offsets.append((owner * 2 + (core ^ who)) * block + (half or 0) * count)
    depth = 2 * block * 2 * RING
    kind = mine[0].dtype
    return pl.pallas_call(
        functools.partial(project_kernel, spans),
        out_shape=[jax.ShapeDtypeStruct((rows.shape[0], widths[0]), jnp.float32)]
        + [jax.ShapeDtypeStruct((depth, width), kind) for width in widths],
        in_specs=[SCALARS, INSIDE] + [ANYWHERE] * (len(mine) + len(other)),
        out_specs=[INSIDE] + [ANYWHERE] * len(widths),
        compiler_params=ROOM,
        scratch_shapes=[
            pltpu.VMEM((depth, sum(widths)), kind),
            pltpu.SemaphoreType.DMA,
            pltpu.SemaphoreType.DMA((len(widths),)),
        ],
    )(jnp.stack(offsets).astype(jnp.int32), rows, *mine, *other)


def pick_kernel(table_ref, conv_ref, feed_ref, mine_ref, other_ref, held, sem):
    slots, side = mine_ref.shape[0], mine_ref.shape[1]
    half = side // 2
    held[...] = jnp.zeros_like(held)

    def one(i, finish):
        at = 5 * i
        kind, piece = table_ref[at], table_ref[at + 1]
        first = pl.multiple_of(table_ref[at + 4] * half, half)

        def move(source, target):
            copy = pltpu.make_async_copy(source, target, sem)
            if finish:
                copy.wait()
            else:
                copy.start()

        def column(k):
            return pl.ds(pl.multiple_of(k * side, side), side)

        @pl.when(kind == 1)
        def _():
            move(
                conv_ref.at[piece, pl.ds(0, half), column(table_ref[at + 2])],
                held.at[0, i, pl.ds(first, half), :],
            )

        for which in range(2):

            @pl.when((kind == 2) & (table_ref[at + 2 + which] >= 0))
            def _():
                move(feed_ref.at[piece + which, :, column(table_ref[at + 2 + which])], held.at[which, i])

    for finish in (False, True):

        def step(i, carry):
            one(i, finish)
            return carry

        lax.fori_loop(0, 2 * slots, step, 0)
    for q in range(slots):
        mine_ref[q] = held[0, q].astype(jnp.float32) + held[1, q].astype(jnp.float32)
        other_ref[q] = held[0, slots + q]


def pick(table, conv, feed, slots, side):
    shape = (slots, side, side)
    return pl.pallas_call(
        pick_kernel,
        out_shape=[jax.ShapeDtypeStruct(shape, jnp.float32), jax.ShapeDtypeStruct(shape, conv.dtype)],
        in_specs=[SCALARS, ANYWHERE, ANYWHERE],
        out_specs=[INSIDE, INSIDE],
        compiler_params=ROOM,
        scratch_shapes=[
            pltpu.VMEM((2, 2 * slots, side, side), conv.dtype),
            pltpu.SemaphoreType.DMA,
        ],
    )(table, conv, feed)


def add_kernel(own_ref, ahead_ref, behind_ref, extra_ref, out_ref):
    width = out_ref.shape[2]
    parts = own_ref.shape[1] // width
    rows = out_ref.shape[1] - extra_ref.shape[1]
    blocks = out_ref.shape[0] // parts
    for i in range(blocks):
        cut = pl.ds(i * rows, rows)
        total = own_ref[cut, :] + ahead_ref[cut, :].astype(jnp.float32)
        total = (total + behind_ref[cut, :].astype(jnp.float32)).astype(out_ref.dtype)
        for k in range(parts):
            out_ref[k * blocks + i, :rows, :] = total[:, k * width : (k + 1) * width]
            out_ref[k * blocks + i, rows:, :] = extra_ref[k]


def add_terms(own, ahead, behind, extra, blocks):
    parts = extra.shape[0]
    rows, width = own.shape[0] // blocks + extra.shape[1], own.shape[1] // parts
    return pl.pallas_call(
        add_kernel,
        out_shape=jax.ShapeDtypeStruct((parts * blocks, rows, width), ahead.dtype),
        in_specs=[INSIDE] * 4,
        out_specs=INSIDE,
        compiler_params=ROOM,
        cost_estimate=pl.CostEstimate(
            flops=50 * 10**9, bytes_accessed=own.size * 8, transcendentals=0
        ),
    )(own, ahead, behind, extra)


def put_kernel(core_ref, slot_ref, mine_ref, other_ref, *refs):
    count = (len(refs) - 3) // 2
    outs, pages = refs[:count], refs[count : 2 * count]
    held, in_sems, out_sems = refs[-3:]
    chips, slots, side = mine_ref.shape[0], mine_ref.shape[1], mine_ref.shape[2]
    loads = [
        pltpu.make_async_copy(source, held.at[i], in_sems.at[i])
        for i, source in enumerate((mine_ref, other_ref))
    ]
    for load in loads:
        load.start()
    for load in loads:
        load.wait()
    tile = 0
    for j in range(count):
        for k in range(outs[j].shape[1] // side):
            slot = slot_ref[tile]
            owner = slot // slots
            pages[j][:, k * side : (k + 1) * side] = held[owner % 2 ^ core_ref[0], owner // 2, slot % slots]
            tile += 1
        pltpu.make_async_copy(pages[j], outs[j], out_sems.at[j]).start()
    for j in range(count):
        pltpu.make_async_copy(pages[j], outs[j], out_sems.at[j]).wait()


def put(core, slot_index, mine, other, widths):
    side = mine.shape[-1]
    return pl.pallas_call(
        put_kernel,
        out_shape=[jax.ShapeDtypeStruct((side, width), mine.dtype) for width in widths],
        in_specs=[SCALARS, SCALARS, ANYWHERE, ANYWHERE],
        out_specs=[ANYWHERE] * len(widths),
        compiler_params=ROOM,
        scratch_shapes=[pltpu.VMEM((side, width), mine.dtype) for width in widths]
        + [
            pltpu.VMEM((2,) + mine.shape, mine.dtype),
            pltpu.SemaphoreType.DMA((2,)),
            pltpu.SemaphoreType.DMA((len(widths),)),
        ],
    )(core.astype(jnp.int32).reshape(1), slot_index, mine, other)


def feed_kernel(order_ref, fed_ref, dy_ref, w_ref, *refs):
    both_ref, act_ref, out_ref, back_ref = refs[-4:]
    width = act_ref.shape[-1]
    mixed = jnp.dot(fed_ref[0], w_ref[:, : 2 * width], preferred_element_type=jnp.float32)
    grad_act = jnp.dot(dy_ref[0], w_ref[:, 2 * width :], preferred_element_type=jnp.float32)
    gate, up = mixed[:, :width], mixed[:, width:]
    sigmoid = jax.nn.sigmoid(gate)
    passed = gate * sigmoid
    activation = (passed * up).astype(jnp.bfloat16)
    grad_gate = grad_act * up * sigmoid * (1.0 + gate * (1.0 - sigmoid))
    grad_up = grad_act * passed
    both = jnp.concatenate([grad_gate.astype(jnp.bfloat16), grad_up.astype(jnp.bfloat16)], axis=1)
    both_ref[0] = both
    act_ref[0] = activation
    back_ref[0] = back_dot(both, w_ref[:, : 2 * width]).astype(jnp.bfloat16)
    out_ref[0] = back_dot(activation, w_ref[:, 2 * width :]).astype(jnp.bfloat16)


def feed_forward(order, fed, grad_feed, weights, first, begun):
    blocks, rows, model_width = fed.shape
    width = weights.shape[1] // 3
    begun = list(begun)

    def turned(i, order_ref):
        return (order_ref[first + i], 0, 0)

    def shape(count, columns):
        return jax.ShapeDtypeStruct((count, rows, columns), jnp.bfloat16)

    whole = grad_feed.shape[0]

    return pl.pallas_call(
        feed_kernel,
        grid_spec=pltpu.PrefetchScalarGridSpec(
            num_scalar_prefetch=1,
            grid=(blocks,),
            in_specs=[
                pl.BlockSpec((1, rows, model_width), lambda i, order_ref: (i, 0, 0)),
                pl.BlockSpec((1, rows, model_width), turned),
                pl.BlockSpec(weights.shape, lambda i, order_ref: (0, 0)),
            ]
            + [ANYWHERE] * len(begun),
            out_specs=[
                pl.BlockSpec((1, rows, 2 * width), lambda i, order_ref: (first + i, 0, 0)),
                pl.BlockSpec((1, rows, width), turned),
                pl.BlockSpec((1, rows, model_width), turned),
                pl.BlockSpec((1, rows, model_width), lambda i, order_ref: (i, 0, 0)),
            ],
        ),
        out_shape=[
            shape(whole, 2 * width),
            shape(whole, width),
            shape(whole, model_width),
            shape(blocks, model_width),
        ],
        input_output_aliases={4 + i: i for i in range(len(begun))},
        compiler_params=ROOM,
        cost_estimate=pl.CostEstimate(
            flops=2 * blocks * rows * model_width * width * 6,
            bytes_accessed=blocks * rows * (4 * model_width + 3 * width) * 2,
            transcendentals=blocks * rows * width,
        ),
    )(order, fed, grad_feed, weights, *begun)


def rms_factor(values):
    return lax.rsqrt(jnp.mean(values * values, axis=-1, keepdims=True) + EPS_NORM)


def norm_back(values, scale_val, gain_row, grad_out):
    weighted = grad_out * gain_row
    inner = jnp.mean(values * weighted, axis=-1, keepdims=True)
    grad_values = scale_val * weighted - values * scale_val * scale_val * scale_val * inner
    grad_gain = jnp.sum(values * scale_val * grad_out, axis=0)
    return (grad_values, grad_gain)


def outer_sum(left_arr, right_arr):
    return lax.dot_general(left_arr, right_arr, TOKEN_DIMS, preferred_element_type=jnp.float32)


def back_dot(left_arr, right_arr):
    return lax.dot_general(left_arr, right_arr, BACK_DIMS, preferred_element_type=jnp.float32)


def exchange(value, axis, groups=None):
    return lax.all_to_all(value, axis, 0, 0, axis_index_groups=groups)


def column_halves(value, parts, core):
    cut = value.reshape(value.shape[0], parts, 2, -1)
    mine = lax.dynamic_index_in_dim(cut, core, 2, keepdims=False).reshape(value.shape[0], -1)
    other = lax.dynamic_index_in_dim(cut, 1 - core, 2, keepdims=False).reshape(value.shape[0], -1)
    return jnp.concatenate([mine, swap(other)])


def slot_table(owner_row, per_owner):
    tile_count = owner_row.shape[0]
    same_owner = owner_row[None, :] == owner_row[:, None]
    before = (
        jnp.arange(tile_count, dtype=jnp.int32)[None, :]
        < jnp.arange(tile_count, dtype=jnp.int32)[:, None]
    )
    slot_rank = jnp.sum((same_owner & before).astype(jnp.int32), axis=1)
    return owner_row * per_owner + slot_rank


def split_dot(left, right, dims, axis):
    def cut(value):
        high = value.astype(jnp.bfloat16)
        rest = value - high.astype(jnp.float32)
        middle = rest.astype(jnp.bfloat16)
        return high, middle, (rest - middle.astype(jnp.float32)).astype(jnp.bfloat16)

    left_cut, right_cut = cut(left), cut(right)
    pairs = ((0, 0), (0, 1), (1, 0), (1, 1), (0, 2), (2, 0))
    return lax.dot_general(
        jnp.concatenate([left_cut[i] for i, _ in pairs], axis[0]),
        jnp.concatenate([right_cut[j] for _, j in pairs], axis[1]),
        dims,
        preferred_element_type=jnp.float32,
    )


def bases_kernel(grad_ref, stats_ref, bases_ref, stats_out, q_ref, m_ref, w_ref):
    tiles, side = grad_ref.shape[0], grad_ref.shape[1]
    count = 2 * tiles
    for i in range(tiles):
        grad = grad_ref[i]
        for j, dims in enumerate((BACK_DIMS, TOKEN_DIMS)):
            axis = 1 - j
            square = near_dot(grad, grad, dims, (axis, axis))
            stats_out[i, j] = BETA_STAT * stats_ref[i, j] + (1.0 - BETA_STAT) * square
    for g in range(count):
        m_ref[g] = split_dot(stats_out[g // 2, g % 2], bases_ref[g // 2, g % 2], PLAIN_DIMS, (1, 0))
    row = lax.broadcasted_iota(jnp.int32, (8, side), 0)
    lane = lax.broadcasted_iota(jnp.int32, (8, side), 1)
    rows = lax.broadcasted_iota(jnp.int32, (PANEL, side), 0)
    lanes = lax.broadcasted_iota(jnp.int32, (PANEL, side), 1)
    all_rows = lax.broadcasted_iota(jnp.int32, (side, side), 0)
    all_lanes = lax.broadcasted_iota(jnp.int32, (side, side), 1)
    for g in range(count):
        w_ref[g] = split_dot(m_ref[g], m_ref[g], TOKEN_DIMS, (0, 0))
    for base in range(0, side, PANEL):
        end = base + PANEL
        panels = [[w_ref[g, i : i + 8, :] for i in range(base, end, 8)] for g in range(count)]
        for k in range(PANEL):
            at, inside = k // 8, k % 8
            hit = lane == base + k
            for g in range(count):
                panel = panels[g]
                column = jnp.broadcast_to(panel[at][:, base + k : base + k + 1], (8, side))
                scale = lax.rsqrt(jnp.broadcast_to(column[inside : inside + 1], (8, side)))
                top = jnp.broadcast_to(panel[at][inside : inside + 1], (8, side))
                top = jnp.where(hit, scale, top * scale)
                part = jnp.where(hit, 0.0, panel[at]) - column * scale * top
                panel[at] = jnp.where(row > inside, part, jnp.where(row == inside, top, panel[at]))
                for i in range(at + 1, PANEL // 8):
                    column = jnp.broadcast_to(panel[i][:, base + k : base + k + 1], (8, side))
                    panel[i] = jnp.where(hit, 0.0, panel[i]) - column * scale * top
        for g in range(count):
            done = jnp.concatenate(panels[g], axis=0)
            w_ref[g, base:end, :] = done
            if end < side:
                upper = (lanes >= base) & (lanes < end) & (lanes - base > rows)
                change = split_dot(done, jnp.where(upper, 0.0, done), TOKEN_DIMS, (0, 0))[end:]
                gone = (all_lanes[end:] >= base) & (all_lanes[end:] < end)
                w_ref[g, end:, :] = jnp.where(gone, 0.0, w_ref[g, end:, :]) - change
    for g in range(count):
        inverse = jnp.where(all_lanes <= all_rows, w_ref[g], 0.0)
        q_ref[g // 2, g % 2] = split_dot(m_ref[g], inverse, BACK_DIMS, (1, 1))


def near_dot(left, right, dims, axis):
    def cut(value):
        high = value.astype(jnp.bfloat16)
        return high, (value - high.astype(jnp.float32)).astype(jnp.bfloat16)

    (left_high, left_rest), (right_high, right_rest) = cut(left), cut(right)
    left_axis, right_axis = axis
    return lax.dot_general(
        jnp.concatenate([left_high, left_high, left_rest], left_axis),
        jnp.concatenate([right_high, right_rest, right_high], right_axis),
        dims,
        preferred_element_type=jnp.float32,
    )


def soap_kernel(
    mine_ref, other_ref, master_ref, first_ref, second_ref, bases_ref,
    grad_ref, master_out, first_out, second_out, low_out,
):
    count, side = mine_ref.shape[0], mine_ref.shape[1]
    for i in range(count):
        grad = mine_ref[i] + other_ref[i].astype(jnp.float32)
        first = BETA_ONE * first_ref[i] + (1.0 - BETA_ONE) * grad
        grad_ref[i] = grad
        first_out[i] = first
    turned = []
    for i in range(count):
        pair_rows = jnp.concatenate([grad_ref[i], first_out[i]], axis=1)
        turned.append(near_dot(bases_ref[i, 0], pair_rows, TOKEN_DIMS, (0, 0)))
    for i in range(count):
        stacked = jnp.concatenate([turned[i][:, :side], turned[i][:, side:]], axis=0)
        both = near_dot(stacked, bases_ref[i, 1], PLAIN_DIMS, (1, 0))
        rotated, moment = both[:side], both[side:]
        second = BETA_TWO * second_ref[i] + (1.0 - BETA_TWO) * rotated * rotated
        second_out[i] = second
        turned[i] = (
            moment
            / (1.0 - BETA_ONE**STEP)
            / (jnp.sqrt(second / (1.0 - BETA_TWO**STEP)) + EPS_ADAM)
        )
    for i in range(count):
        turned[i] = near_dot(bases_ref[i, 0], turned[i], PLAIN_DIMS, (1, 0))
    for i in range(count):
        step = near_dot(turned[i], bases_ref[i, 1], BACK_DIMS, (1, 1))
        master = master_ref[i] - RATE_MATRIX * (step + DECAY_WEIGHT * master_ref[i])
        master_out[i] = master
        for j in range(low_out.shape[0]):
            low_out[j, i] = master.astype(low_out.dtype)


def soap_update(mine, other, master, first, second, bases, copies):
    tiles = jax.ShapeDtypeStruct(mine.shape, jnp.float32)
    return pl.pallas_call(
        soap_kernel,
        out_shape=[tiles] * 4 + [jax.ShapeDtypeStruct((copies,) + mine.shape, jnp.bfloat16)],
        in_specs=[INSIDE] * 6,
        out_specs=[INSIDE] * 5,
        compiler_params=ROOM,
    )(mine, other, master, first, second, bases)


def bases_update(grad_tiles, stats, bases):
    tiles, _, side, _ = bases.shape
    whole = jax.ShapeDtypeStruct(bases.shape, jnp.float32)
    return pl.pallas_call(
        bases_kernel,
        out_shape=[whole, whole],
        in_specs=[INSIDE] * 3,
        out_specs=[INSIDE] * 2,
        scratch_shapes=[pltpu.VMEM((2 * tiles, side, side), jnp.float32) for _ in range(2)],
        compiler_params=ROOM,
        cost_estimate=pl.CostEstimate(
            flops=30 * 10**9, bytes_accessed=20 * bases.size, transcendentals=0
        ),
    )(grad_tiles, stats, bases)


def shards(
    block_in,
    cotangent,
    lengths,
    vector_params,
    vector_first,
    vector_second,
    w_in,
    w_out,
    w_gate,
    w_up,
    w_down,
    tile_owner,
    tile_master,
    tile_first,
    tile_second,
    tile_stats,
    tile_bases,
):
    micro_count, _, tok_count, model_width = block_in.shape
    hidden_width = w_gate.shape[1]
    shard_rows = w_in.shape[0]
    half_rows = shard_rows // 2
    parts = lax.axis_size("fsdp")
    owners = lax.axis_size("dp")
    chips = owners // 2
    owner_id = lax.axis_index("dp")
    core = owner_id % 2
    place, far = place_of("dp")
    chip_group = [list(range(i, i + 2 * RING)) for i in range(0, owners, 2 * RING)]
    same_core = [[2 * i + c for i in range(chips)] for c in range(2)]
    same_ring_place = [
        [(h * 2 * RING + i) * parts + f for h in range(owners // (2 * RING)) for f in range(parts)]
        for i in range(2 * RING)
    ]
    tile_side = tile_master.shape[-1]
    per_owner = tile_master.shape[1]
    tile_count = tile_owner.shape[1]
    g_one, g_two, k_zero, k_one, k_two = [vector_params[i] for i in range(5)]

    def half_of(matrix):
        return lax.dynamic_slice(matrix, (core * half_rows, 0), (half_rows, matrix.shape[1]))

    conv_block = jnp.concatenate([half_of(w_in), half_of(w_out)], axis=1)
    conv_pieces = spread(conv_block, "fsdp")
    positions = lax.axis_index("fsdp") * tok_count + jnp.arange(tok_count, dtype=jnp.int32)
    live_mask = (positions[None, :] < lengths).astype(jnp.float32)[:, :, None]
    seed_grad = (cotangent[:, 0] * live_mask).reshape(-1, model_width)
    grad_feed = lax.all_gather(
        seed_grad.astype(jnp.bfloat16), "dp", axis_index_groups=chip_group, axis=0
    )
    hidden = hidden_width // RING // 2
    wide = -(-hidden // tile_side) * tile_side
    shift = 2 * hidden - wide
    columns = jnp.arange(wide, dtype=jnp.int32)
    kept = (columns >= core * (wide - hidden)) & (columns < hidden + core * (wide - hidden))

    def slice_of(matrix):
        first = place * (2 * hidden) + core * shift
        return jnp.where(
            kept[None, :], lax.dynamic_slice(matrix, (0, first), (shard_rows, wide)), jnp.zeros((), matrix.dtype)
        )

    feed_block = jnp.concatenate([slice_of(matrix) for matrix in (w_gate, w_up, w_down)], axis=1)
    feed_weights = lax.all_gather(
        after(feed_block, *conv_pieces[0][4:]), "fsdp", axis=0, tiled=True
    )

    token_rows = block_in.astype(jnp.float32).reshape(-1, model_width)
    scale_one = rms_factor(token_rows)
    normed = (token_rows * scale_one * g_one).astype(jnp.bfloat16)
    mixed_all, whole_in, whole_out = project(normed, conv_pieces, (3 * model_width, model_width))
    part_b = mixed_all[:, :model_width]
    part_c = mixed_all[:, model_width : 2 * model_width]
    part_x = mixed_all[:, 2 * model_width :]
    product = (part_b * part_x).reshape(micro_count, tok_count, model_width)
    extended = jnp.concatenate([from_behind(product[:, -2:], "fsdp", 1), product], axis=1)
    convolved = (
        k_zero * extended[:, :-2] + k_one * extended[:, 1:-1] + k_two * extended[:, 2:]
    ).reshape(-1, model_width)
    gated_conv = (part_c * convolved).astype(jnp.bfloat16)
    residual = token_rows + jnp.dot(gated_conv, whole_out, preferred_element_type=jnp.float32)
    scale_two = rms_factor(residual)
    normed_two = (residual * scale_two * g_two).astype(jnp.bfloat16)

    fed = spread_ring(normed_two, "dp")
    fed, normed_halves, gated_halves = lax.optimization_barrier(
        (fed, column_halves(normed, parts, core), column_halves(gated_conv, parts, core))
    )
    steps = jnp.array([0, RING - 1, 1, 2], dtype=jnp.int32)
    ring_places = (place + steps) % RING * 2
    order = jnp.concatenate([ring_places + core, ring_places + 1 - core]).astype(jnp.int32)
    fed_other = swap(fed)
    begun, back_parts = (), []
    for who, rows in enumerate((fed, fed_other)):
        *begun, back = feed_forward(
            order, rows.reshape(RING, -1, model_width), grad_feed, feed_weights, who * RING, begun
        )
        back_parts.append(back)
    grad_both, activation, out_parts = begun
    grad_normed_two, far_parts = collect_ring(*back_parts, "dp")
    grad_both, far_parts = lax.optimization_barrier((grad_both, far_parts))
    fed = jnp.concatenate([fed, fed_other])
    low = jnp.bfloat16
    feed_sums = jnp.concatenate(
        [
            outer_sum(fed, grad_both.reshape(-1, 2 * wide)).astype(low),
            outer_sum(grad_feed.reshape(-1, model_width), activation.reshape(-1, wide)).astype(low),
        ],
        axis=1,
    )
    grad_normed_two, feed_sums = lax.optimization_barrier((grad_normed_two, feed_sums))
    feed_rows = lax.psum_scatter(feed_sums, "fsdp", scatter_dimension=0, tiled=True)

    grad_res_norm, grad_gain_two = norm_back(residual, scale_two, g_two, grad_normed_two)
    grad_resid = seed_grad + grad_res_norm
    grad_branch = grad_resid.astype(jnp.bfloat16)
    grad_gated = back_dot(grad_branch, whole_out)
    grad_part_c = grad_gated * convolved
    grad_conv = (grad_gated * part_c).reshape(micro_count, tok_count, model_width)
    grad_ext = jnp.concatenate([grad_conv, from_behind(grad_conv[:, :2], "fsdp", -1)], axis=1)
    grad_product = (
        k_two * grad_conv + k_one * grad_ext[:, 1 : tok_count + 1] + k_zero * grad_ext[:, 2:]
    ).reshape(-1, model_width)
    grad_kernel = jnp.stack(
        [
            jnp.sum(grad_conv * extended[:, :-2], axis=(0, 1)),
            jnp.sum(grad_conv * extended[:, 1:-1], axis=(0, 1)),
            jnp.sum(grad_conv * extended[:, 2:], axis=(0, 1)),
        ]
    )
    grad_all = jnp.concatenate(
        [
            (grad_product * part_x).astype(low),
            grad_part_c.astype(low),
            (grad_product * part_b).astype(low),
            grad_branch,
        ],
        axis=1,
    )
    grad_mixed = grad_all[:, : 3 * model_width]

    def conv_block(step, grads):
        index = (place + step) % RING
        right = [
            lax.dynamic_slice(part, (0, index * model_width), (part.shape[0], model_width)) for part in grads
        ]
        left = jnp.where(index == RING - 1, gated_halves, normed_halves)
        return outer_sum(left, jnp.concatenate(right))

    grads = (grad_all, swap(grad_all))
    conv_far = conv_block(2, grads).astype(low)
    middle = conv_far.shape[0] // 2
    one, two = ring(conv_far[:middle], "dp", -1), ring(conv_far[middle:], "dp", 1)
    *grads, _ = lax.optimization_barrier((*grads, conv_far))
    behind, ahead = conv_block(-1, grads), conv_block(1, grads)
    one, two = one.astype(jnp.float32), two.astype(jnp.float32)
    behind = (behind + jnp.concatenate([one, jnp.zeros_like(one)])).astype(low)
    ahead = (ahead + jnp.concatenate([jnp.zeros_like(two), two])).astype(low)
    conv_sums = conv_block(0, grads)
    conv_cols = [conv_sums, ring(behind, "dp", -1), ring(ahead, "dp", 1)]

    grad_normed = back_dot(after(grad_mixed, behind, ahead), whole_in)
    grad_rows_norm, grad_gain_one = norm_back(token_rows, scale_one, g_one, grad_normed)
    vector_grads = jnp.concatenate([grad_gain_one[None], grad_gain_two[None], grad_kernel], axis=0)
    vector_rows = vector_grads.shape[0]
    feed_rows = after(feed_rows, behind, ahead)
    feed_rows = feed_rows.astype(jnp.float32) + pair(feed_rows, "dp").astype(jnp.float32)
    feed_tiles = lax.all_gather(feed_rows.astype(low), "dp", axis_index_groups=chip_group, axis=0)
    block_width = model_width // (chips // RING)
    extra = jnp.stack([padded(rows, 16) for rows in packed(vector_grads, block_width)])
    conv_cols = add_terms(*conv_cols, extra, parts)
    conv_own = exchange(conv_cols, ("dp", "fsdp"), same_ring_place)
    conv_own = jnp.sum(conv_own.astype(jnp.float32), axis=0)
    packed_rows = vector_rows * (model_width // block_width)
    vector_part = jnp.concatenate(packed(conv_own[half_rows : half_rows + packed_rows], block_width))
    conv_own = jnp.concatenate([conv_own[:half_rows].astype(low), padded(vector_part, 32)])
    conv_tiles = exchange(jnp.broadcast_to(conv_own, (chips,) + conv_own.shape), "dp", same_core)
    vector_part = jnp.sum(
        conv_tiles[:, half_rows : half_rows + 2 * packed_rows].astype(jnp.float32), axis=0
    ).reshape(2 * vector_rows, model_width)
    vector_grads = vector_part[:vector_rows] + vector_part[vector_rows:]
    vector_grads = vector_grads + swap(vector_grads)
    feed_out = lax.psum_scatter(
        after(out_parts, conv_own), "dp", scatter_dimension=0, axis_index_groups=chip_group
    )

    slot_index = slot_table(tile_owner[0], per_owner)
    slot_match = slot_index[None, :] == jnp.arange(per_owner * owners, dtype=jnp.int32)[:, None]
    tile_of_slot = (
        jnp.sum(
            jnp.where(slot_match, jnp.arange(1, tile_count + 1, dtype=jnp.int32)[None, :], 0), axis=1
        )
        - 1
    )
    wanted = jnp.concatenate(
        [
            lax.dynamic_slice(tile_of_slot, (owner_id * per_owner,), (per_owner,)),
            lax.dynamic_slice(tile_of_slot, ((owner_id ^ 1) * per_owner,), (per_owner,)),
        ]
    )
    conv_count = 4 * model_width // tile_side
    each_conv, each_feed = conv_count // chips, 2 * hidden // tile_side
    parts_far = chips // RING
    feed_tile = wanted - conv_count
    within = feed_tile % each_feed
    feed_first = feed_tile // (each_feed * RING) * (wide // tile_side)
    is_conv = wanted < conv_count
    own_slot = jnp.arange(2 * per_owner) < per_owner
    left, right = within < wide // tile_side, within >= shift // tile_side
    table = jnp.stack(
        [
            jnp.where(is_conv, 1, jnp.where(own_slot, 2, 0)),
            jnp.where(
                is_conv,
                wanted // each_conv % parts_far * RING + wanted // each_conv // parts_far,
                feed_tile // each_feed % RING * 2,
            ),
            jnp.where(is_conv, wanted % each_conv, jnp.where(left, feed_first + within, -1)),
            jnp.where(right, feed_first + within - shift // tile_side, -1),
            jnp.where(is_conv, core, 0),
        ],
        axis=1,
    )
    table = jnp.where(wanted[:, None] < 0, 0, table).astype(jnp.int32).reshape(-1)
    mine, other = pick(table, conv_tiles, feed_tiles, per_owner, tile_side)
    owned_grads, master_new, first_new, second_new, master_low = soap_update(
        mine, swap(other), tile_master[0], tile_first[0], tile_second[0], tile_bases[0], chips
    )
    masters = exchange(master_low, "dp", same_core)
    stats_new, bases_new = bases_update(owned_grads, tile_stats[0], tile_bases[0])
    bases_new, feed_out, vector_grads, grad_resid = lax.optimization_barrier(
        (bases_new, feed_out, vector_grads, grad_resid)
    )
    result_rows = residual + feed_out.astype(jnp.float32)
    grad_rows = grad_resid + grad_rows_norm
    vec_first = BETA_ONE * vector_first + (1.0 - BETA_ONE) * vector_grads
    vec_second = BETA_TWO * vector_second + (1.0 - BETA_TWO) * vector_grads * vector_grads
    vec_new = vector_params - RATE_VECTOR * (vec_first / (1.0 - BETA_ONE**STEP)) / (
        jnp.sqrt(vec_second / (1.0 - BETA_TWO**STEP)) + EPS_ADAM
    )
    masters, bases_new, stats_new, result_rows, grad_rows, vec_new, vec_first, vec_second = (
        lax.optimization_barrier(
            (masters, bases_new, stats_new, result_rows, grad_rows, vec_new, vec_first, vec_second)
        )
    )
    widths = (3 * model_width, model_width, hidden_width, hidden_width, hidden_width)
    w_in_new, w_out_new, w_gate_new, w_up_new, w_down_new = put(
        core, slot_index, masters, swap(masters), widths
    )
    whole_shape = (micro_count, 1, tok_count, model_width)
    return (
        result_rows.reshape(whole_shape),
        grad_rows.reshape(whole_shape),
        vec_new,
        vec_first,
        vec_second,
        w_in_new,
        w_out_new,
        w_gate_new,
        w_up_new,
        w_down_new,
        master_new[None],
        first_new[None],
        second_new[None],
        stats_new[None],
        bases_new[None],
    )


def solution(mesh):
    return jax.shard_map(
        shards,
        mesh=mesh,
        in_specs=(
            P(None, "dp", "fsdp", None),
            P(None, "dp", "fsdp", None),
            P(None, "dp"),
            P(),
            P(),
            P(),
            P("fsdp", None),
            P("fsdp", None),
            P("fsdp", None),
            P("fsdp", None),
            P("fsdp", None),
            P("fsdp", None),
            P("fsdp", "dp", None, None),
            P("fsdp", "dp", None, None),
            P("fsdp", "dp", None, None),
            P("fsdp", "dp", None, None, None),
            P("fsdp", "dp", None, None, None),
        ),
        out_specs=(
            P(None, "dp", "fsdp", None),
            P(None, "dp", "fsdp", None),
            P(),
            P(),
            P(),
            P("fsdp", None),
            P("fsdp", None),
            P("fsdp", None),
            P("fsdp", None),
            P("fsdp", None),
            P("fsdp", "dp", None, None),
            P("fsdp", "dp", None, None),
            P("fsdp", "dp", None, None),
            P("fsdp", "dp", None, None, None),
            P("fsdp", "dp", None, None, None),
        ),
        check_vma=False,
    )
```

```python
import functools

import jax
import jax.numpy as jnp
from jax import lax
from jax.experimental import pallas as pl
from jax.experimental.pallas import tpu as pltpu
from jax.sharding import PartitionSpec as P

STEP = 10


EPS_NORM = 1e-05
EPS_ADAM = 1e-08
BETA_ONE = 0.5
BETA_TWO = 0.5
BETA_STAT = 0.5
RATE_MATRIX = 0.03
RATE_VECTOR = 0.2
DECAY_WEIGHT = 0.01
PRECISE = lax.Precision.HIGHEST
BACK_DIMS = (((1,), (1,)), ((), ()))
TOKEN_DIMS = (((0,), (0,)), ((), ()))

PLAIN_DIMS = (((1,), (0,)), ((), ()))
PANEL = 16


def from_behind(value, axis, by):
    length = lax.axis_size(axis)
    pairs = [(i, i + by) for i in range(length) if 0 <= i + by < length]
    return lax.ppermute(value, axis, pairs)


def flip(value, axis, bit):
    length = lax.axis_size(axis)
    return lax.ppermute(value, axis, [(i, i ^ bit) for i in range(length)])


RING = 4


def ring(value, axis, by):
    length = lax.axis_size(axis)
    low = 2 if axis == "dp" else 1
    pairs = []
    for i in range(length):
        place = i // low % RING
        pairs.append((i, i + ((place + by) % RING - place) * low))
    return lax.ppermute(value, axis, pairs)


def pair(value, axis):
    return flip(value, axis, lax.axis_size(axis) // 2)


def swap(value):
    return flip(value, "dp", 1)


def place_of(axis):
    index = lax.axis_index(axis)
    low = 2 if axis == "dp" else 1
    return index // low % RING, index // (low * RING)


def spread(block, axis, meanwhile):
    half = block.shape[0] // 2
    behind, ahead, side = ring(block, axis, 1), ring(block, axis, -1), pair(block, axis)
    behind, *meanwhile = lax.optimization_barrier((behind, *meanwhile))
    fore = ring(jnp.concatenate([behind[:half], side[:half]]), axis, 1)
    back = ring(jnp.concatenate([ahead[half:], side[half:]]), axis, -1)
    cross = pair(jnp.concatenate([behind[half:], ahead[:half]]), axis)
    early = [swap(array) for array in (block, behind, ahead)]
    *early, fore, back = lax.optimization_barrier((*early, fore, back))
    late = [fore, back, cross, ring(fore[half:], axis, 1), ring(back[half:], axis, -1)]
    other = early + [swap(array) for array in [side] + late]
    spans = [
        [(0, 2 * half, 0, 0, None)],
        [(0, 2 * half, -1, 0, None)],
        [(0, 2 * half, 1, 0, None)],
        [(0, 2 * half, 0, 1, None)],
        [(0, half, 2, 0, 0), (half, half, -1, 1, 0)],
        [(0, half, 2, 0, 1), (half, half, 1, 1, 1)],
        [(0, half, -1, 1, 1), (half, half, 1, 1, 0)],
        [(0, half, 2, 1, 0)],
        [(0, half, 2, 1, 1)],
    ]
    return [block, behind, ahead, side] + late, other, spans, *meanwhile


def spread_ring(block, axis):
    half = block.shape[0] // 2
    before, after = ring(block, axis, 1), ring(block, axis, -1)
    return jnp.concatenate(
        [block, before, after, ring(before[:half], axis, 1), ring(after[half:], axis, -1)]
    )


def collect_ring(mine, other, axis):
    half = mine.shape[1] // 2
    low, wide = jnp.bfloat16, jnp.float32
    far = mine[3].astype(wide) + swap(other[3]).astype(wide)
    rest = swap(other[:3])
    one = ring(far[:half].astype(low), axis, -1)
    two = ring(far[half:].astype(low), axis, 1)
    behind = mine[1].astype(wide) + rest[1].astype(wide)
    ahead = mine[2].astype(wide) + rest[2].astype(wide)
    behind = jnp.concatenate([behind[:half] + one.astype(wide), behind[half:]])
    ahead = jnp.concatenate([ahead[:half], ahead[half:] + two.astype(wide)])
    from_ahead = ring(behind.astype(low), axis, -1)
    from_back = ring(ahead.astype(low), axis, 1)
    return [mine, rest, from_ahead, from_back], (one, two)


def after(value, *others):
    return lax.optimization_barrier((value,) + others)[0]


def packed(rows, width):
    high = rows.astype(jnp.bfloat16)
    rest = (rows - high.astype(jnp.float32)).astype(jnp.bfloat16)
    return high.reshape(-1, width), rest.reshape(-1, width)


def padded(rows, multiple):
    return jnp.pad(rows, ((0, -rows.shape[0] % multiple), (0, 0)))


ANYWHERE = pl.BlockSpec(memory_space=pl.ANY)
SCALARS = pl.BlockSpec(memory_space=pltpu.SMEM)
INSIDE = pl.BlockSpec(memory_space=pltpu.VMEM)
ROOM = pltpu.CompilerParams(vmem_limit_bytes=56 * 2**20)


def project_kernel(spans, offsets_ref, rows_ref, *refs):
    count = len(refs) - 8
    pieces, (out_ref, *whole_refs) = refs[:count], refs[count : count + 3]
    held, page, in_sem, out_sems, page_sem = refs[count + 3 :]
    for i, (which, first, rows) in enumerate(spans):
        offset = pl.multiple_of(offsets_ref[i], rows)
        pltpu.make_async_copy(
            pieces[which].at[pl.ds(first, rows)], held.at[pl.ds(offset, rows)], in_sem
        ).start()
    pltpu.make_async_copy(held, held, in_sem).wait()
    stores, column = [], 0
    for j, whole in enumerate(whole_refs):
        width = whole.shape[1]
        stores.append(
            pltpu.make_async_copy(held.at[:, pl.ds(column, width)], whole, out_sems.at[j])
        )
        stores[-1].start()
        column += width
    step = 512
    for column in range(0, out_ref.shape[1], step):
        cut = pl.ds(column, step)
        page[:, cut] = jnp.dot(rows_ref[...], held[:, cut], preferred_element_type=jnp.float32)
        pltpu.make_async_copy(page.at[:, cut], out_ref.at[:, cut], page_sem).start()
    pltpu.make_async_copy(page, out_ref, page_sem).wait()
    for store in stores:
        store.wait()


def project(rows, gathered, widths):
    core = lax.axis_index("dp") % 2
    place, side = place_of("fsdp")
    mine, other, pieces = gathered
    block = mine[0].shape[0]
    spans, offsets = [], []
    for who in range(2):
        for at, cuts in enumerate(pieces):
            for first, count, step, across, half in cuts:
                owner = (side ^ across) * RING + (place + step) % RING
                spans.append((who * len(pieces) + at, first, count))
                offsets.append((owner * 2 + (core ^ who)) * block + (half or 0) * count)
    depth = 2 * block * 2 * RING
    kind = mine[0].dtype
    return pl.pallas_call(
        functools.partial(project_kernel, spans),
        out_shape=[jax.ShapeDtypeStruct((rows.shape[0], widths[0]), jnp.float32)]
        + [jax.ShapeDtypeStruct((depth, width), kind) for width in widths],
        in_specs=[SCALARS, INSIDE] + [ANYWHERE] * (len(mine) + len(other)),
        out_specs=[ANYWHERE] * (1 + len(widths)),
        compiler_params=ROOM,
        scratch_shapes=[
            pltpu.VMEM((depth, sum(widths)), kind),
            pltpu.VMEM((rows.shape[0], widths[0]), jnp.float32),
            pltpu.SemaphoreType.DMA,
            pltpu.SemaphoreType.DMA((len(widths),)),
            pltpu.SemaphoreType.DMA,
        ],
    )(jnp.stack(offsets).astype(jnp.int32), rows, *mine, *other)


def pick_kernel(table_ref, conv_ref, feed_ref, mine_ref, other_ref, held, sem):
    slots, side = mine_ref.shape[0], mine_ref.shape[1]
    half = side // 2
    held[...] = jnp.zeros_like(held)

    def one(i, finish):
        at = 5 * i
        kind, piece = table_ref[at], table_ref[at + 1]
        first = pl.multiple_of(table_ref[at + 4] * half, half)

        def move(source, target):
            copy = pltpu.make_async_copy(source, target, sem)
            if finish:
                copy.wait()
            else:
                copy.start()

        def column(k):
            return pl.ds(pl.multiple_of(k * side, side), side)

        @pl.when(kind == 1)
        def _():
            move(
                conv_ref.at[piece, pl.ds(0, half), column(table_ref[at + 2])],
                held.at[0, i, pl.ds(first, half), :],
            )

        for which in range(2):

            @pl.when((kind == 2) & (table_ref[at + 2 + which] >= 0))
            def _():
                move(feed_ref.at[piece + which, :, column(table_ref[at + 2 + which])], held.at[which, i])

    for finish in (False, True):

        def step(i, carry):
            one(i, finish)
            return carry

        lax.fori_loop(0, 2 * slots, step, 0)
    for q in range(slots):
        mine_ref[q] = held[0, q].astype(jnp.float32) + held[1, q].astype(jnp.float32)
        other_ref[q] = held[0, slots + q]


def pick(table, conv, feed, slots, side):
    shape = (slots, side, side)
    return pl.pallas_call(
        pick_kernel,
        out_shape=[jax.ShapeDtypeStruct(shape, jnp.float32), jax.ShapeDtypeStruct(shape, conv.dtype)],
        in_specs=[SCALARS, ANYWHERE, ANYWHERE],
        out_specs=[INSIDE, INSIDE],
        compiler_params=ROOM,
        scratch_shapes=[
            pltpu.VMEM((2, 2 * slots, side, side), conv.dtype),
            pltpu.SemaphoreType.DMA,
        ],
    )(table, conv, feed)


def add_kernel(own_ref, ahead_ref, behind_ref, extra_ref, out_ref):
    width = out_ref.shape[2]
    parts = own_ref.shape[1] // width
    rows = out_ref.shape[1] - extra_ref.shape[1]
    blocks = out_ref.shape[0] // parts
    for i in range(blocks):
        cut = pl.ds(i * rows, rows)
        total = own_ref[cut, :] + ahead_ref[cut, :].astype(jnp.float32)
        total = (total + behind_ref[cut, :].astype(jnp.float32)).astype(out_ref.dtype)
        for k in range(parts):
            out_ref[k * blocks + i, :rows, :] = total[:, k * width : (k + 1) * width]
            out_ref[k * blocks + i, rows:, :] = extra_ref[k]


def add_terms(own, ahead, behind, extra, blocks):
    parts = extra.shape[0]
    rows, width = own.shape[0] // blocks + extra.shape[1], own.shape[1] // parts
    return pl.pallas_call(
        add_kernel,
        out_shape=jax.ShapeDtypeStruct((parts * blocks, rows, width), ahead.dtype),
        in_specs=[INSIDE] * 4,
        out_specs=INSIDE,
        compiler_params=ROOM,
        cost_estimate=pl.CostEstimate(
            flops=50 * 10**9, bytes_accessed=own.size * 8, transcendentals=0
        ),
    )(own, ahead, behind, extra)


def put_kernel(at_ref, mine_ref, other_ref, *refs):
    count = (len(refs) - 3) // 2
    outs, pages = refs[:count], refs[count : 2 * count]
    held, in_sems, out_sems = refs[-3:]
    count_held, side = mine_ref.shape[0], mine_ref.shape[1]
    loads = [
        pltpu.make_async_copy(source, held.at[pl.ds(i * count_held, count_held)], in_sems.at[i])
        for i, source in enumerate((mine_ref, other_ref))
    ]
    for load in loads:
        load.start()
    for load in loads:
        load.wait()
    tile = 0
    for j in range(count):
        for k in range(outs[j].shape[1] // side):
            pages[j][:, k * side : (k + 1) * side] = held[at_ref[tile]]
            tile += 1
        pltpu.make_async_copy(pages[j], outs[j], out_sems.at[j]).start()
    for j in range(count):
        pltpu.make_async_copy(pages[j], outs[j], out_sems.at[j]).wait()


def put(core, slot_index, mine, other, widths):
    chips, slots, side, _ = mine.shape
    owner = slot_index // slots
    at = ((owner % 2 ^ core) * chips + owner // 2) * slots + slot_index % slots
    flat = (chips * slots, side, side)
    return pl.pallas_call(
        put_kernel,
        out_shape=[jax.ShapeDtypeStruct((side, width), mine.dtype) for width in widths],
        in_specs=[SCALARS, ANYWHERE, ANYWHERE],
        out_specs=[ANYWHERE] * len(widths),
        compiler_params=ROOM,
        scratch_shapes=[pltpu.VMEM((side, width), mine.dtype) for width in widths]
        + [
            pltpu.VMEM((2 * chips * slots, side, side), mine.dtype),
            pltpu.SemaphoreType.DMA((2,)),
            pltpu.SemaphoreType.DMA((len(widths),)),
        ],
    )(at.astype(jnp.int32), mine.reshape(flat), other.reshape(flat))


def feed_kernel(order_ref, fed_ref, dy_ref, w_ref, *refs):
    both_ref, act_ref, back_ref = refs[-3:]
    width = act_ref.shape[-1]
    mixed = jnp.dot(fed_ref[0], w_ref[:, : 2 * width], preferred_element_type=jnp.float32)
    grad_act = jnp.dot(dy_ref[0], w_ref[:, 2 * width :], preferred_element_type=jnp.float32)
    gate, up = mixed[:, :width], mixed[:, width:]
    sigmoid = jax.nn.sigmoid(gate)
    passed = gate * sigmoid
    activation = (passed * up).astype(jnp.bfloat16)
    grad_gate = grad_act * up * sigmoid * (1.0 + gate * (1.0 - sigmoid))
    grad_up = grad_act * passed
    both = jnp.concatenate([grad_gate.astype(jnp.bfloat16), grad_up.astype(jnp.bfloat16)], axis=1)
    both_ref[0] = both
    act_ref[0] = activation
    back_ref[0] = back_dot(both, w_ref[:, : 2 * width]).astype(jnp.bfloat16)


def feed_forward(order, fed, grad_feed, weights, first, begun):
    blocks, rows, model_width = fed.shape
    width = weights.shape[1] // 3
    begun = list(begun)

    def turned(i, order_ref):
        return (order_ref[first + i], 0, 0)

    def shape(count, columns):
        return jax.ShapeDtypeStruct((count, rows, columns), jnp.bfloat16)

    whole = grad_feed.shape[0]

    return pl.pallas_call(
        feed_kernel,
        grid_spec=pltpu.PrefetchScalarGridSpec(
            num_scalar_prefetch=1,
            grid=(blocks,),
            in_specs=[
                pl.BlockSpec((1, rows, model_width), lambda i, order_ref: (i, 0, 0)),
                pl.BlockSpec((1, rows, model_width), turned),
                pl.BlockSpec(weights.shape, lambda i, order_ref: (0, 0)),
            ]
            + [ANYWHERE] * len(begun),
            out_specs=[
                pl.BlockSpec((1, rows, 2 * width), lambda i, order_ref: (first + i, 0, 0)),
                pl.BlockSpec((1, rows, width), turned),
                pl.BlockSpec((1, rows, model_width), lambda i, order_ref: (i, 0, 0)),
            ],
        ),
        out_shape=[
            shape(whole, 2 * width),
            shape(whole, width),
            shape(blocks, model_width),
        ],
        input_output_aliases={4 + i: i for i in range(len(begun))},
        compiler_params=ROOM,
        cost_estimate=pl.CostEstimate(
            flops=2 * blocks * rows * model_width * width * 5,
            bytes_accessed=blocks * rows * (4 * model_width + 3 * width) * 2,
            transcendentals=blocks * rows * width,
        ),
    )(order, fed, grad_feed, weights, *begun)


def turn_kernel(
    own_ref, other_ref, ahead_ref, behind_ref, values_ref, scale_ref, gain_ref, seed_ref, w_ref, part_ref, conv_ref,
    resid_out, branch_out, part_out, conv_out, gain_out,
):
    wide = jnp.float32
    grads = own_ref[0].astype(wide) + other_ref[0].astype(wide)
    grads = grads + ahead_ref[...].astype(wide) + behind_ref[...].astype(wide)
    values, scale = values_ref[...], scale_ref[...]
    weighted = grads * gain_ref[...]
    inner = jnp.mean(values * weighted, axis=-1, keepdims=True)
    resid = seed_ref[...] + scale * weighted - values * (scale * scale * scale * inner)
    gain_out[0] = jnp.sum(values * scale * grads, axis=0, keepdims=True)
    resid_out[...] = resid
    branch = resid.astype(branch_out.dtype)
    branch_out[...] = branch
    gated = back_dot(branch, w_ref[...])
    part_out[...] = (gated * conv_ref[...]).astype(part_out.dtype)
    conv_out[...] = gated * part_ref[...]


def turn_back(terms, values, scale, gain, seed, weights, mixed, convolved, steps):
    rows, width = values.shape
    cut = rows // steps

    def tokens(i):
        return (i, 0)

    block = pl.BlockSpec((cut, width), tokens)
    first = pl.BlockSpec((1, cut, width), lambda i: (0, i, 0))
    wide, low = jnp.float32, jnp.bfloat16
    *results, gains = pl.pallas_call(
        turn_kernel,
        grid=(steps,),
        out_shape=[jax.ShapeDtypeStruct((rows, width), kind) for kind in (wide, low, low, wide)]
        + [jax.ShapeDtypeStruct((steps, 1, width), wide)],
        in_specs=[
            first,
            first,
            block,
            block,
            block,
            pl.BlockSpec((cut, 1), tokens),
            pl.BlockSpec((1, width), lambda i: (0, 0)),
            block,
            pl.BlockSpec(weights.shape, lambda i: (0, 0)),
            pl.BlockSpec((cut, width), lambda i: (i, 1)),
            block,
        ],
        out_specs=[block] * 4 + [pl.BlockSpec((1, 1, width), lambda i: (i, 0, 0))],
        compiler_params=ROOM,
    )(*terms, values, scale, gain[None], seed, weights, mixed, convolved)
    return (*results, jnp.sum(gains, axis=(0, 1)))


def rms_factor(values):
    return lax.rsqrt(jnp.mean(values * values, axis=-1, keepdims=True) + EPS_NORM)


def norm_back(values, scale_val, gain_row, grad_out):
    weighted = grad_out * gain_row
    inner = jnp.mean(values * weighted, axis=-1, keepdims=True)
    grad_values = scale_val * weighted - values * scale_val * scale_val * scale_val * inner
    grad_gain = jnp.sum(values * scale_val * grad_out, axis=0)
    return (grad_values, grad_gain)


def outer_sum(left_arr, right_arr):
    return lax.dot_general(left_arr, right_arr, TOKEN_DIMS, preferred_element_type=jnp.float32)


def back_dot(left_arr, right_arr):
    return lax.dot_general(left_arr, right_arr, BACK_DIMS, preferred_element_type=jnp.float32)


def exchange(value, axis, groups=None):
    return lax.all_to_all(value, axis, 0, 0, axis_index_groups=groups)


def column_halves(value, parts, core):
    cut = value.reshape(value.shape[0], parts, 2, -1)
    mine = lax.dynamic_index_in_dim(cut, core, 2, keepdims=False).reshape(value.shape[0], -1)
    other = lax.dynamic_index_in_dim(cut, 1 - core, 2, keepdims=False).reshape(value.shape[0], -1)
    return jnp.concatenate([mine, swap(other)])


def slot_table(owner_row, per_owner):
    tile_count = owner_row.shape[0]
    same_owner = owner_row[None, :] == owner_row[:, None]
    before = (
        jnp.arange(tile_count, dtype=jnp.int32)[None, :]
        < jnp.arange(tile_count, dtype=jnp.int32)[:, None]
    )
    slot_rank = jnp.sum((same_owner & before).astype(jnp.int32), axis=1)
    return owner_row * per_owner + slot_rank


def split_dot(left, right, dims, axis):
    def cut(value):
        high = value.astype(jnp.bfloat16)
        rest = value - high.astype(jnp.float32)
        middle = rest.astype(jnp.bfloat16)
        return high, middle, (rest - middle.astype(jnp.float32)).astype(jnp.bfloat16)

    left_cut, right_cut = cut(left), cut(right)
    pairs = ((0, 0), (0, 1), (1, 0), (1, 1), (0, 2), (2, 0))
    return lax.dot_general(
        jnp.concatenate([left_cut[i] for i, _ in pairs], axis[0]),
        jnp.concatenate([right_cut[j] for _, j in pairs], axis[1]),
        dims,
        preferred_element_type=jnp.float32,
    )


def bases_kernel(grad_ref, stats_ref, bases_ref, stats_out, q_ref, m_ref, w_ref):
    tiles, side = grad_ref.shape[0], grad_ref.shape[1]
    count = 2 * tiles
    for i in range(tiles):
        grad = grad_ref[i]
        for j, dims in enumerate((BACK_DIMS, TOKEN_DIMS)):
            axis = 1 - j
            square = near_dot(grad, grad, dims, (axis, axis))
            stats_out[i, j] = BETA_STAT * stats_ref[i, j] + (1.0 - BETA_STAT) * square
    for g in range(count):
        m_ref[g] = split_dot(stats_out[g // 2, g % 2], bases_ref[g // 2, g % 2], PLAIN_DIMS, (1, 0))
    row = lax.broadcasted_iota(jnp.int32, (8, side), 0)
    lane = lax.broadcasted_iota(jnp.int32, (8, side), 1)
    rows = lax.broadcasted_iota(jnp.int32, (PANEL, side), 0)
    lanes = lax.broadcasted_iota(jnp.int32, (PANEL, side), 1)
    all_rows = lax.broadcasted_iota(jnp.int32, (side, side), 0)
    all_lanes = lax.broadcasted_iota(jnp.int32, (side, side), 1)
    for g in range(count):
        w_ref[g] = split_dot(m_ref[g], m_ref[g], TOKEN_DIMS, (0, 0))
    for base in range(0, side, PANEL):
        end = base + PANEL
        panels = [[w_ref[g, i : i + 8, :] for i in range(base, end, 8)] for g in range(count)]
        for k in range(PANEL):
            at, inside = k // 8, k % 8
            hit = lane == base + k
            for g in range(count):
                panel = panels[g]
                column = jnp.broadcast_to(panel[at][:, base + k : base + k + 1], (8, side))
                scale = lax.rsqrt(jnp.broadcast_to(column[inside : inside + 1], (8, side)))
                top = jnp.broadcast_to(panel[at][inside : inside + 1], (8, side))
                top = jnp.where(hit, scale, top * scale)
                part = jnp.where(hit, 0.0, panel[at]) - column * scale * top
                panel[at] = jnp.where(row > inside, part, jnp.where(row == inside, top, panel[at]))
                for i in range(at + 1, PANEL // 8):
                    column = jnp.broadcast_to(panel[i][:, base + k : base + k + 1], (8, side))
                    panel[i] = jnp.where(hit, 0.0, panel[i]) - column * scale * top
        for g in range(count):
            done = jnp.concatenate(panels[g], axis=0)
            w_ref[g, base:end, :] = done
            if end < side:
                upper = (lanes >= base) & (lanes < end) & (lanes - base > rows)
                change = split_dot(done, jnp.where(upper, 0.0, done), TOKEN_DIMS, (0, 0))[end:]
                gone = (all_lanes[end:] >= base) & (all_lanes[end:] < end)
                w_ref[g, end:, :] = jnp.where(gone, 0.0, w_ref[g, end:, :]) - change
    for g in range(count):
        inverse = jnp.where(all_lanes <= all_rows, w_ref[g], 0.0)
        q_ref[g // 2, g % 2] = split_dot(m_ref[g], inverse, BACK_DIMS, (1, 1))


def near_dot(left, right, dims, axis):
    def cut(value):
        high = value.astype(jnp.bfloat16)
        return high, (value - high.astype(jnp.float32)).astype(jnp.bfloat16)

    (left_high, left_rest), (right_high, right_rest) = cut(left), cut(right)
    left_axis, right_axis = axis
    return lax.dot_general(
        jnp.concatenate([left_high, left_high, left_rest], left_axis),
        jnp.concatenate([right_high, right_rest, right_high], right_axis),
        dims,
        preferred_element_type=jnp.float32,
    )


def soap_kernel(
    mine_ref, other_ref, master_ref, first_ref, second_ref, bases_ref,
    grad_ref, master_out, first_out, second_out, low_out,
):
    count, side = mine_ref.shape[0], mine_ref.shape[1]
    for i in range(count):
        grad = mine_ref[i] + other_ref[i].astype(jnp.float32)
        first = BETA_ONE * first_ref[i] + (1.0 - BETA_ONE) * grad
        grad_ref[i] = grad
        first_out[i] = first
    turned = []
    for i in range(count):
        pair_rows = jnp.concatenate([grad_ref[i], first_out[i]], axis=1)
        turned.append(near_dot(bases_ref[i, 0], pair_rows, TOKEN_DIMS, (0, 0)))
    for i in range(count):
        stacked = jnp.concatenate([turned[i][:, :side], turned[i][:, side:]], axis=0)
        both = near_dot(stacked, bases_ref[i, 1], PLAIN_DIMS, (1, 0))
        rotated, moment = both[:side], both[side:]
        second = BETA_TWO * second_ref[i] + (1.0 - BETA_TWO) * rotated * rotated
        second_out[i] = second
        turned[i] = (
            moment
            / (1.0 - BETA_ONE**STEP)
            / (jnp.sqrt(second / (1.0 - BETA_TWO**STEP)) + EPS_ADAM)
        )
    for i in range(count):
        turned[i] = near_dot(bases_ref[i, 0], turned[i], PLAIN_DIMS, (1, 0))
    for i in range(count):
        step = near_dot(turned[i], bases_ref[i, 1], BACK_DIMS, (1, 1))
        master = master_ref[i] - RATE_MATRIX * (step + DECAY_WEIGHT * master_ref[i])
        master_out[i] = master
        for j in range(low_out.shape[0]):
            low_out[j, i] = master.astype(low_out.dtype)


def soap_update(mine, other, master, first, second, bases, copies):
    tiles = jax.ShapeDtypeStruct(mine.shape, jnp.float32)
    return pl.pallas_call(
        soap_kernel,
        out_shape=[tiles] * 4 + [jax.ShapeDtypeStruct((copies,) + mine.shape, jnp.bfloat16)],
        in_specs=[INSIDE] * 6,
        out_specs=[INSIDE] * 5,
        compiler_params=ROOM,
    )(mine, other, master, first, second, bases)


def bases_update(grad_tiles, stats, bases):
    tiles, _, side, _ = bases.shape
    whole = jax.ShapeDtypeStruct(bases.shape, jnp.float32)
    return pl.pallas_call(
        bases_kernel,
        out_shape=[whole, whole],
        in_specs=[INSIDE] * 3,
        out_specs=[INSIDE] * 2,
        scratch_shapes=[pltpu.VMEM((2 * tiles, side, side), jnp.float32) for _ in range(2)],
        compiler_params=ROOM,
        cost_estimate=pl.CostEstimate(
            flops=30 * 10**9, bytes_accessed=20 * bases.size, transcendentals=0
        ),
    )(grad_tiles, stats, bases)


def shards(
    block_in,
    cotangent,
    lengths,
    vector_params,
    vector_first,
    vector_second,
    w_in,
    w_out,
    w_gate,
    w_up,
    w_down,
    tile_owner,
    tile_master,
    tile_first,
    tile_second,
    tile_stats,
    tile_bases,
):
    micro_count, _, tok_count, model_width = block_in.shape
    hidden_width = w_gate.shape[1]
    shard_rows = w_in.shape[0]
    half_rows = shard_rows // 2
    parts = lax.axis_size("fsdp")
    owners = lax.axis_size("dp")
    chips = owners // 2
    owner_id = lax.axis_index("dp")
    core = owner_id % 2
    place, far = place_of("dp")
    chip_group = [list(range(i, i + 2 * RING)) for i in range(0, owners, 2 * RING)]
    same_core = [[2 * i + c for i in range(chips)] for c in range(2)]
    same_ring_place = [
        [(h * 2 * RING + i) * parts + f for h in range(owners // (2 * RING)) for f in range(parts)]
        for i in range(2 * RING)
    ]
    tile_side = tile_master.shape[-1]
    per_owner = tile_master.shape[1]
    tile_count = tile_owner.shape[1]
    g_one, g_two, k_zero, k_one, k_two = [vector_params[i] for i in range(5)]

    def half_of(matrix):
        return lax.dynamic_slice(matrix, (core * half_rows, 0), (half_rows, matrix.shape[1]))

    conv_block = jnp.concatenate([half_of(w_in), half_of(w_out)], axis=1)
    positions = lax.axis_index("fsdp") * tok_count + jnp.arange(tok_count, dtype=jnp.int32)
    live_mask = (positions[None, :] < lengths).astype(jnp.float32)[:, :, None]
    seed_grad = (cotangent[:, 0] * live_mask).reshape(-1, model_width)
    grad_feed = lax.all_gather(
        seed_grad.astype(jnp.bfloat16), "dp", axis_index_groups=chip_group, axis=0
    )
    hidden = hidden_width // RING // 2
    wide = -(-hidden // tile_side) * tile_side
    shift = 2 * hidden - wide
    columns = jnp.arange(wide, dtype=jnp.int32)
    kept = (columns >= core * (wide - hidden)) & (columns < hidden + core * (wide - hidden))

    def slice_of(matrix):
        first = place * (2 * hidden) + core * shift
        return jnp.where(
            kept[None, :], lax.dynamic_slice(matrix, (0, first), (shard_rows, wide)), jnp.zeros((), matrix.dtype)
        )

    feed_block = jnp.concatenate([slice_of(matrix) for matrix in (w_gate, w_up, w_down)], axis=1)
    token_rows = block_in.astype(jnp.float32).reshape(-1, model_width)
    scale_one = rms_factor(token_rows)
    normed = (token_rows * scale_one * g_one).astype(jnp.bfloat16)
    *conv_pieces, normed, feed_block = spread(conv_block, "fsdp", (normed, feed_block))
    feed_weights = lax.all_gather(
        after(feed_block, *conv_pieces[0][4:]), "fsdp", axis=0, tiled=True
    )

    mixed_all, whole_in, whole_out = project(normed, conv_pieces, (3 * model_width, model_width))
    part_b = mixed_all[:, :model_width]
    part_c = mixed_all[:, model_width : 2 * model_width]
    part_x = mixed_all[:, 2 * model_width :]
    product = (part_b * part_x).reshape(micro_count, tok_count, model_width)
    extended = jnp.concatenate([from_behind(product[:, -2:], "fsdp", 1), product], axis=1)
    convolved = (
        k_zero * extended[:, :-2] + k_one * extended[:, 1:-1] + k_two * extended[:, 2:]
    ).reshape(-1, model_width)
    gated_conv = (part_c * convolved).astype(jnp.bfloat16)
    residual = token_rows + jnp.dot(gated_conv, whole_out, preferred_element_type=jnp.float32)
    scale_two = rms_factor(residual)
    normed_two = (residual * scale_two * g_two).astype(jnp.bfloat16)

    fed = spread_ring(normed_two, "dp")
    fed, normed_halves, gated_halves = lax.optimization_barrier(
        (fed, column_halves(normed, parts, core), column_halves(gated_conv, parts, core))
    )
    steps = jnp.array([0, RING - 1, 1, 2], dtype=jnp.int32)
    ring_places = (place + steps) % RING * 2
    order = jnp.concatenate([ring_places + core, ring_places + 1 - core]).astype(jnp.int32)
    fed_other = swap(fed)
    begun, back_parts = (), []
    for who, rows in enumerate((fed, fed_other)):
        *begun, back = feed_forward(
            order, rows.reshape(RING, -1, model_width), grad_feed, feed_weights, who * RING, begun
        )
        back_parts.append(back)
    grad_both, activation = begun
    grad_terms, far_parts = collect_ring(*back_parts, "dp")
    grad_both, far_parts = lax.optimization_barrier((grad_both, far_parts))
    fed = jnp.concatenate([fed, fed_other])
    low = jnp.bfloat16
    feed_sums = jnp.concatenate(
        [
            outer_sum(fed, grad_both.reshape(-1, 2 * wide)).astype(low),
            outer_sum(grad_feed.reshape(-1, model_width), activation.reshape(-1, wide)).astype(low),
        ],
        axis=1,
    )
    *grad_terms, feed_sums = lax.optimization_barrier((*grad_terms, feed_sums))
    feed_rows = lax.psum_scatter(feed_sums, "fsdp", scatter_dimension=0, tiled=True)

    grad_resid, grad_branch, grad_part_c, grad_conv, grad_gain_two = turn_back(
        grad_terms, residual, scale_two, g_two, seed_grad, whole_out, mixed_all, convolved, micro_count
    )
    grad_conv = grad_conv.reshape(micro_count, tok_count, model_width)
    grad_ext = jnp.concatenate([grad_conv, from_behind(grad_conv[:, :2], "fsdp", -1)], axis=1)
    grad_product = (
        k_two * grad_conv + k_one * grad_ext[:, 1 : tok_count + 1] + k_zero * grad_ext[:, 2:]
    ).reshape(-1, model_width)
    grad_kernel = jnp.stack(
        [
            jnp.sum(grad_conv * extended[:, :-2], axis=(0, 1)),
            jnp.sum(grad_conv * extended[:, 1:-1], axis=(0, 1)),
            jnp.sum(grad_conv * extended[:, 2:], axis=(0, 1)),
        ]
    )
    grad_all = jnp.concatenate(
        [
            (grad_product * part_x).astype(low),
            grad_part_c,
            (grad_product * part_b).astype(low),
            grad_branch,
        ],
        axis=1,
    )
    grad_mixed = grad_all[:, : 3 * model_width]

    def conv_block(step, grads):
        index = (place + step) % RING
        right = [
            lax.dynamic_slice(part, (0, index * model_width), (part.shape[0], model_width)) for part in grads
        ]
        left = jnp.where(index == RING - 1, gated_halves, normed_halves)
        return outer_sum(left, jnp.concatenate(right))

    grads = (grad_all, swap(grad_all))
    conv_far = conv_block(2, grads).astype(low)
    middle = conv_far.shape[0] // 2
    one, two = ring(conv_far[:middle], "dp", -1), ring(conv_far[middle:], "dp", 1)
    *grads, _ = lax.optimization_barrier((*grads, conv_far))
    behind, ahead = conv_block(-1, grads), conv_block(1, grads)
    one, two = one.astype(jnp.float32), two.astype(jnp.float32)
    behind = (behind + jnp.concatenate([one, jnp.zeros_like(one)])).astype(low)
    ahead = (ahead + jnp.concatenate([jnp.zeros_like(two), two])).astype(low)
    conv_sums = conv_block(0, grads)
    conv_cols = [conv_sums, ring(behind, "dp", -1), ring(ahead, "dp", 1)]

    grad_normed = back_dot(after(grad_mixed, behind, ahead), whole_in)
    grad_rows_norm, grad_gain_one = norm_back(token_rows, scale_one, g_one, grad_normed)
    vector_grads = jnp.concatenate([grad_gain_one[None], grad_gain_two[None], grad_kernel], axis=0)
    vector_rows = vector_grads.shape[0]
    feed_rows = after(feed_rows, behind, ahead)
    feed_rows = feed_rows.astype(jnp.float32) + pair(feed_rows, "dp").astype(jnp.float32)
    feed_tiles = lax.all_gather(feed_rows.astype(low), "dp", axis_index_groups=chip_group, axis=0)
    block_width = model_width // (chips // RING)
    extra = jnp.stack([padded(rows, 16) for rows in packed(vector_grads, block_width)])
    conv_cols = add_terms(*conv_cols, extra, parts)
    conv_own = exchange(conv_cols, ("dp", "fsdp"), same_ring_place)
    conv_own = jnp.sum(conv_own.astype(jnp.float32), axis=0)
    packed_rows = vector_rows * (model_width // block_width)
    vector_part = jnp.concatenate(packed(conv_own[half_rows : half_rows + packed_rows], block_width))
    conv_own = jnp.concatenate([conv_own[:half_rows].astype(low), padded(vector_part, 32)])
    conv_tiles = exchange(jnp.broadcast_to(conv_own, (chips,) + conv_own.shape), "dp", same_core)
    vector_part = jnp.sum(
        conv_tiles[:, half_rows : half_rows + 2 * packed_rows].astype(jnp.float32), axis=0
    ).reshape(2 * vector_rows, model_width)
    vector_grads = vector_part[:vector_rows] + vector_part[vector_rows:]
    vector_grads = vector_grads + swap(vector_grads)
    out_parts = back_dot(
        after(activation, conv_cols).reshape(-1, wide), feed_weights[:, 2 * wide :]
    ).astype(low).reshape(grad_feed.shape)
    feed_out = lax.psum_scatter(
        after(out_parts, conv_own), "dp", scatter_dimension=0, axis_index_groups=chip_group
    )

    slot_index = slot_table(tile_owner[0], per_owner)
    slot_match = slot_index[None, :] == jnp.arange(per_owner * owners, dtype=jnp.int32)[:, None]
    tile_of_slot = (
        jnp.sum(
            jnp.where(slot_match, jnp.arange(1, tile_count + 1, dtype=jnp.int32)[None, :], 0), axis=1
        )
        - 1
    )
    wanted = jnp.concatenate(
        [
            lax.dynamic_slice(tile_of_slot, (owner_id * per_owner,), (per_owner,)),
            lax.dynamic_slice(tile_of_slot, ((owner_id ^ 1) * per_owner,), (per_owner,)),
        ]
    )
    conv_count = 4 * model_width // tile_side
    each_conv, each_feed = conv_count // chips, 2 * hidden // tile_side
    parts_far = chips // RING
    feed_tile = wanted - conv_count
    within = feed_tile % each_feed
    feed_first = feed_tile // (each_feed * RING) * (wide // tile_side)
    is_conv = wanted < conv_count
    own_slot = jnp.arange(2 * per_owner) < per_owner
    left, right = within < wide // tile_side, within >= shift // tile_side
    table = jnp.stack(
        [
            jnp.where(is_conv, 1, jnp.where(own_slot, 2, 0)),
            jnp.where(
                is_conv,
                wanted // each_conv % parts_far * RING + wanted // each_conv // parts_far,
                feed_tile // each_feed % RING * 2,
            ),
            jnp.where(is_conv, wanted % each_conv, jnp.where(left, feed_first + within, -1)),
            jnp.where(right, feed_first + within - shift // tile_side, -1),
            jnp.where(is_conv, core, 0),
        ],
        axis=1,
    )
    table = jnp.where(wanted[:, None] < 0, 0, table).astype(jnp.int32).reshape(-1)
    mine, other = pick(table, conv_tiles, feed_tiles, per_owner, tile_side)
    owned_grads, master_new, first_new, second_new, master_low = soap_update(
        mine, swap(other), tile_master[0], tile_first[0], tile_second[0], tile_bases[0], chips
    )
    masters = exchange(master_low, "dp", same_core)
    stats_new, bases_new = bases_update(owned_grads, tile_stats[0], tile_bases[0])
    bases_new, feed_out, vector_grads, grad_resid = lax.optimization_barrier(
        (bases_new, feed_out, vector_grads, grad_resid)
    )
    result_rows = residual + feed_out.astype(jnp.float32)
    grad_rows = grad_resid + grad_rows_norm
    vec_first = BETA_ONE * vector_first + (1.0 - BETA_ONE) * vector_grads
    vec_second = BETA_TWO * vector_second + (1.0 - BETA_TWO) * vector_grads * vector_grads
    vec_new = vector_params - RATE_VECTOR * (vec_first / (1.0 - BETA_ONE**STEP)) / (
        jnp.sqrt(vec_second / (1.0 - BETA_TWO**STEP)) + EPS_ADAM
    )
    masters, bases_new, stats_new, result_rows, grad_rows, vec_new, vec_first, vec_second = (
        lax.optimization_barrier(
            (masters, bases_new, stats_new, result_rows, grad_rows, vec_new, vec_first, vec_second)
        )
    )
    widths = (3 * model_width, model_width, hidden_width, hidden_width, hidden_width)
    w_in_new, w_out_new, w_gate_new, w_up_new, w_down_new = put(
        core, slot_index, masters, swap(masters), widths
    )
    whole_shape = (micro_count, 1, tok_count, model_width)
    return (
        result_rows.reshape(whole_shape),
        grad_rows.reshape(whole_shape),
        vec_new,
        vec_first,
        vec_second,
        w_in_new,
        w_out_new,
        w_gate_new,
        w_up_new,
        w_down_new,
        master_new[None],
        first_new[None],
        second_new[None],
        stats_new[None],
        bases_new[None],
    )


def solution(mesh):
    return jax.shard_map(
        shards,
        mesh=mesh,
        in_specs=(
            P(None, "dp", "fsdp", None),
            P(None, "dp", "fsdp", None),
            P(None, "dp"),
            P(),
            P(),
            P(),
            P("fsdp", None),
            P("fsdp", None),
            P("fsdp", None),
            P("fsdp", None),
            P("fsdp", None),
            P("fsdp", None),
            P("fsdp", "dp", None, None),
            P("fsdp", "dp", None, None),
            P("fsdp", "dp", None, None),
            P("fsdp", "dp", None, None, None),
            P("fsdp", "dp", None, None, None),
        ),
        out_specs=(
            P(None, "dp", "fsdp", None),
            P(None, "dp", "fsdp", None),
            P(),
            P(),
            P(),
            P("fsdp", None),
            P("fsdp", None),
            P("fsdp", None),
            P("fsdp", None),
            P("fsdp", None),
            P("fsdp", "dp", None, None),
            P("fsdp", "dp", None, None),
            P("fsdp", "dp", None, None),
            P("fsdp", "dp", None, None, None),
            P("fsdp", "dp", None, None, None),
        ),
        check_vma=False,
    )
```

```python
import functools

import jax
import jax.numpy as jnp
from jax import lax
from jax.experimental import pallas as pl
from jax.experimental.pallas import tpu as pltpu
from jax.sharding import PartitionSpec as P

STEP = 10


EPS_NORM = 1e-05
EPS_ADAM = 1e-08
BETA_ONE = 0.5
BETA_TWO = 0.5
BETA_STAT = 0.5
RATE_MATRIX = 0.03
RATE_VECTOR = 0.2
DECAY_WEIGHT = 0.01
PRECISE = lax.Precision.HIGHEST
BACK_DIMS = (((1,), (1,)), ((), ()))
TOKEN_DIMS = (((0,), (0,)), ((), ()))

PLAIN_DIMS = (((1,), (0,)), ((), ()))
PANEL = 16


def from_behind(value, axis, by):
    length = lax.axis_size(axis)
    pairs = [(i, i + by) for i in range(length) if 0 <= i + by < length]
    return lax.ppermute(value, axis, pairs)


def flip(value, axis, bit):
    length = lax.axis_size(axis)
    return lax.ppermute(value, axis, [(i, i ^ bit) for i in range(length)])


RING = 4


def ring(value, axis, by):
    length = lax.axis_size(axis)
    low = 2 if axis == "dp" else 1
    pairs = []
    for i in range(length):
        place = i // low % RING
        pairs.append((i, i + ((place + by) % RING - place) * low))
    return lax.ppermute(value, axis, pairs)


def pair(value, axis):
    return flip(value, axis, lax.axis_size(axis) // 2)


def swap(value):
    return flip(value, "dp", 1)


def place_of(axis):
    index = lax.axis_index(axis)
    low = 2 if axis == "dp" else 1
    return index // low % RING, index // (low * RING)


def spread(block, axis, meanwhile):
    half = block.shape[0] // 2
    behind, ahead, side = ring(block, axis, 1), ring(block, axis, -1), pair(block, axis)
    behind, *meanwhile = lax.optimization_barrier((behind, *meanwhile))
    fore = ring(jnp.concatenate([behind[:half], side[:half]]), axis, 1)
    back = ring(jnp.concatenate([ahead[half:], side[half:]]), axis, -1)
    cross = pair(jnp.concatenate([behind[half:], ahead[:half]]), axis)
    early = [swap(array) for array in (block, behind, ahead)]
    *early, fore, back = lax.optimization_barrier((*early, fore, back))
    late = [fore, back, cross, ring(fore[half:], axis, 1), ring(back[half:], axis, -1)]
    other = early + [swap(array) for array in [side] + late]
    spans = [
        [(0, 2 * half, 0, 0, None)],
        [(0, 2 * half, -1, 0, None)],
        [(0, 2 * half, 1, 0, None)],
        [(0, 2 * half, 0, 1, None)],
        [(0, half, 2, 0, 0), (half, half, -1, 1, 0)],
        [(0, half, 2, 0, 1), (half, half, 1, 1, 1)],
        [(0, half, -1, 1, 1), (half, half, 1, 1, 0)],
        [(0, half, 2, 1, 0)],
        [(0, half, 2, 1, 1)],
    ]
    return [block, behind, ahead, side] + late, other, spans, *meanwhile


def spread_ring(block, axis):
    half = block.shape[0] // 2
    before, after = ring(block, axis, 1), ring(block, axis, -1)
    return jnp.concatenate(
        [block, before, after, ring(before[:half], axis, 1), ring(after[half:], axis, -1)]
    )


def collect_ring(mine, other, axis):
    half = mine.shape[1] // 2
    low, wide = jnp.bfloat16, jnp.float32
    far = mine[3].astype(wide) + swap(other[3]).astype(wide)
    rest = swap(other[:3])
    one = ring(far[:half].astype(low), axis, -1)
    two = ring(far[half:].astype(low), axis, 1)
    behind = mine[1].astype(wide) + rest[1].astype(wide)
    ahead = mine[2].astype(wide) + rest[2].astype(wide)
    behind = jnp.concatenate([behind[:half] + one.astype(wide), behind[half:]])
    ahead = jnp.concatenate([ahead[:half], ahead[half:] + two.astype(wide)])
    from_ahead = ring(behind.astype(low), axis, -1)
    from_back = ring(ahead.astype(low), axis, 1)
    return [mine, rest, from_ahead, from_back], (one, two)


def after(value, *others):
    return lax.optimization_barrier((value,) + others)[0]


def packed(rows, width):
    high = rows.astype(jnp.bfloat16)
    rest = (rows - high.astype(jnp.float32)).astype(jnp.bfloat16)
    return high.reshape(-1, width), rest.reshape(-1, width)


def padded(rows, multiple):
    return jnp.pad(rows, ((0, -rows.shape[0] % multiple), (0, 0)))


ANYWHERE = pl.BlockSpec(memory_space=pl.ANY)
SCALARS = pl.BlockSpec(memory_space=pltpu.SMEM)
INSIDE = pl.BlockSpec(memory_space=pltpu.VMEM)
ROOM = pltpu.CompilerParams(vmem_limit_bytes=56 * 2**20)


def project_kernel(spans, offsets_ref, rows_ref, *refs):
    count = len(refs) - 8
    pieces, (out_ref, *whole_refs) = refs[:count], refs[count : count + 3]
    held, page, in_sem, out_sems, page_sem = refs[count + 3 :]
    for i, (which, first, rows) in enumerate(spans):
        offset = pl.multiple_of(offsets_ref[i], rows)
        pltpu.make_async_copy(
            pieces[which].at[pl.ds(first, rows)], held.at[pl.ds(offset, rows)], in_sem
        ).start()
    pltpu.make_async_copy(held, held, in_sem).wait()
    stores, column = [], 0
    for j, whole in enumerate(whole_refs):
        width = whole.shape[1]
        stores.append(
            pltpu.make_async_copy(held.at[:, pl.ds(column, width)], whole, out_sems.at[j])
        )
        stores[-1].start()
        column += width
    step = 512
    for column in range(0, out_ref.shape[1], step):
        cut = pl.ds(column, step)
        page[:, cut] = jnp.dot(rows_ref[...], held[:, cut], preferred_element_type=jnp.float32)
        pltpu.make_async_copy(page.at[:, cut], out_ref.at[:, cut], page_sem).start()
    pltpu.make_async_copy(page, out_ref, page_sem).wait()
    for store in stores:
        store.wait()


def project(rows, gathered, widths):
    core = lax.axis_index("dp") % 2
    place, side = place_of("fsdp")
    mine, other, pieces = gathered
    block = mine[0].shape[0]
    spans, offsets = [], []
    for who in range(2):
        for at, cuts in enumerate(pieces):
            for first, count, step, across, half in cuts:
                owner = (side ^ across) * RING + (place + step) % RING
                spans.append((who * len(pieces) + at, first, count))
                offsets.append((owner * 2 + (core ^ who)) * block + (half or 0) * count)
    depth = 2 * block * 2 * RING
    kind = mine[0].dtype
    return pl.pallas_call(
        functools.partial(project_kernel, spans),
        out_shape=[jax.ShapeDtypeStruct((rows.shape[0], widths[0]), jnp.float32)]
        + [jax.ShapeDtypeStruct((depth, width), kind) for width in widths],
        in_specs=[SCALARS, INSIDE] + [ANYWHERE] * (len(mine) + len(other)),
        out_specs=[ANYWHERE] * (1 + len(widths)),
        compiler_params=ROOM,
        scratch_shapes=[
            pltpu.VMEM((depth, sum(widths)), kind),
            pltpu.VMEM((rows.shape[0], widths[0]), jnp.float32),
            pltpu.SemaphoreType.DMA,
            pltpu.SemaphoreType.DMA((len(widths),)),
            pltpu.SemaphoreType.DMA,
        ],
    )(jnp.stack(offsets).astype(jnp.int32), rows, *mine, *other)


def pick_kernel(table_ref, conv_ref, feed_ref, mine_ref, other_ref, held, sem):
    slots, side = mine_ref.shape[0], mine_ref.shape[1]
    half = side // 2
    held[...] = jnp.zeros_like(held)

    def one(i, finish):
        at = 5 * i
        kind, piece = table_ref[at], table_ref[at + 1]
        first = pl.multiple_of(table_ref[at + 4] * half, half)

        def move(source, target):
            copy = pltpu.make_async_copy(source, target, sem)
            if finish:
                copy.wait()
            else:
                copy.start()

        def column(k):
            return pl.ds(pl.multiple_of(k * side, side), side)

        @pl.when(kind == 1)
        def _():
            move(
                conv_ref.at[piece, pl.ds(0, half), column(table_ref[at + 2])],
                held.at[0, i, pl.ds(first, half), :],
            )

        for which in range(2):

            @pl.when((kind == 2) & (table_ref[at + 2 + which] >= 0))
            def _():
                move(feed_ref.at[piece + which, :, column(table_ref[at + 2 + which])], held.at[which, i])

    for finish in (False, True):

        def step(i, carry):
            one(i, finish)
            return carry

        lax.fori_loop(0, 2 * slots, step, 0)
    for q in range(slots):
        mine_ref[q] = held[0, q].astype(jnp.float32) + held[1, q].astype(jnp.float32)
        other_ref[q] = held[0, slots + q]


def pick(table, conv, feed, slots, side):
    shape = (slots, side, side)
    return pl.pallas_call(
        pick_kernel,
        out_shape=[jax.ShapeDtypeStruct(shape, jnp.float32), jax.ShapeDtypeStruct(shape, conv.dtype)],
        in_specs=[SCALARS, ANYWHERE, ANYWHERE],
        out_specs=[INSIDE, INSIDE],
        compiler_params=ROOM,
        scratch_shapes=[
            pltpu.VMEM((2, 2 * slots, side, side), conv.dtype),
            pltpu.SemaphoreType.DMA,
        ],
    )(table, conv, feed)


def add_kernel(own_ref, ahead_ref, behind_ref, extra_ref, out_ref):
    width = out_ref.shape[2]
    parts = own_ref.shape[1] // width
    rows = out_ref.shape[1] - extra_ref.shape[1]
    blocks = out_ref.shape[0] // parts
    for i in range(blocks):
        cut = pl.ds(i * rows, rows)
        total = own_ref[cut, :] + ahead_ref[cut, :].astype(jnp.float32)
        total = (total + behind_ref[cut, :].astype(jnp.float32)).astype(out_ref.dtype)
        for k in range(parts):
            out_ref[k * blocks + i, :rows, :] = total[:, k * width : (k + 1) * width]
            out_ref[k * blocks + i, rows:, :] = extra_ref[k]


def add_terms(own, ahead, behind, extra, blocks):
    parts = extra.shape[0]
    rows, width = own.shape[0] // blocks + extra.shape[1], own.shape[1] // parts
    return pl.pallas_call(
        add_kernel,
        out_shape=jax.ShapeDtypeStruct((parts * blocks, rows, width), ahead.dtype),
        in_specs=[INSIDE] * 4,
        out_specs=INSIDE,
        compiler_params=ROOM,
        cost_estimate=pl.CostEstimate(
            flops=50 * 10**9, bytes_accessed=own.size * 8, transcendentals=0
        ),
    )(own, ahead, behind, extra)


def put_kernel(at_ref, mine_ref, other_ref, *refs):
    count = (len(refs) - 3) // 2
    outs, pages = refs[:count], refs[count : 2 * count]
    held, in_sems, out_sems = refs[-3:]
    count_held, side = mine_ref.shape[0], mine_ref.shape[1]
    loads = [
        pltpu.make_async_copy(source, held.at[pl.ds(i * count_held, count_held)], in_sems.at[i])
        for i, source in enumerate((mine_ref, other_ref))
    ]
    for load in loads:
        load.start()
    for load in loads:
        load.wait()
    tile = 0
    for j in range(count):
        for k in range(outs[j].shape[1] // side):
            pages[j][:, k * side : (k + 1) * side] = held[at_ref[tile]]
            tile += 1
        pltpu.make_async_copy(pages[j], outs[j], out_sems.at[j]).start()
    for j in range(count):
        pltpu.make_async_copy(pages[j], outs[j], out_sems.at[j]).wait()


def put(core, slot_index, mine, other, widths):
    chips, slots, side, _ = mine.shape
    owner = slot_index // slots
    at = ((owner % 2 ^ core) * chips + owner // 2) * slots + slot_index % slots
    flat = (chips * slots, side, side)
    return pl.pallas_call(
        put_kernel,
        out_shape=[jax.ShapeDtypeStruct((side, width), mine.dtype) for width in widths],
        in_specs=[SCALARS, ANYWHERE, ANYWHERE],
        out_specs=[ANYWHERE] * len(widths),
        compiler_params=pltpu.CompilerParams(vmem_limit_bytes=62 * 2**20),
        scratch_shapes=[pltpu.VMEM((side, width), mine.dtype) for width in widths]
        + [
            pltpu.VMEM((2 * chips * slots, side, side), mine.dtype),
            pltpu.SemaphoreType.DMA((2,)),
            pltpu.SemaphoreType.DMA((len(widths),)),
        ],
    )(at.astype(jnp.int32), mine.reshape(flat), other.reshape(flat))


def feed_kernel(order_ref, fed_ref, dy_ref, w_ref, *refs):
    both_ref, act_ref, back_ref = refs[-3:]
    width = act_ref.shape[-1]
    mixed = jnp.dot(fed_ref[0], w_ref[:, : 2 * width], preferred_element_type=jnp.float32)
    grad_act = jnp.dot(dy_ref[0], w_ref[:, 2 * width :], preferred_element_type=jnp.float32)
    gate, up = mixed[:, :width], mixed[:, width:]
    sigmoid = jax.nn.sigmoid(gate)
    passed = gate * sigmoid
    activation = (passed * up).astype(jnp.bfloat16)
    grad_gate = grad_act * up * sigmoid * (1.0 + gate * (1.0 - sigmoid))
    grad_up = grad_act * passed
    both = jnp.concatenate([grad_gate.astype(jnp.bfloat16), grad_up.astype(jnp.bfloat16)], axis=1)
    both_ref[0] = both
    act_ref[0] = activation
    back_ref[0] = back_dot(both, w_ref[:, : 2 * width]).astype(jnp.bfloat16)


def feed_forward(order, fed, grad_feed, weights, first, begun):
    blocks, rows, model_width = fed.shape
    width = weights.shape[1] // 3
    begun = list(begun)

    def turned(i, order_ref):
        return (order_ref[first + i], 0, 0)

    def shape(count, columns):
        return jax.ShapeDtypeStruct((count, rows, columns), jnp.bfloat16)

    whole = grad_feed.shape[0]

    return pl.pallas_call(
        feed_kernel,
        grid_spec=pltpu.PrefetchScalarGridSpec(
            num_scalar_prefetch=1,
            grid=(blocks,),
            in_specs=[
                pl.BlockSpec((1, rows, model_width), lambda i, order_ref: (i, 0, 0)),
                pl.BlockSpec((1, rows, model_width), turned),
                pl.BlockSpec(weights.shape, lambda i, order_ref: (0, 0)),
            ]
            + [ANYWHERE] * len(begun),
            out_specs=[
                pl.BlockSpec((1, rows, 2 * width), lambda i, order_ref: (first + i, 0, 0)),
                pl.BlockSpec((1, rows, width), turned),
                pl.BlockSpec((1, rows, model_width), lambda i, order_ref: (i, 0, 0)),
            ],
        ),
        out_shape=[
            shape(whole, 2 * width),
            shape(whole, width),
            shape(blocks, model_width),
        ],
        input_output_aliases={4 + i: i for i in range(len(begun))},
        compiler_params=ROOM,
        cost_estimate=pl.CostEstimate(
            flops=2 * blocks * rows * model_width * width * 5,
            bytes_accessed=blocks * rows * (4 * model_width + 3 * width) * 2,
            transcendentals=blocks * rows * width,
        ),
    )(order, fed, grad_feed, weights, *begun)


def turn_kernel(
    own_ref, other_ref, ahead_ref, behind_ref, values_ref, scale_ref, gain_ref, seed_ref, w_ref, part_ref, conv_ref,
    resid_out, branch_out, part_out, conv_out, gain_out,
):
    wide = jnp.float32
    grads = own_ref[0].astype(wide) + other_ref[0].astype(wide)
    grads = grads + ahead_ref[...].astype(wide) + behind_ref[...].astype(wide)
    values, scale = values_ref[...], scale_ref[...]
    weighted = grads * gain_ref[...]
    inner = jnp.mean(values * weighted, axis=-1, keepdims=True)
    resid = seed_ref[...] + scale * weighted - values * (scale * scale * scale * inner)
    gain_out[0] = jnp.sum(values * scale * grads, axis=0, keepdims=True)
    resid_out[...] = resid
    branch = resid.astype(branch_out.dtype)
    branch_out[...] = branch
    gated = back_dot(branch, w_ref[...])
    part_out[...] = (gated * conv_ref[...]).astype(part_out.dtype)
    conv_out[...] = gated * part_ref[...]


def turn_back(terms, values, scale, gain, seed, weights, mixed, convolved, steps):
    rows, width = values.shape
    cut = rows // steps

    def tokens(i):
        return (i, 0)

    block = pl.BlockSpec((cut, width), tokens)
    first = pl.BlockSpec((1, cut, width), lambda i: (0, i, 0))
    wide, low = jnp.float32, jnp.bfloat16
    *results, gains = pl.pallas_call(
        turn_kernel,
        grid=(steps,),
        out_shape=[jax.ShapeDtypeStruct((rows, width), kind) for kind in (wide, low, low, wide)]
        + [jax.ShapeDtypeStruct((steps, 1, width), wide)],
        in_specs=[
            first,
            first,
            block,
            block,
            block,
            pl.BlockSpec((cut, 1), tokens),
            pl.BlockSpec((1, width), lambda i: (0, 0)),
            block,
            pl.BlockSpec(weights.shape, lambda i: (0, 0)),
            pl.BlockSpec((cut, width), lambda i: (i, 1)),
            block,
        ],
        out_specs=[block] * 4 + [pl.BlockSpec((1, 1, width), lambda i: (i, 0, 0))],
        compiler_params=ROOM,
    )(*terms, values, scale, gain[None], seed, weights, mixed, convolved)
    return (*results, jnp.sum(gains, axis=(0, 1)))


def rms_factor(values):
    return lax.rsqrt(jnp.mean(values * values, axis=-1, keepdims=True) + EPS_NORM)


def norm_back(values, scale_val, gain_row, grad_out):
    weighted = grad_out * gain_row
    inner = jnp.mean(values * weighted, axis=-1, keepdims=True)
    grad_values = scale_val * weighted - values * scale_val * scale_val * scale_val * inner
    grad_gain = jnp.sum(values * scale_val * grad_out, axis=0)
    return (grad_values, grad_gain)


def outer_sum(left_arr, right_arr):
    return lax.dot_general(left_arr, right_arr, TOKEN_DIMS, preferred_element_type=jnp.float32)


def back_dot(left_arr, right_arr):
    return lax.dot_general(left_arr, right_arr, BACK_DIMS, preferred_element_type=jnp.float32)


def exchange(value, axis, groups=None):
    return lax.all_to_all(value, axis, 0, 0, axis_index_groups=groups)


def column_halves(value, parts, core):
    cut = value.reshape(value.shape[0], parts, 2, -1)
    mine = lax.dynamic_index_in_dim(cut, core, 2, keepdims=False).reshape(value.shape[0], -1)
    other = lax.dynamic_index_in_dim(cut, 1 - core, 2, keepdims=False).reshape(value.shape[0], -1)
    return jnp.concatenate([mine, swap(other)])


def slot_table(owner_row, per_owner):
    tile_count = owner_row.shape[0]
    same_owner = owner_row[None, :] == owner_row[:, None]
    before = (
        jnp.arange(tile_count, dtype=jnp.int32)[None, :]
        < jnp.arange(tile_count, dtype=jnp.int32)[:, None]
    )
    slot_rank = jnp.sum((same_owner & before).astype(jnp.int32), axis=1)
    return owner_row * per_owner + slot_rank


def split_dot(left, right, dims, axis):
    def cut(value):
        high = value.astype(jnp.bfloat16)
        rest = value - high.astype(jnp.float32)
        middle = rest.astype(jnp.bfloat16)
        return high, middle, (rest - middle.astype(jnp.float32)).astype(jnp.bfloat16)

    left_cut, right_cut = cut(left), cut(right)
    pairs = ((0, 0), (0, 1), (1, 0), (1, 1), (0, 2), (2, 0))
    return lax.dot_general(
        jnp.concatenate([left_cut[i] for i, _ in pairs], axis[0]),
        jnp.concatenate([right_cut[j] for _, j in pairs], axis[1]),
        dims,
        preferred_element_type=jnp.float32,
    )


def bases_kernel(grad_ref, stats_ref, bases_ref, stats_out, q_ref, m_ref, w_ref):
    tiles, side = grad_ref.shape[0], grad_ref.shape[1]
    count = 2 * tiles
    for i in range(tiles):
        grad = grad_ref[i]
        for j, dims in enumerate((BACK_DIMS, TOKEN_DIMS)):
            axis = 1 - j
            square = near_dot(grad, grad, dims, (axis, axis))
            stats_out[i, j] = BETA_STAT * stats_ref[i, j] + (1.0 - BETA_STAT) * square
    for g in range(count):
        m_ref[g] = split_dot(stats_out[g // 2, g % 2], bases_ref[g // 2, g % 2], PLAIN_DIMS, (1, 0))
    row = lax.broadcasted_iota(jnp.int32, (8, side), 0)
    lane = lax.broadcasted_iota(jnp.int32, (8, side), 1)
    rows = lax.broadcasted_iota(jnp.int32, (PANEL, side), 0)
    lanes = lax.broadcasted_iota(jnp.int32, (PANEL, side), 1)
    all_rows = lax.broadcasted_iota(jnp.int32, (side, side), 0)
    all_lanes = lax.broadcasted_iota(jnp.int32, (side, side), 1)
    for g in range(count):
        w_ref[g] = split_dot(m_ref[g], m_ref[g], TOKEN_DIMS, (0, 0))
    for base in range(0, side, PANEL):
        end = base + PANEL
        panels = [[w_ref[g, i : i + 8, :] for i in range(base, end, 8)] for g in range(count)]
        for k in range(PANEL):
            at, inside = k // 8, k % 8
            hit = lane == base + k
            for g in range(count):
                panel = panels[g]
                column = jnp.broadcast_to(panel[at][:, base + k : base + k + 1], (8, side))
                scale = lax.rsqrt(jnp.broadcast_to(column[inside : inside + 1], (8, side)))
                top = jnp.broadcast_to(panel[at][inside : inside + 1], (8, side))
                top = jnp.where(hit, scale, top * scale)
                part = jnp.where(hit, 0.0, panel[at]) - column * scale * top
                panel[at] = jnp.where(row > inside, part, jnp.where(row == inside, top, panel[at]))
                for i in range(at + 1, PANEL // 8):
                    column = jnp.broadcast_to(panel[i][:, base + k : base + k + 1], (8, side))
                    panel[i] = jnp.where(hit, 0.0, panel[i]) - column * scale * top
        for g in range(count):
            done = jnp.concatenate(panels[g], axis=0)
            w_ref[g, base:end, :] = done
            if end < side:
                upper = (lanes >= base) & (lanes < end) & (lanes - base > rows)
                change = split_dot(done, jnp.where(upper, 0.0, done), TOKEN_DIMS, (0, 0))[end:]
                gone = (all_lanes[end:] >= base) & (all_lanes[end:] < end)
                w_ref[g, end:, :] = jnp.where(gone, 0.0, w_ref[g, end:, :]) - change
    for g in range(count):
        inverse = jnp.where(all_lanes <= all_rows, w_ref[g], 0.0)
        q_ref[g // 2, g % 2] = split_dot(m_ref[g], inverse, BACK_DIMS, (1, 1))


def near_dot(left, right, dims, axis):
    def cut(value):
        high = value.astype(jnp.bfloat16)
        return high, (value - high.astype(jnp.float32)).astype(jnp.bfloat16)

    (left_high, left_rest), (right_high, right_rest) = cut(left), cut(right)
    left_axis, right_axis = axis
    return lax.dot_general(
        jnp.concatenate([left_high, left_high, left_rest], left_axis),
        jnp.concatenate([right_high, right_rest, right_high], right_axis),
        dims,
        preferred_element_type=jnp.float32,
    )


def soap_kernel(
    mine_ref, other_ref, master_ref, first_ref, second_ref, bases_ref,
    grad_ref, master_out, first_out, second_out, low_out,
):
    count, side = mine_ref.shape[0], mine_ref.shape[1]
    for i in range(count):
        grad = mine_ref[i] + other_ref[i].astype(jnp.float32)
        first = BETA_ONE * first_ref[i] + (1.0 - BETA_ONE) * grad
        grad_ref[i] = grad
        first_out[i] = first
    turned = []
    for i in range(count):
        pair_rows = jnp.concatenate([grad_ref[i], first_out[i]], axis=1)
        turned.append(near_dot(bases_ref[i, 0], pair_rows, TOKEN_DIMS, (0, 0)))
    for i in range(count):
        stacked = jnp.concatenate([turned[i][:, :side], turned[i][:, side:]], axis=0)
        both = near_dot(stacked, bases_ref[i, 1], PLAIN_DIMS, (1, 0))
        rotated, moment = both[:side], both[side:]
        second = BETA_TWO * second_ref[i] + (1.0 - BETA_TWO) * rotated * rotated
        second_out[i] = second
        turned[i] = (
            moment
            / (1.0 - BETA_ONE**STEP)
            / (jnp.sqrt(second / (1.0 - BETA_TWO**STEP)) + EPS_ADAM)
        )
    for i in range(count):
        turned[i] = near_dot(bases_ref[i, 0], turned[i], PLAIN_DIMS, (1, 0))
    for i in range(count):
        step = near_dot(turned[i], bases_ref[i, 1], BACK_DIMS, (1, 1))
        master = master_ref[i] - RATE_MATRIX * (step + DECAY_WEIGHT * master_ref[i])
        master_out[i] = master
        for j in range(low_out.shape[0]):
            low_out[j, i] = master.astype(low_out.dtype)


def soap_update(mine, other, master, first, second, bases, copies):
    tiles = jax.ShapeDtypeStruct(mine.shape, jnp.float32)
    return pl.pallas_call(
        soap_kernel,
        out_shape=[tiles] * 4 + [jax.ShapeDtypeStruct((copies,) + mine.shape, jnp.bfloat16)],
        in_specs=[INSIDE] * 6,
        out_specs=[INSIDE] * 5,
        compiler_params=ROOM,
    )(mine, other, master, first, second, bases)


def bases_update(grad_tiles, stats, bases):
    tiles, _, side, _ = bases.shape
    whole = jax.ShapeDtypeStruct(bases.shape, jnp.float32)
    return pl.pallas_call(
        bases_kernel,
        out_shape=[whole, whole],
        in_specs=[INSIDE] * 3,
        out_specs=[INSIDE] * 2,
        scratch_shapes=[pltpu.VMEM((2 * tiles, side, side), jnp.float32) for _ in range(2)],
        compiler_params=ROOM,
        cost_estimate=pl.CostEstimate(
            flops=30 * 10**9, bytes_accessed=20 * bases.size, transcendentals=0
        ),
    )(grad_tiles, stats, bases)


def shards(
    block_in,
    cotangent,
    lengths,
    vector_params,
    vector_first,
    vector_second,
    w_in,
    w_out,
    w_gate,
    w_up,
    w_down,
    tile_owner,
    tile_master,
    tile_first,
    tile_second,
    tile_stats,
    tile_bases,
):
    micro_count, _, tok_count, model_width = block_in.shape
    hidden_width = w_gate.shape[1]
    shard_rows = w_in.shape[0]
    half_rows = shard_rows // 2
    parts = lax.axis_size("fsdp")
    owners = lax.axis_size("dp")
    chips = owners // 2
    owner_id = lax.axis_index("dp")
    core = owner_id % 2
    place, far = place_of("dp")
    chip_group = [list(range(i, i + 2 * RING)) for i in range(0, owners, 2 * RING)]
    same_core = [[2 * i + c for i in range(chips)] for c in range(2)]
    same_ring_place = [
        [(h * 2 * RING + i) * parts + f for h in range(owners // (2 * RING)) for f in range(parts)]
        for i in range(2 * RING)
    ]
    tile_side = tile_master.shape[-1]
    per_owner = tile_master.shape[1]
    tile_count = tile_owner.shape[1]
    g_one, g_two, k_zero, k_one, k_two = [vector_params[i] for i in range(5)]

    def half_of(matrix):
        return lax.dynamic_slice(matrix, (core * half_rows, 0), (half_rows, matrix.shape[1]))

    conv_block = jnp.concatenate([half_of(w_in), half_of(w_out)], axis=1)
    positions = lax.axis_index("fsdp") * tok_count + jnp.arange(tok_count, dtype=jnp.int32)
    live_mask = (positions[None, :] < lengths).astype(jnp.float32)[:, :, None]
    seed_grad = (cotangent[:, 0] * live_mask).reshape(-1, model_width)
    grad_feed = lax.all_gather(
        seed_grad.astype(jnp.bfloat16), "dp", axis_index_groups=chip_group, axis=0
    )
    hidden = hidden_width // RING // 2
    wide = -(-hidden // tile_side) * tile_side
    shift = 2 * hidden - wide
    columns = jnp.arange(wide, dtype=jnp.int32)
    kept = (columns >= core * (wide - hidden)) & (columns < hidden + core * (wide - hidden))

    def slice_of(matrix):
        first = place * (2 * hidden) + core * shift
        return jnp.where(
            kept[None, :], lax.dynamic_slice(matrix, (0, first), (shard_rows, wide)), jnp.zeros((), matrix.dtype)
        )

    feed_block = jnp.concatenate([slice_of(matrix) for matrix in (w_gate, w_up, w_down)], axis=1)
    token_rows = block_in.astype(jnp.float32).reshape(-1, model_width)
    scale_one = rms_factor(token_rows)
    normed = (token_rows * scale_one * g_one).astype(jnp.bfloat16)
    *conv_pieces, normed, feed_block = spread(conv_block, "fsdp", (normed, feed_block))
    feed_weights = lax.all_gather(
        after(feed_block, *conv_pieces[0][4:]), "fsdp", axis=0, tiled=True
    )

    mixed_all, whole_in, whole_out = project(normed, conv_pieces, (3 * model_width, model_width))
    part_b = mixed_all[:, :model_width]
    part_c = mixed_all[:, model_width : 2 * model_width]
    part_x = mixed_all[:, 2 * model_width :]
    product = (part_b * part_x).reshape(micro_count, tok_count, model_width)
    extended = jnp.concatenate([from_behind(product[:, -2:], "fsdp", 1), product], axis=1)
    convolved = (
        k_zero * extended[:, :-2] + k_one * extended[:, 1:-1] + k_two * extended[:, 2:]
    ).reshape(-1, model_width)
    gated_conv = (part_c * convolved).astype(jnp.bfloat16)
    residual = token_rows + jnp.dot(gated_conv, whole_out, preferred_element_type=jnp.float32)
    scale_two = rms_factor(residual)
    normed_two = (residual * scale_two * g_two).astype(jnp.bfloat16)

    fed = spread_ring(normed_two, "dp")
    fed, normed_halves, gated_halves = lax.optimization_barrier(
        (fed, column_halves(normed, parts, core), column_halves(gated_conv, parts, core))
    )
    steps = jnp.array([0, RING - 1, 1, 2], dtype=jnp.int32)
    ring_places = (place + steps) % RING * 2
    order = jnp.concatenate([ring_places + core, ring_places + 1 - core]).astype(jnp.int32)
    fed_other = swap(fed)
    begun, back_parts = (), []
    for who, rows in enumerate((fed, fed_other)):
        *begun, back = feed_forward(
            order, rows.reshape(RING, -1, model_width), grad_feed, feed_weights, who * RING, begun
        )
        back_parts.append(back)
    grad_both, activation = begun
    grad_terms, far_parts = collect_ring(*back_parts, "dp")
    grad_both, far_parts = lax.optimization_barrier((grad_both, far_parts))
    fed = jnp.concatenate([fed, fed_other])
    low = jnp.bfloat16
    feed_sums = jnp.concatenate(
        [
            outer_sum(fed, grad_both.reshape(-1, 2 * wide)).astype(low),
            outer_sum(grad_feed.reshape(-1, model_width), activation.reshape(-1, wide)).astype(low),
        ],
        axis=1,
    )
    *grad_terms, feed_sums = lax.optimization_barrier((*grad_terms, feed_sums))
    feed_rows = lax.psum_scatter(feed_sums, "fsdp", scatter_dimension=0, tiled=True)

    grad_resid, grad_branch, grad_part_c, grad_conv, grad_gain_two = turn_back(
        grad_terms, residual, scale_two, g_two, seed_grad, whole_out, mixed_all, convolved, micro_count
    )
    grad_conv = grad_conv.reshape(micro_count, tok_count, model_width)
    grad_ext = jnp.concatenate([grad_conv, from_behind(grad_conv[:, :2], "fsdp", -1)], axis=1)
    grad_product = (
        k_two * grad_conv + k_one * grad_ext[:, 1 : tok_count + 1] + k_zero * grad_ext[:, 2:]
    ).reshape(-1, model_width)
    grad_kernel = jnp.stack(
        [
            jnp.sum(grad_conv * extended[:, :-2], axis=(0, 1)),
            jnp.sum(grad_conv * extended[:, 1:-1], axis=(0, 1)),
            jnp.sum(grad_conv * extended[:, 2:], axis=(0, 1)),
        ]
    )
    grad_all = jnp.concatenate(
        [
            (grad_product * part_x).astype(low),
            grad_part_c,
            (grad_product * part_b).astype(low),
            grad_branch,
        ],
        axis=1,
    )
    grad_mixed = grad_all[:, : 3 * model_width]

    def conv_block(step, grads):
        index = (place + step) % RING
        right = [
            lax.dynamic_slice(part, (0, index * model_width), (part.shape[0], model_width)) for part in grads
        ]
        left = jnp.where(index == RING - 1, gated_halves, normed_halves)
        return outer_sum(left, jnp.concatenate(right))

    grads = (grad_all, swap(grad_all))
    conv_far = conv_block(2, grads).astype(low)
    middle = conv_far.shape[0] // 2
    one, two = ring(conv_far[:middle], "dp", -1), ring(conv_far[middle:], "dp", 1)
    *grads, _ = lax.optimization_barrier((*grads, conv_far))
    behind, ahead = conv_block(-1, grads), conv_block(1, grads)
    one, two = one.astype(jnp.float32), two.astype(jnp.float32)
    behind = (behind + jnp.concatenate([one, jnp.zeros_like(one)])).astype(low)
    ahead = (ahead + jnp.concatenate([jnp.zeros_like(two), two])).astype(low)
    conv_sums = conv_block(0, grads)
    conv_cols = [conv_sums, ring(behind, "dp", -1), ring(ahead, "dp", 1)]

    grad_normed = back_dot(after(grad_mixed, behind, ahead), whole_in)
    grad_rows_norm, grad_gain_one = norm_back(token_rows, scale_one, g_one, grad_normed)
    vector_grads = jnp.concatenate([grad_gain_one[None], grad_gain_two[None], grad_kernel], axis=0)
    vector_rows = vector_grads.shape[0]
    feed_rows = after(feed_rows, behind, ahead)
    feed_rows = feed_rows.astype(jnp.float32) + pair(feed_rows, "dp").astype(jnp.float32)
    feed_tiles = lax.all_gather(feed_rows.astype(low), "dp", axis_index_groups=chip_group, axis=0)
    block_width = model_width // (chips // RING)
    extra = jnp.stack([padded(rows, 16) for rows in packed(vector_grads, block_width)])
    conv_cols = add_terms(*conv_cols, extra, parts)
    conv_own = exchange(conv_cols, ("dp", "fsdp"), same_ring_place)
    conv_own = jnp.sum(conv_own.astype(jnp.float32), axis=0)
    packed_rows = vector_rows * (model_width // block_width)
    vector_part = jnp.concatenate(packed(conv_own[half_rows : half_rows + packed_rows], block_width))
    conv_own = jnp.concatenate([conv_own[:half_rows].astype(low), padded(vector_part, 32)])
    conv_tiles = exchange(jnp.broadcast_to(conv_own, (chips,) + conv_own.shape), "dp", same_core)
    vector_part = jnp.sum(
        conv_tiles[:, half_rows : half_rows + 2 * packed_rows].astype(jnp.float32), axis=0
    ).reshape(2 * vector_rows, model_width)
    vector_grads = vector_part[:vector_rows] + vector_part[vector_rows:]
    vector_grads = vector_grads + swap(vector_grads)
    out_parts = back_dot(
        after(activation, conv_cols).reshape(-1, wide), feed_weights[:, 2 * wide :]
    ).astype(low).reshape(grad_feed.shape)
    feed_out = lax.psum_scatter(
        after(out_parts, conv_own), "dp", scatter_dimension=0, axis_index_groups=chip_group
    )

    slot_index = slot_table(tile_owner[0], per_owner)
    slot_match = slot_index[None, :] == jnp.arange(per_owner * owners, dtype=jnp.int32)[:, None]
    tile_of_slot = (
        jnp.sum(
            jnp.where(slot_match, jnp.arange(1, tile_count + 1, dtype=jnp.int32)[None, :], 0), axis=1
        )
        - 1
    )
    wanted = jnp.concatenate(
        [
            lax.dynamic_slice(tile_of_slot, (owner_id * per_owner,), (per_owner,)),
            lax.dynamic_slice(tile_of_slot, ((owner_id ^ 1) * per_owner,), (per_owner,)),
        ]
    )
    conv_count = 4 * model_width // tile_side
    each_conv, each_feed = conv_count // chips, 2 * hidden // tile_side
    parts_far = chips // RING
    feed_tile = wanted - conv_count
    within = feed_tile % each_feed
    feed_first = feed_tile // (each_feed * RING) * (wide // tile_side)
    is_conv = wanted < conv_count
    own_slot = jnp.arange(2 * per_owner) < per_owner
    left, right = within < wide // tile_side, within >= shift // tile_side
    table = jnp.stack(
        [
            jnp.where(is_conv, 1, jnp.where(own_slot, 2, 0)),
            jnp.where(
                is_conv,
                wanted // each_conv % parts_far * RING + wanted // each_conv // parts_far,
                feed_tile // each_feed % RING * 2,
            ),
            jnp.where(is_conv, wanted % each_conv, jnp.where(left, feed_first + within, -1)),
            jnp.where(right, feed_first + within - shift // tile_side, -1),
            jnp.where(is_conv, core, 0),
        ],
        axis=1,
    )
    table = jnp.where(wanted[:, None] < 0, 0, table).astype(jnp.int32).reshape(-1)
    mine, other = pick(table, conv_tiles, feed_tiles, per_owner, tile_side)
    owned_grads, master_new, first_new, second_new, master_low = soap_update(
        mine, swap(other), tile_master[0], tile_first[0], tile_second[0], tile_bases[0], chips
    )
    masters = exchange(master_low, "dp", same_core)
    stats_new, bases_new = bases_update(owned_grads, tile_stats[0], tile_bases[0])
    bases_new, feed_out, vector_grads, grad_resid = lax.optimization_barrier(
        (bases_new, feed_out, vector_grads, grad_resid)
    )
    result_rows = residual + feed_out.astype(jnp.float32)
    grad_rows = grad_resid + grad_rows_norm
    vec_first = BETA_ONE * vector_first + (1.0 - BETA_ONE) * vector_grads
    vec_second = BETA_TWO * vector_second + (1.0 - BETA_TWO) * vector_grads * vector_grads
    vec_new = vector_params - RATE_VECTOR * (vec_first / (1.0 - BETA_ONE**STEP)) / (
        jnp.sqrt(vec_second / (1.0 - BETA_TWO**STEP)) + EPS_ADAM
    )
    masters, bases_new, stats_new, result_rows, grad_rows, vec_new, vec_first, vec_second = (
        lax.optimization_barrier(
            (masters, bases_new, stats_new, result_rows, grad_rows, vec_new, vec_first, vec_second)
        )
    )
    widths = (3 * model_width, model_width, hidden_width, hidden_width, hidden_width)
    w_in_new, w_out_new, w_gate_new, w_up_new, w_down_new = put(
        core, slot_index, masters, swap(masters), widths
    )
    whole_shape = (micro_count, 1, tok_count, model_width)
    return (
        result_rows.reshape(whole_shape),
        grad_rows.reshape(whole_shape),
        vec_new,
        vec_first,
        vec_second,
        w_in_new,
        w_out_new,
        w_gate_new,
        w_up_new,
        w_down_new,
        master_new[None],
        first_new[None],
        second_new[None],
        stats_new[None],
        bases_new[None],
    )


def solution(mesh):
    return jax.shard_map(
        shards,
        mesh=mesh,
        in_specs=(
            P(None, "dp", "fsdp", None),
            P(None, "dp", "fsdp", None),
            P(None, "dp"),
            P(),
            P(),
            P(),
            P("fsdp", None),
            P("fsdp", None),
            P("fsdp", None),
            P("fsdp", None),
            P("fsdp", None),
            P("fsdp", None),
            P("fsdp", "dp", None, None),
            P("fsdp", "dp", None, None),
            P("fsdp", "dp", None, None),
            P("fsdp", "dp", None, None, None),
            P("fsdp", "dp", None, None, None),
        ),
        out_specs=(
            P(None, "dp", "fsdp", None),
            P(None, "dp", "fsdp", None),
            P(),
            P(),
            P(),
            P("fsdp", None),
            P("fsdp", None),
            P("fsdp", None),
            P("fsdp", None),
            P("fsdp", None),
            P("fsdp", "dp", None, None),
            P("fsdp", "dp", None, None),
            P("fsdp", "dp", None, None),
            P("fsdp", "dp", None, None, None),
            P("fsdp", "dp", None, None, None),
        ),
        check_vma=False,
    )
```
